32 devices in a mesh: psg: 8 (over z, y), qry: 4 (over x, core).
Axes of the slice: x: 2, y: 2, z: 4, core: 2. Of those that a mesh axis runs over, the one named last changes fastest.
Arguments:
- queries: bfloat16 [128, 32, 128], P(('psg', 'qry')), may hold values from -6 to 6
- passages: bfloat16 [256, 256, 128], P('psg'), may hold values from -6 to 6
- candidates: int32 [128, 32], P(('psg', 'qry')), may hold values from 0 to 255, as said below
- teacher: float32 [128, 32], P(('psg', 'qry')), may hold values from -8 to 8
Outputs:
- pair_loss: float32 [128], P(('psg', 'qry'))
- grad_queries: bfloat16 [128, 32, 128], P(('psg', 'qry'))
- grad_passages: bfloat16 [256, 256, 128], P('psg', 'qry')
The draws below stay inside these ranges and needn't reach their ends.
Inputs may be any that keep to these rules, and one draw needn't show every extreme that they name: Passage p lies in block p // 32. Among the 4 x 32 candidates of one device's queries (aligned blocks of 4 rows), at most 40 lie in one passage block; one passage block, the same for all devices, holds exactly 40 of every device's candidates. Candidate ids of one query may repeat.
All inputs are finite; a program needn't handle non-finite values.
Results may differ from the reference program's by a relative error of at most 0.019.
Values may be sent and summed in bfloat16 or wider, within the bound.
No kernel may reach another device: no remote copies, remote signals or barrier semaphores. Data moves between devices by JAX's collectives and lax.ppermute only.
A program may use at most 64 MiB of HBM per device.

```python
import jax
import jax.numpy as jnp
from jax import lax

E = 128
QT = 32
PT = 256
C = 32
QD = 4
PS_DEV = 32
NQ = 128
NP = 256
CAP = 40
N_QRY = 4


def draw_candidates(key, part):
    blocks = NQ // QD
    owners = NP // PS_DEV
    pair_count = QD * C
    slot_count = owners * CAP
    hottest = jax.random.randint(jax.random.fold_in(key, 11), (), 0, owners)

    def one_block(block_key):
        subkeys = jax.random.split(block_key, 4)
        ranking = jax.random.permutation(subkeys[0], owners)
        slot_owner = jnp.arange(slot_count) // CAP
        owner_rank = ranking[slot_owner]
        jitter = jax.random.randint(subkeys[1], (slot_count,), 0, 4096)
        precedence_rank = jitter + (owners - 1 - owner_rank) * (8192 // owners)
        precedence_rank = jnp.where(slot_owner == hottest, 16384, precedence_rank)
        distinct = precedence_rank * 8192 + jnp.arange(slot_count)
        picked = jnp.argsort(-distinct, stable=True)[:pair_count]
        picked = jax.random.permutation(subkeys[2], picked)
        local_ids = jax.random.randint(subkeys[3], (pair_count,), 0, PS_DEV)
        return (picked // CAP * PS_DEV + local_ids).reshape(QD, C).astype(jnp.int32)
    result = jax.vmap(one_block)(jax.random.split(jax.random.fold_in(key, 7), blocks))
    return result.reshape(NQ, C).astype(jnp.int32)


def steps_of(rng, dims, cuts, low, top_value):
    level, own = 1.0, jax.random.fold_in(rng, 6)
    for dim, shards_of in cuts:
        heights = jnp.exp(jax.random.uniform(jax.random.fold_in(own, dim), (shards_of,), jnp.float32, low / len(cuts), top_value / len(cuts)))
        level = level * jnp.repeat(heights, dims[dim] // shards_of).reshape([-1 if axis == dim else 1 for axis in range(len(dims))])
    return level


def normal_values(own_key, dims, deviation, bound, cuts=(), dtype=jnp.bfloat16):
    values = deviation * jax.random.normal(own_key, dims, jnp.float32)
    if cuts:
        values = values * steps_of(own_key, dims, cuts, -0.22, 0.18)
    return jnp.clip(values, -bound, bound).astype(dtype)


def setup_inputs(seed: int = 0) -> dict:
    key_of = jax.random.split(jax.random.key(seed), 5)
    queries = normal_values(key_of[0], (NQ, QT, E), 1.0, 6.0, ((0, 32),))
    passages = normal_values(key_of[1], (NP, PT, E), 1.0, 6.0, ((0, 8),))
    candidates = draw_candidates(jax.random.fold_in(key_of[4], 71), 0)
    teacher = normal_values(key_of[3], (NQ, C), 2.0, 8.0, ((0, 32),), jnp.float32)
    return {"queries": queries, "passages": passages, "candidates": candidates, "teacher": teacher}


epsilon = 1e-06
softness_scale = 0.05

def normalize(values):
    widened = values.astype(jnp.float32)
    inverse_norm = lax.rsqrt(lax.optimization_barrier(jnp.sum(widened * widened, -1, keepdims=True)) + epsilon)
    return (widened * inverse_norm, inverse_norm)

def token_terms(passage_norm, query_row, passage_ids):
    gathered = jnp.take(passage_norm, passage_ids, axis=0).astype(jnp.float32)
    token_products = jnp.einsum('qe,cpe->cqp', query_row.astype(jnp.float32), gathered)
    power_value = jnp.exp(token_products / softness_scale)
    return (gathered, power_value, lax.optimization_barrier(jnp.sum(power_value, -1)))

def take_shard(values, shard):
    group_count = NQ // (QD * N_QRY)
    shaped = values.reshape((group_count, N_QRY, QD) + values.shape[1:])
    return shaped[:, shard].reshape((group_count * QD,) + values.shape[1:])

def reference(queries, passages, candidates, teacher):
    query_unit, query_inverse = normalize(queries)
    passage_unit, passage_inverse = normalize(passages)
    query_norm = query_unit.astype(jnp.bfloat16)
    passage_norm = passage_unit.astype(jnp.bfloat16)

    def score_one(element):
        reduced_sum = token_terms(passage_norm, element[0], element[1])[2]
        return lax.optimization_barrier(jnp.sum(softness_scale * jnp.log(reduced_sum), -1))
    scores = lax.map(score_one, (query_norm, candidates))
    teacher_exp = jnp.exp(teacher)
    mentor_score_sum = lax.optimization_barrier(jnp.sum(teacher_exp, -1, keepdims=True))
    target = teacher_exp / mentor_score_sum
    log_target = teacher - jnp.log(mentor_score_sum)
    score_exp = jnp.exp(scores)
    score_total = lax.optimization_barrier(jnp.sum(score_exp, -1, keepdims=True))
    likelihood = score_exp / score_total
    pair_loss = lax.optimization_barrier(jnp.sum(target * (log_target - scores), -1)) + jnp.log(score_total[:, 0])
    score_grad = likelihood - target
    group_count = NQ // (QD * N_QRY)
    query_parts = []
    unit_passage_grad = jnp.zeros((NP, PT, E), jnp.float32)
    for shard in range(N_QRY):

        def step(running, element):
            query_row, passage_ids, grad_row = element
            gathered, power_value, reduced_sum = token_terms(passage_norm, query_row, passage_ids)
            weights = (grad_row[:, None, None] * power_value / reduced_sum[:, :, None]).astype(jnp.bfloat16)
            weights = lax.optimization_barrier(weights).astype(jnp.float32)
            query_delta = jnp.einsum('cqp,cpe->qe', weights, gathered)
            pair_grads = jnp.einsum('cqp,qe->cpe', weights, query_row.astype(jnp.float32))
            return (running.at[passage_ids].add(pair_grads), query_delta)
        partial_value, query_grads = lax.scan(step, jnp.zeros((NP, PT, E), jnp.float32), (take_shard(query_norm, shard), take_shard(candidates, shard), take_shard(score_grad, shard)))
        rounded = lax.optimization_barrier(partial_value.astype(jnp.bfloat16))
        unit_passage_grad = unit_passage_grad + rounded.astype(jnp.float32)
        query_parts.append(query_grads.reshape(group_count, QD, QT, E))
    unit_query_grad = jnp.stack(query_parts, 1).reshape(NQ, QT, E)
    grad_queries = query_inverse * (unit_query_grad - query_unit * lax.optimization_barrier(jnp.sum(query_unit * unit_query_grad, -1, keepdims=True)))
    grad_passages = passage_inverse * (unit_passage_grad - passage_unit * lax.optimization_barrier(jnp.sum(passage_unit * unit_passage_grad, -1, keepdims=True)))
    return (pair_loss, grad_queries.astype(jnp.bfloat16), grad_passages.astype(jnp.bfloat16))
```

```python
import math

import jax
import jax.numpy as jnp
from jax import lax
from jax.experimental import pallas as pl
from jax.experimental.pallas import tpu as pltpu
from jax.sharding import PartitionSpec as P

epsilon = 1e-06
softness_scale = 0.05
block_pairs = 16
vmem_bytes = 20 << 20
row_pad = 8

VMEM = pl.BlockSpec(memory_space=pltpu.VMEM)


def params():
    return pltpu.CompilerParams(vmem_limit_bytes=vmem_bytes)


def unit_rows(values):
    widened = values.astype(jnp.float32)
    inverse = lax.rsqrt(jnp.sum(widened * widened, -1, keepdims=True) + epsilon)
    return widened * inverse, inverse


def lane_ids(shape):
    return lax.broadcasted_iota(jnp.int32, shape, len(shape) - 1)


def tangent(raw, grad):
    unit, inverse = unit_rows(raw)
    return inverse * (grad - unit * jnp.sum(unit * grad, -1, keepdims=True))


def passages_kernel(slices, in_ref, norm_ref, flip_ref, own_ref):
    count, tokens, _ = in_ref.shape
    share = tokens // slices
    me = lax.axis_index("qry")
    base = pl.program_id(0) * count
    for item in range(count):
        for place in range(slices):
            start = pl.multiple_of((me ^ place) * share, share)
            raw = in_ref[item, pl.ds(start, share), :]
            if place == 0:
                own_ref[base + item] = raw
            norm_ref[base + item, pl.ds(place * share, share), :] = unit_rows(raw)[0].astype(
                jnp.bfloat16
            )
        flip_ref[base + item] = jnp.transpose(norm_ref[base + item], (1, 0))


def prepare_passages(passages, slices):
    count, tokens, width = passages.shape
    step = math.gcd(count, 8)
    share = tokens // slices
    return pl.pallas_call(
        lambda *refs: passages_kernel(slices, *refs),
        grid=(count // step,),
        in_specs=[pl.BlockSpec((step, tokens, width), lambda i: (i, 0, 0))],
        out_specs=[VMEM, VMEM, VMEM],
        out_shape=[
            pltpu.VMEM((count, tokens, width), jnp.bfloat16),
            pltpu.VMEM((count, width, tokens), jnp.bfloat16),
            pltpu.VMEM((count, share, width), jnp.bfloat16),
        ],
        compiler_params=params(),
        cost_estimate=pl.CostEstimate(flops=1 << 24, bytes_accessed=6 << 20, transcendentals=0),
        name="prepare_passages",
    )(passages)


def each_extra(pass_count, list_smem, count_row, visit):
    def passage_step(p, used):
        pairs = list_smem[count_row, p]
        blocks = (pairs + block_pairs - 1) // block_pairs
        extra = jnp.maximum(blocks - 1, 0)

        def step(b, carry):
            visit(p, (b + 1) * block_pairs, pass_count + used + b)
            return carry

        lax.fori_loop(0, extra, step, 0)
        return used + extra

    lax.fori_loop(0, pass_count, passage_step, jnp.int32(0))


def forward_kernel(
    cand_count,
    query_count,
    query_tokens,
    recv_ref,
    norm_ref,
    soft_ref,
    qn_ref,
    score_ref,
    many_ref,
    target_ref,
    list_ref,
    zw_ref,
    ext_ref,
    low_ref,
    sums_ref,
    list_smem,
    sem,
):
    sources = recv_ref.shape[0]
    pass_count, tokens, width = norm_ref.shape
    group = sources * query_count
    rows = query_count * query_tokens
    stride = group + row_pad
    count_row = list_ref.shape[0] - row_pad
    owner = lax.axis_index("psg").astype(jnp.float32)
    for s in range(sources):
        packed = recv_ref[s, rows : rows + 16, :].astype(jnp.float32)
        ext_ref[s * query_count : (s + 1) * query_count, :] = packed[:query_count]
        low_ref[s * query_count : (s + 1) * query_count, :] = packed[8 : 8 + query_count]
        qn_ref[s * rows : (s + 1) * rows, :] = unit_rows(recv_ref[s, :rows, :])[0].astype(
            jnp.bfloat16
        )
    qn_ref[sources * rows :, :] = jnp.zeros((query_tokens, width), jnp.bfloat16)

    main = ext_ref[...]
    lanes = lane_ids(main.shape)
    lanes_float = lanes.astype(jnp.float32)
    live = lanes < cand_count
    local = pltpu.roll(main, 128 - cand_count, 1)
    logits = (
        pltpu.roll(main, 128 - 2 * cand_count, 1)
        + pltpu.roll(main, 128 - 3 * cand_count, 1)
        + low_ref[...]
    )
    raised = jnp.where(live, jnp.exp(logits), 0.0)
    target = raised / jnp.sum(raised, -1, keepdims=True)
    local = jnp.where(main == owner, local, -1.0)
    many = jnp.zeros(main.shape, jnp.float32)
    wanted = jnp.zeros(main.shape, jnp.float32)
    for c in range(cand_count):
        same = local[:, c : c + 1] == lanes_float
        many = many + jnp.where(same, 1.0, 0.0)
        wanted = wanted + jnp.where(same, target[:, c : c + 1], 0.0)
    many_ref[...] = many
    target_ref[...] = wanted
    active = many > 0.0
    lower = (
        lax.broadcasted_iota(jnp.int32, (group, group), 0)
        > lax.broadcasted_iota(jnp.int32, (group, group), 1)
    ).astype(jnp.bfloat16)
    active_value = jnp.where(active, 1.0, 0.0)
    rank = jnp.dot(lower, active_value.astype(jnp.bfloat16), preferred_element_type=jnp.float32)
    rank = jnp.where(active, rank, -1.0)
    less = lax.broadcasted_iota(jnp.int32, main.shape, 0).astype(jnp.float32) - group
    for k in range(count_row):
        found = jnp.sum(jnp.where(rank == k, less, 0.0), 0, keepdims=True) + group
        list_ref[k : k + 1, :] = found.astype(jnp.int32)
    total = jnp.sum(active_value, 0, keepdims=True).astype(jnp.int32)
    list_ref[count_row:, :] = jnp.broadcast_to(total, (row_pad, 128))
    copy = pltpu.make_async_copy(list_ref, list_smem, sem)
    copy.start()
    copy.wait()

    half = block_pairs // 2

    def block(p, first, slot):
        passage = norm_ref[p]
        for h in range(2):
            ids = [list_smem[first + h * half + r, p] for r in range(half)]
            tile = jnp.concatenate(
                [
                    qn_ref[pl.ds(pl.multiple_of(n * query_tokens, query_tokens), query_tokens), :]
                    for n in ids
                ],
                0,
            )
            dots = lax.dot_general(
                passage, tile, (((1,), (1,)), ((), ())), preferred_element_type=jnp.float32
            )
            power = jnp.exp(dots * (1.0 / softness_scale))
            sums = jnp.sum(power, 0, keepdims=True)
            span = half * query_tokens
            soft_ref[slot, :, h * span : (h + 1) * span] = (power * (1.0 / sums)).astype(
                jnp.bfloat16
            )
            for r in range(half):
                sums_ref[pl.ds(p * stride + ids[r], 1), :query_tokens] = sums[
                    :, r * query_tokens : (r + 1) * query_tokens
                ]

    def step(p, carry):
        block(2 * p, 0, 2 * p)
        block(2 * p + 1, 0, 2 * p + 1)
        return carry

    lax.fori_loop(0, pass_count // 2, step, 0)
    each_extra(pass_count, list_smem, count_row, block)

    scores = jnp.zeros(main.shape, jnp.float32)
    for p in range(pass_count):
        logs = jnp.log(sums_ref[p * stride : p * stride + group, :])
        value = softness_scale * jnp.sum(
            jnp.where(lanes < query_tokens, logs, 0.0), -1, keepdims=True
        )
        scores = jnp.where(lanes == p, value, scores)
    scores = jnp.where(active, scores, 0.0)
    score_ref[...] = scores
    mass = jnp.sum(many * jnp.exp(scores), -1, keepdims=True)
    agreed = jnp.sum(wanted * scores, -1, keepdims=True)
    message = jnp.where(lanes == 0, mass, jnp.where(lanes == 1, agreed, 0.0))
    for s in range(sources):
        zw_ref[s] = message


def forward(received, norm, cand_count, query_count, query_tokens):
    sources = received.shape[0]
    pass_count, tokens, width = norm.shape
    group = sources * query_count
    capacity = max(2, -(-5 * query_count * cand_count // (2 * sources)))
    blocks = pass_count + sources * capacity // block_pairs
    list_rows = -(-group // block_pairs) * block_pairs + row_pad
    rows = query_count * query_tokens
    flops = 2 * pass_count * block_pairs * query_tokens * tokens * width
    return pl.pallas_call(
        lambda *refs: forward_kernel(cand_count, query_count, query_tokens, *refs),
        in_specs=[VMEM, VMEM],
        out_specs=[VMEM] * 7,
        out_shape=[
            pltpu.VMEM((blocks, tokens, block_pairs * query_tokens), jnp.bfloat16),
            pltpu.VMEM((sources * rows + query_tokens, width), jnp.bfloat16),
            pltpu.VMEM((group, 128), jnp.float32),
            pltpu.VMEM((group, 128), jnp.float32),
            pltpu.VMEM((group, 128), jnp.float32),
            pltpu.VMEM((list_rows, 128), jnp.int32),
            jax.ShapeDtypeStruct((sources, group, 128), jnp.float32),
        ],
        scratch_shapes=[
            pltpu.VMEM((group, 128), jnp.float32),
            pltpu.VMEM((group, 128), jnp.float32),
            pltpu.VMEM((pass_count * (group + row_pad), 128), jnp.float32),
            pltpu.SMEM((list_rows, 128), jnp.int32),
            pltpu.SemaphoreType.DMA,
        ],
        compiler_params=params(),
        cost_estimate=pl.CostEstimate(flops=flops, bytes_accessed=12 << 20, transcendentals=1 << 22),
        name="forward",
    )(received, norm)


def attend_kernel(flip_ref, soft_ref, list_ref, out_ref, list_smem, sem):
    pass_count = flip_ref.shape[0]
    copy = pltpu.make_async_copy(list_ref, list_smem, sem)
    copy.start()

    def block(p, first, slot):
        mixed = jnp.dot(flip_ref[p], soft_ref[slot], preferred_element_type=jnp.float32)
        out_ref[slot] = jnp.transpose(mixed, (1, 0)).astype(jnp.bfloat16)

    def step(p, carry):
        block(2 * p, 0, 2 * p)
        block(2 * p + 1, 0, 2 * p + 1)
        return carry

    lax.fori_loop(0, pass_count // 2, step, 0)
    copy.wait()
    each_extra(pass_count, list_smem, list_ref.shape[0] - row_pad, block)


def attend(flip, soft, ids):
    blocks, tokens, columns = soft.shape
    width = flip.shape[1]
    flops = 2 * flip.shape[0] * columns * tokens * width
    return pl.pallas_call(
        attend_kernel,
        in_specs=[VMEM] * 3,
        out_specs=VMEM,
        out_shape=pltpu.VMEM((blocks, columns, width), jnp.bfloat16),
        scratch_shapes=[pltpu.SMEM(ids.shape, jnp.int32), pltpu.SemaphoreType.DMA],
        compiler_params=params(),
        cost_estimate=pl.CostEstimate(flops=flops, bytes_accessed=12 << 20, transcendentals=0),
        name="attend",
    )(flip, soft, ids)


def backward_kernel(
    query_tokens,
    zw_ref,
    score_ref,
    many_ref,
    target_ref,
    list_ref,
    qn_ref,
    soft_ref,
    mixed_ref,
    query_ref,
    own_ref,
    core_ref,
    far_ref,
    cross_ref,
    grad_ref,
    accum_ref,
    list_smem,
    sem,
):
    copy = pltpu.make_async_copy(list_ref, list_smem, sem)
    copy.start()
    sources, group, _ = zw_ref.shape
    pass_count, share, width = own_ref.shape
    stride = group + row_pad
    count_row = list_ref.shape[0] - row_pad
    sums = zw_ref[0]
    for s in range(1, sources):
        sums = sums + zw_ref[s]
    many = many_ref[...]
    grads = many * jnp.exp(score_ref[...]) / sums[:, :1] - target_ref[...]
    for p in range(pass_count):
        grad_ref[p * stride : p * stride + group, :] = jnp.broadcast_to(
            grads[:, p : p + 1], (group, 128)
        )
        grad_ref[p * stride + group : (p + 1) * stride, :] = jnp.zeros((row_pad, 128), jnp.float32)
    accum_ref[...] = jnp.zeros(accum_ref.shape, jnp.float32)
    copy.wait()

    def query_rows(n):
        return pl.ds(pl.multiple_of(n * query_tokens, query_tokens), query_tokens)

    def pair_block(p, first, slot):
        ids = [list_smem[first + r, p] for r in range(block_pairs)]
        scales = [grad_ref[pl.ds(p * stride + n, 1), :] for n in ids]
        tile = jnp.concatenate(
            [
                (qn_ref[query_rows(n), :].astype(jnp.float32) * scale).astype(jnp.bfloat16)
                for n, scale in zip(ids, scales)
            ],
            0,
        )
        added = [
            accum_ref[query_rows(n), :]
            + mixed_ref[slot, r * query_tokens : (r + 1) * query_tokens, :].astype(jnp.float32)
            * scales[r]
            for r, n in enumerate(ids)
        ]
        for n, value in zip(ids, added):
            accum_ref[query_rows(n), :] = value
        return jnp.dot(soft_ref[slot], tile, preferred_element_type=jnp.float32)

    outs = (own_ref, core_ref, far_ref, cross_ref)

    def block(p):
        value = pair_block(p, 0, p).astype(jnp.bfloat16)
        for place, ref in enumerate(outs):
            ref[p] = value[place * share : (place + 1) * share]

    def extra(p, first, slot):
        value = pair_block(p, first, slot)
        for place, ref in enumerate(outs):
            piece = value[place * share : (place + 1) * share]
            ref[p] = (ref[p].astype(jnp.float32) + piece).astype(jnp.bfloat16)

    def step(p, carry):
        block(2 * p)
        block(2 * p + 1)
        return carry

    lax.fori_loop(0, pass_count // 2, step, 0)
    each_extra(pass_count, list_smem, count_row, extra)
    query_ref[...] = accum_ref[: group * query_tokens, :].astype(jnp.bfloat16)


def backward(zw, score, many, target, ids, qn, soft, mixed, pass_count, query_tokens, slices):
    sources, group, _ = zw.shape
    tokens = soft.shape[1]
    width = qn.shape[1]
    piece = jax.ShapeDtypeStruct((pass_count, tokens // slices, width), jnp.bfloat16)
    flops = 2 * pass_count * soft.shape[2] * tokens * width
    return pl.pallas_call(
        lambda *refs: backward_kernel(query_tokens, *refs),
        in_specs=[VMEM] * 8,
        out_specs=[VMEM] * 5,
        out_shape=[
            jax.ShapeDtypeStruct((group * query_tokens, width), jnp.bfloat16),
            piece,
            piece,
            piece,
            piece,
        ],
        scratch_shapes=[
            pltpu.VMEM((pass_count * (group + row_pad), 128), jnp.float32),
            pltpu.VMEM(((group + 1) * query_tokens, width), jnp.float32),
            pltpu.SMEM(ids.shape, jnp.int32),
            pltpu.SemaphoreType.DMA,
        ],
        compiler_params=params(),
        cost_estimate=pl.CostEstimate(flops=flops, bytes_accessed=16 << 20, transcendentals=0),
        name="backward",
    )(zw, score, many, target, ids, qn, soft, mixed)


def finish_kernel(raw_ref, *refs):
    out_ref = refs[-1]
    grad = refs[0][...].astype(jnp.float32)
    for ref in refs[1:-1]:
        grad = grad + ref[...].astype(jnp.float32)
    out_ref[...] = tangent(raw_ref[...], grad).astype(jnp.bfloat16)


def finish(raw, parts):
    shape = raw.shape
    step = math.gcd(shape[0], 8)
    spec = pl.BlockSpec((step,) + shape[1:], lambda i: (i, 0, 0))
    return pl.pallas_call(
        finish_kernel,
        grid=(shape[0] // step,),
        in_specs=[spec] * (1 + len(parts)),
        out_specs=spec,
        out_shape=jax.ShapeDtypeStruct(shape, jnp.bfloat16),
        compiler_params=params(),
        name="finish",
    )(raw, *parts)


def finish_queries_kernel(raw_ref, parts_ref, out_ref):
    grad = parts_ref[0].astype(jnp.float32)
    for s in range(1, parts_ref.shape[0]):
        grad = grad + parts_ref[s].astype(jnp.float32)
    out_ref[...] = tangent(raw_ref[...], grad).astype(jnp.bfloat16)


def finish_queries(raw, parts):
    return pl.pallas_call(
        finish_queries_kernel,
        in_specs=[VMEM, VMEM],
        out_specs=VMEM,
        out_shape=jax.ShapeDtypeStruct(raw.shape, jnp.bfloat16),
        compiler_params=params(),
        name="finish_queries",
    )(raw, parts)


def three_parts(values):
    high = lax.reduce_precision(values, 8, 7)
    rest = values - high
    middle = lax.reduce_precision(rest, 8, 7)
    return high, middle, rest - middle


def shards(queries, passages, candidates, teacher):
    query_count, query_tokens, width = queries.shape
    pass_count = passages.shape[0]
    cand_count = candidates.shape[1]
    sources = lax.axis_size("psg")
    slices = lax.axis_size("qry")
    rows = query_count * query_tokens

    high, middle, low = three_parts(teacher)
    main = jnp.concatenate(
        [
            (candidates // pass_count).astype(jnp.float32),
            (candidates % pass_count).astype(jnp.float32),
            high,
            middle,
        ],
        1,
    )
    low = jnp.pad(low, ((0, 8 - query_count), (0, 128 - cand_count)))
    main = jnp.pad(main, ((0, 8 - query_count), (0, 0)))
    packed = jnp.concatenate(
        [queries.reshape(rows, width), main.astype(jnp.bfloat16), low.astype(jnp.bfloat16)], 0
    )
    received = lax.all_to_all(
        jnp.broadcast_to(packed[None], (sources,) + packed.shape),
        "psg",
        split_axis=0,
        concat_axis=0,
        tiled=True,
    )
    norm, flip, own_raw = prepare_passages(passages, slices)
    soft, qn, score, many, target, ids, zw = forward(
        received, norm, cand_count, query_count, query_tokens
    )
    zw = lax.all_to_all(zw, "psg", split_axis=0, concat_axis=0, tiled=True)
    mixed = attend(flip, soft, ids)
    query_parts, own, core, far, cross = backward(
        zw, score, many, target, ids, qn, soft, mixed, pass_count, query_tokens, slices
    )

    near = [(k, k ^ 1) for k in range(slices)]
    away = [(k, k ^ 2) for k in range(slices)]
    cross = lax.ppermute(cross, "qry", near)
    far = (far.astype(jnp.float32) + cross.astype(jnp.float32)).astype(jnp.bfloat16)
    far = lax.ppermute(far, "qry", away)
    core = lax.ppermute(core, "qry", near)
    query_parts = lax.all_to_all(
        query_parts.reshape(sources, rows, width), "psg", split_axis=0, concat_axis=0, tiled=True
    )
    grad_queries = finish_queries(queries.reshape(rows, width), query_parts)
    grad_passages = finish(own_raw, [own, core, far])

    raised = jnp.exp(teacher)
    raised_sum = jnp.sum(raised, -1, keepdims=True)
    log_target = teacher - jnp.log(raised_sum)
    known = jnp.sum(raised / raised_sum * log_target, -1)
    mine = lax.dynamic_slice_in_dim(
        zw[:, :, :2], lax.axis_index("psg") * query_count, query_count, 1
    )
    mine = jnp.sum(mine, 0)
    pair_loss = known - mine[:, 1] + jnp.log(mine[:, 0])
    return (pair_loss, grad_queries.reshape(queries.shape), grad_passages)


def solution(mesh):
    placed = (
        P(("psg", "qry"), None, None),
        P("psg", None, None),
        P(("psg", "qry"), None),
        P(("psg", "qry"), None),
    )
    return jax.shard_map(
        shards,
        mesh=mesh,
        in_specs=placed,
        out_specs=(P(("psg", "qry")), P(("psg", "qry"), None, None), P("psg", "qry", None)),
        check_vma=False,
    )
```

```python
import math

import jax
import jax.numpy as jnp
from jax import lax
from jax.experimental import pallas as pl
from jax.experimental.pallas import tpu as pltpu
from jax.sharding import PartitionSpec as P

epsilon = 1e-06
softness_scale = 0.05
block_pairs = 16
vmem_bytes = 44 << 20
row_pad = 8

VMEM = pl.BlockSpec(memory_space=pltpu.VMEM)
HBM = pl.BlockSpec(memory_space=pltpu.HBM)
unroll = 4


def in_hbm(array):
    return pltpu.with_memory_space_constraint(array, pltpu.HBM)


def params():
    return pltpu.CompilerParams(vmem_limit_bytes=vmem_bytes)


def unit_rows(values):
    widened = values.astype(jnp.float32)
    inverse = lax.rsqrt(jnp.sum(widened * widened, -1, keepdims=True) + epsilon)
    return widened * inverse, inverse


def round_bf16(values):
    return values.astype(jnp.bfloat16).astype(jnp.float32)


def pack_kernel(pass_count, *refs):
    sources, targets, out_ref, sems = refs[:3], refs[4:7], refs[3], refs[7]
    copies = [
        pltpu.make_async_copy(source, target, sems.at[i])
        for i, (source, target) in enumerate(zip(sources, targets))
    ]
    for copy in copies:
        copy.start()
    for copy in copies:
        copy.wait()
    queries_ref, candidates_ref, teacher_ref = targets
    query_count, cand_count = teacher_ref.shape
    ids = candidates_ref[...].astype(jnp.float32)
    owner = jnp.floor((ids + 0.5) * (1.0 / pass_count))
    values = teacher_ref[...]
    high = round_bf16(values)
    middle = round_bf16(values - high)
    low = values - high - middle
    main = jnp.concatenate([owner, ids - owner * pass_count, high, middle], 1)
    blank = jnp.zeros((8 - query_count, 128), jnp.float32)
    low = jnp.concatenate([low, jnp.zeros((query_count, 128 - cand_count), jnp.float32)], 1)
    extra = jnp.concatenate([main, blank, low, blank], 0).astype(jnp.bfloat16)
    rows = queries_ref.shape[0]
    for d in range(out_ref.shape[0]):
        out_ref[d, :rows, :] = queries_ref[...]
        out_ref[d, rows:, :] = extra


def pack(queries, candidates, teacher, sources, pass_count):
    rows, width = queries.shape
    return pl.pallas_call(
        lambda *refs: pack_kernel(pass_count, *refs),
        in_specs=[HBM] * 3,
        out_specs=VMEM,
        out_shape=jax.ShapeDtypeStruct((sources, rows + 16, width), jnp.bfloat16),
        scratch_shapes=[
            pltpu.VMEM(queries.shape, queries.dtype),
            pltpu.VMEM(candidates.shape, candidates.dtype),
            pltpu.VMEM(teacher.shape, teacher.dtype),
            pltpu.SemaphoreType.DMA((3,)),
        ],
        compiler_params=params(),
        name="pack",
    )(in_hbm(queries), in_hbm(candidates), in_hbm(teacher))


def lane_ids(shape):
    return lax.broadcasted_iota(jnp.int32, shape, len(shape) - 1)


def tangent(raw, grad):
    unit, inverse = unit_rows(raw)
    return inverse * (grad - unit * jnp.sum(unit * grad, -1, keepdims=True))


def passages_kernel(slices, in_ref, norm_ref, flip_ref, own_ref):
    count, tokens, _ = in_ref.shape
    share = tokens // slices
    me = lax.axis_index("qry")
    for item in range(count):
        for place in range(slices):
            start = pl.multiple_of((me ^ place) * share, share)
            raw = in_ref[item, pl.ds(start, share), :]
            if place == 0:
                own_ref[item] = raw
            norm_ref[item, pl.ds(place * share, share), :] = unit_rows(raw)[0].astype(
                jnp.bfloat16
            )
        flip_ref[item] = jnp.transpose(norm_ref[item], (1, 0))


def prepare_passages(passages, slices):
    count, tokens, width = passages.shape
    step = math.gcd(count, 8)
    share = tokens // slices
    return pl.pallas_call(
        lambda *refs: passages_kernel(slices, *refs),
        grid=(count // step,),
        in_specs=[pl.BlockSpec((step, tokens, width), lambda i: (i, 0, 0))],
        out_specs=[
            pl.BlockSpec((step, tokens, width), lambda i: (i, 0, 0)),
            pl.BlockSpec((step, width, tokens), lambda i: (i, 0, 0)),
            pl.BlockSpec((step, share, width), lambda i: (i, 0, 0)),
        ],
        out_shape=[
            jax.ShapeDtypeStruct((count, tokens, width), jnp.bfloat16),
            jax.ShapeDtypeStruct((count, width, tokens), jnp.bfloat16),
            jax.ShapeDtypeStruct((count, share, width), jnp.bfloat16),
        ],
        compiler_params=params(),
        cost_estimate=pl.CostEstimate(flops=1 << 24, bytes_accessed=6 << 20, transcendentals=0),
        name="prepare_passages",
    )(in_hbm(passages))


def each_extra(pass_count, list_smem, count_row, visit):
    def passage_step(p, used):
        pairs = list_smem[count_row, p]
        blocks = (pairs + block_pairs - 1) // block_pairs
        extra = jnp.maximum(blocks - 1, 0)

        def step(b, carry):
            visit(p, (b + 1) * block_pairs, pass_count + used + b)
            return carry

        lax.fori_loop(0, extra, step, 0)
        return used + extra

    return lax.fori_loop(0, pass_count, passage_step, jnp.int32(0))


def forward_kernel(
    cand_count,
    query_count,
    query_tokens,
    recv_ref,
    norm_hbm,
    soft_hbm,
    qn_ref,
    score_ref,
    many_ref,
    target_ref,
    list_ref,
    zw_ref,
    norm_ref,
    soft_ref,
    ext_ref,
    low_ref,
    sums_ref,
    list_smem,
    sem,
    norm_sem,
    soft_sems,
):
    norm_copy = pltpu.make_async_copy(norm_hbm, norm_ref, norm_sem)
    norm_copy.start()
    sources = recv_ref.shape[0]
    pass_count, tokens, width = norm_ref.shape
    group = sources * query_count
    rows = query_count * query_tokens
    stride = group + row_pad
    count_row = list_ref.shape[0] - row_pad
    owner = lax.axis_index("psg").astype(jnp.float32)
    for s in range(sources):
        packed = recv_ref[s, rows : rows + 16, :].astype(jnp.float32)
        ext_ref[s * query_count : (s + 1) * query_count, :] = packed[:query_count]
        low_ref[s * query_count : (s + 1) * query_count, :] = packed[8 : 8 + query_count]
        qn_ref[s * rows : (s + 1) * rows, :] = unit_rows(recv_ref[s, :rows, :])[0].astype(
            jnp.bfloat16
        )
    qn_ref[sources * rows :, :] = jnp.zeros((query_tokens, width), jnp.bfloat16)

    main = ext_ref[...]
    lanes = lane_ids(main.shape)
    lanes_float = lanes.astype(jnp.float32)
    live = lanes < cand_count
    local = pltpu.roll(main, 128 - cand_count, 1)
    logits = (
        pltpu.roll(main, 128 - 2 * cand_count, 1)
        + pltpu.roll(main, 128 - 3 * cand_count, 1)
        + low_ref[...]
    )
    raised = jnp.where(live, jnp.exp(logits), 0.0)
    target = raised / jnp.sum(raised, -1, keepdims=True)
    local = jnp.where(main == owner, local, -1.0)
    many = jnp.zeros(main.shape, jnp.float32)
    wanted = jnp.zeros(main.shape, jnp.float32)
    for c in range(cand_count):
        same = local[:, c : c + 1] == lanes_float
        many = many + jnp.where(same, 1.0, 0.0)
        wanted = wanted + jnp.where(same, target[:, c : c + 1], 0.0)
    many_ref[...] = many
    target_ref[...] = wanted
    active = many > 0.0
    lower = (
        lax.broadcasted_iota(jnp.int32, (group, group), 0)
        > lax.broadcasted_iota(jnp.int32, (group, group), 1)
    ).astype(jnp.bfloat16)
    active_value = jnp.where(active, 1.0, 0.0)
    rank = jnp.dot(lower, active_value.astype(jnp.bfloat16), preferred_element_type=jnp.float32)
    rank = jnp.where(active, rank, -1.0)
    less = lax.broadcasted_iota(jnp.int32, main.shape, 0).astype(jnp.float32) - group
    for k in range(count_row):
        found = jnp.sum(jnp.where(rank == k, less, 0.0), 0, keepdims=True) + group
        list_ref[k : k + 1, :] = found.astype(jnp.int32)
    total = jnp.sum(active_value, 0, keepdims=True).astype(jnp.int32)
    list_ref[count_row:, :] = jnp.broadcast_to(total, (row_pad, 128))
    copy = pltpu.make_async_copy(list_ref, list_smem, sem)
    copy.start()
    norm_copy.wait()
    copy.wait()

    half = block_pairs // 2

    def soft_copy(slot):
        return pltpu.make_async_copy(soft_ref.at[slot], soft_hbm.at[slot], soft_sems.at[slot])

    def block(p, first, slot):
        passage = norm_ref[p]
        for h in range(2):
            ids = [list_smem[first + h * half + r, p] for r in range(half)]
            tile = jnp.concatenate(
                [
                    qn_ref[pl.ds(pl.multiple_of(n * query_tokens, query_tokens), query_tokens), :]
                    for n in ids
                ],
                0,
            )
            dots = lax.dot_general(
                passage, tile, (((1,), (1,)), ((), ())), preferred_element_type=jnp.float32
            )
            power = jnp.exp2(dots * (math.log2(math.e) / softness_scale))
            sums = jnp.sum(power, 0, keepdims=True)
            span = half * query_tokens
            soft_ref[slot, :, h * span : (h + 1) * span] = (power * (1.0 / sums)).astype(
                jnp.bfloat16
            )
            for r in range(half):
                sums_ref[pl.ds(p * stride + ids[r], 1), :query_tokens] = sums[
                    :, r * query_tokens : (r + 1) * query_tokens
                ]

    def step(p, carry):
        for u in range(unroll):
            block(unroll * p + u, 0, unroll * p + u)
        for u in range(unroll):
            soft_copy(unroll * p + u).start()
        return carry

    def extra(p, first, slot):
        block(p, first, slot)
        soft_copy(slot).start()

    lax.fori_loop(0, pass_count // unroll, step, 0)
    used = each_extra(pass_count, list_smem, count_row, extra)

    scores = jnp.zeros(main.shape, jnp.float32)
    for p in range(pass_count):
        logs = jnp.log(sums_ref[p * stride : p * stride + group, :])
        value = softness_scale * jnp.sum(
            jnp.where(lanes < query_tokens, logs, 0.0), -1, keepdims=True
        )
        scores = jnp.where(lanes == p, value, scores)
    scores = jnp.where(active, scores, 0.0)
    score_ref[...] = scores
    mass = jnp.sum(many * jnp.exp(scores), -1, keepdims=True)
    agreed = jnp.sum(wanted * scores, -1, keepdims=True)
    message = jnp.where(lanes == 0, mass, jnp.where(lanes == 1, agreed, 0.0))
    for s in range(sources):
        zw_ref[s] = message

    def drain(slot, carry):
        soft_copy(slot).wait()
        return carry

    lax.fori_loop(0, pass_count + used, drain, 0)


def forward(received, norm, cand_count, query_count, query_tokens):
    sources = received.shape[0]
    pass_count, tokens, width = norm.shape
    group = sources * query_count
    capacity = max(2, -(-5 * query_count * cand_count // (2 * sources)))
    blocks = pass_count + sources * capacity // block_pairs
    list_rows = -(-group // block_pairs) * block_pairs + row_pad
    rows = query_count * query_tokens
    soft_shape = (blocks, tokens, block_pairs * query_tokens)
    flops = 2 * pass_count * block_pairs * query_tokens * tokens * width
    return pl.pallas_call(
        lambda *refs: forward_kernel(cand_count, query_count, query_tokens, *refs),
        in_specs=[VMEM, HBM],
        out_specs=[HBM] + [VMEM] * 6,
        out_shape=[
            pltpu.HBM(soft_shape, jnp.bfloat16),
            jax.ShapeDtypeStruct((sources * rows + query_tokens, width), jnp.bfloat16),
            jax.ShapeDtypeStruct((group, 128), jnp.float32),
            jax.ShapeDtypeStruct((group, 128), jnp.float32),
            jax.ShapeDtypeStruct((group, 128), jnp.float32),
            jax.ShapeDtypeStruct((list_rows, 128), jnp.int32),
            jax.ShapeDtypeStruct((sources, group, 128), jnp.float32),
        ],
        scratch_shapes=[
            pltpu.VMEM(norm.shape, jnp.bfloat16),
            pltpu.VMEM(soft_shape, jnp.bfloat16),
            pltpu.VMEM((group, 128), jnp.float32),
            pltpu.VMEM((group, 128), jnp.float32),
            pltpu.VMEM((pass_count * (group + row_pad), 128), jnp.float32),
            pltpu.SMEM((list_rows, 128), jnp.int32),
            pltpu.SemaphoreType.DMA,
            pltpu.SemaphoreType.DMA,
            pltpu.SemaphoreType.DMA((blocks,)),
        ],
        compiler_params=params(),
        cost_estimate=pl.CostEstimate(flops=flops, bytes_accessed=12 << 20, transcendentals=1 << 22),
        name="forward",
    )(received, in_hbm(norm))


def spread(ref, values, pass_count, stride):
    group = values.shape[0]
    for p in range(pass_count):
        ref[p * stride : p * stride + group, :] = jnp.broadcast_to(
            values[:, p : p + 1], (group, 128)
        )
        ref[p * stride + group : (p + 1) * stride, :] = jnp.zeros((stride - group, 128), jnp.float32)


def attend_kernel(
    query_tokens,
    flip_hbm,
    soft_hbm,
    list_ref,
    score_ref,
    many_ref,
    target_ref,
    raised_ref,
    wanted_ref,
    flip_ref,
    soft_ref,
    raised_rows,
    wanted_rows,
    raised_sum,
    wanted_sum,
    list_smem,
    sem,
    flip_sem,
    soft_sems,
):
    pass_count = flip_ref.shape[0]
    group = score_ref.shape[0]
    stride = group + row_pad
    list_copy = pltpu.make_async_copy(list_ref, list_smem, sem)
    list_copy.start()
    flip_copy = pltpu.make_async_copy(flip_hbm, flip_ref, flip_sem)
    flip_copy.start()

    def soft_copy(slot):
        return pltpu.make_async_copy(soft_hbm.at[slot], soft_ref.at[slot], soft_sems.at[slot])

    def fetch(slot, carry):
        soft_copy(slot).start()
        return carry

    lax.fori_loop(0, pass_count, fetch, 0)
    spread(raised_rows, many_ref[...] * jnp.exp(score_ref[...]), pass_count, stride)
    spread(wanted_rows, target_ref[...], pass_count, stride)
    raised_sum[...] = jnp.zeros(raised_sum.shape, jnp.float32)
    wanted_sum[...] = jnp.zeros(wanted_sum.shape, jnp.float32)
    list_copy.wait()
    flip_copy.wait()

    def block(p, first, slot):
        mixed = jnp.dot(flip_ref[p], soft_ref[slot], preferred_element_type=jnp.float32)
        mixed = jnp.transpose(mixed, (1, 0))
        ids = [list_smem[first + r, p] for r in range(block_pairs)]
        places = [pl.ds(pl.multiple_of(n * query_tokens, query_tokens), query_tokens) for n in ids]
        for total, rows in ((raised_sum, raised_rows), (wanted_sum, wanted_rows)):
            added = [
                total[place, :]
                + mixed[r * query_tokens : (r + 1) * query_tokens]
                * rows[pl.ds(p * stride + ids[r], 1), :]
                for r, place in enumerate(places)
            ]
            for place, value in zip(places, added):
                total[place, :] = value

    def step(p, carry):
        for u in range(unroll):
            soft_copy(unroll * p + u).wait()
        for u in range(unroll):
            block(unroll * p + u, 0, unroll * p + u)
        return carry

    def extra(p, first, slot):
        soft_copy(slot).start()
        soft_copy(slot).wait()
        block(p, first, slot)

    lax.fori_loop(0, pass_count // unroll, step, 0)
    each_extra(pass_count, list_smem, list_ref.shape[0] - row_pad, extra)
    raised_ref[...] = raised_sum[: group * query_tokens, :]
    wanted_ref[...] = wanted_sum[: group * query_tokens, :]


def attend(flip, soft, ids, score, many, target, query_tokens):
    blocks, tokens, columns = soft.shape
    pass_count, width, _ = flip.shape
    group = score.shape[0]
    flops = 2 * pass_count * columns * tokens * width
    total = jax.ShapeDtypeStruct((group * query_tokens, width), jnp.float32)
    rows = pltpu.VMEM((pass_count * (group + row_pad), 128), jnp.float32)
    padded = pltpu.VMEM(((group + 1) * query_tokens, width), jnp.float32)
    return pl.pallas_call(
        lambda *refs: attend_kernel(query_tokens, *refs),
        in_specs=[HBM, HBM] + [VMEM] * 4,
        out_specs=[VMEM] * 2,
        out_shape=[total, total],
        scratch_shapes=[
            pltpu.VMEM(flip.shape, jnp.bfloat16),
            pltpu.VMEM(soft.shape, jnp.bfloat16),
            rows,
            rows,
            padded,
            padded,
            pltpu.SMEM(ids.shape, jnp.int32),
            pltpu.SemaphoreType.DMA,
            pltpu.SemaphoreType.DMA,
            pltpu.SemaphoreType.DMA((blocks,)),
        ],
        compiler_params=params(),
        cost_estimate=pl.CostEstimate(flops=flops, bytes_accessed=12 << 20, transcendentals=0),
        name="attend",
    )(in_hbm(flip), in_hbm(soft), ids, score, many, target)


def halving_order(count):
    order = [0]
    bit = count // 2
    while bit:
        order = order + [x | bit for x in order]
        bit //= 2
    return order


def query_kernel(
    query_tokens,
    zw_ref,
    score_ref,
    many_ref,
    target_ref,
    raised_ref,
    wanted_ref,
    keep_ref,
    send_ref,
    grads_ref,
    scale_ref,
    query_ref,
):
    sources, group, _ = zw_ref.shape
    sums = zw_ref[0]
    for s in range(1, sources):
        sums = sums + zw_ref[s]
    inverse = 1.0 / sums[:, :1]
    grads_ref[...] = many_ref[...] * jnp.exp(score_ref[...]) * inverse - target_ref[...]
    scale_ref[...] = jnp.broadcast_to(inverse, scale_ref.shape)
    for n in range(group):
        place = pl.ds(n * query_tokens, query_tokens)
        query_ref[place, :] = (
            raised_ref[place, :] * scale_ref[n : n + 1, :] - wanted_ref[place, :]
        ).astype(jnp.bfloat16)
    me = lax.axis_index("psg")
    rows = group // sources * query_tokens
    half = keep_ref.shape[0]
    for place, d in enumerate(halving_order(sources)):
        start = pl.multiple_of((me ^ d) * rows, rows)
        value = query_ref[pl.ds(start, rows), :]
        if place < half:
            keep_ref[place] = value
        else:
            send_ref[place - half] = value


def query_backward(zw, score, many, target, raised, wanted):
    sources, group, _ = zw.shape
    rows, width = raised.shape
    part = jax.ShapeDtypeStruct((sources // 2, rows // sources, width), jnp.bfloat16)
    return pl.pallas_call(
        lambda *refs: query_kernel(rows // group, *refs),
        in_specs=[VMEM] * 6,
        out_specs=[VMEM] * 3,
        out_shape=[part, part, jax.ShapeDtypeStruct((group, 128), jnp.float32)],
        scratch_shapes=[
            pltpu.VMEM((group, 128), jnp.float32),
            pltpu.VMEM((rows, width), jnp.bfloat16),
        ],
        compiler_params=params(),
        name="query_backward",
    )(zw, score, many, target, raised, wanted)


def passage_kernel(
    query_tokens,
    list_ref,
    grads_ref,
    qn_ref,
    soft_hbm,
    own_ref,
    core_ref,
    far_ref,
    cross_ref,
    soft_ref,
    grad_ref,
    list_smem,
    sem,
    soft_sems,
):
    list_copy = pltpu.make_async_copy(list_ref, list_smem, sem)
    list_copy.start()
    pass_count, share, width = own_ref.shape
    stride = grads_ref.shape[0] + row_pad
    count_row = list_ref.shape[0] - row_pad

    def soft_copy(slot):
        return pltpu.make_async_copy(soft_hbm.at[slot], soft_ref.at[slot], soft_sems.at[slot])

    def fetch(slot, carry):
        soft_copy(slot).start()
        return carry

    lax.fori_loop(0, pass_count, fetch, 0)
    spread(grad_ref, grads_ref[...], pass_count, stride)
    list_copy.wait()

    def product(p, first, slot):
        ids = [list_smem[first + r, p] for r in range(block_pairs)]
        tile = jnp.concatenate(
            [
                (
                    qn_ref[
                        pl.ds(pl.multiple_of(n * query_tokens, query_tokens), query_tokens), :
                    ].astype(jnp.float32)
                    * grad_ref[pl.ds(p * stride + n, 1), :]
                ).astype(jnp.bfloat16)
                for n in ids
            ],
            0,
        )
        return jnp.dot(soft_ref[slot], tile, preferred_element_type=jnp.float32)

    outs = (own_ref, core_ref, far_ref, cross_ref)

    def step(p, carry):
        for u in range(unroll):
            soft_copy(unroll * p + u).wait()
        for u in range(unroll):
            value = product(unroll * p + u, 0, unroll * p + u).astype(jnp.bfloat16)
            for place, ref in enumerate(outs):
                ref[unroll * p + u] = value[place * share : (place + 1) * share]
        return carry

    def extra(p, first, slot):
        soft_copy(slot).start()
        soft_copy(slot).wait()
        value = product(p, first, slot)
        for place, ref in enumerate(outs):
            piece = value[place * share : (place + 1) * share]
            ref[p] = (ref[p].astype(jnp.float32) + piece).astype(jnp.bfloat16)

    lax.fori_loop(0, pass_count // unroll, step, 0)
    each_extra(pass_count, list_smem, count_row, extra)


def passage_backward(ids, grads, qn, soft, pass_count, query_tokens, slices):
    tokens = soft.shape[1]
    width = qn.shape[1]
    piece = jax.ShapeDtypeStruct((pass_count, tokens // slices, width), jnp.bfloat16)
    flops = 2 * pass_count * soft.shape[2] * tokens * width
    return pl.pallas_call(
        lambda *refs: passage_kernel(query_tokens, *refs),
        in_specs=[VMEM] * 3 + [HBM],
        out_specs=[VMEM] * 4,
        out_shape=[piece] * 4,
        scratch_shapes=[
            pltpu.VMEM(soft.shape, jnp.bfloat16),
            pltpu.VMEM((pass_count * (grads.shape[0] + row_pad), 128), jnp.float32),
            pltpu.SMEM(ids.shape, jnp.int32),
            pltpu.SemaphoreType.DMA,
            pltpu.SemaphoreType.DMA((soft.shape[0],)),
        ],
        compiler_params=params(),
        cost_estimate=pl.CostEstimate(flops=flops, bytes_accessed=12 << 20, transcendentals=0),
        name="passage_backward",
    )(ids, grads, qn, in_hbm(soft))


def finish_kernel(raw_ref, *refs):
    out_ref = refs[-1]
    grad = refs[0][...].astype(jnp.float32)
    for ref in refs[1:-1]:
        grad = grad + ref[...].astype(jnp.float32)
    out_ref[...] = tangent(raw_ref[...], grad).astype(jnp.bfloat16)


def finish(raw, parts):
    shape = raw.shape
    step = math.gcd(shape[0], 8)
    spec = pl.BlockSpec((step,) + shape[1:], lambda i: (i, 0, 0))
    return pl.pallas_call(
        finish_kernel,
        grid=(shape[0] // step,),
        in_specs=[spec] * (1 + len(parts)),
        out_specs=spec,
        out_shape=jax.ShapeDtypeStruct(shape, jnp.bfloat16),
        compiler_params=params(),
        name="finish",
    )(raw, *parts)


def finish_queries(raw, parts):
    return pl.pallas_call(
        finish_kernel,
        in_specs=[VMEM] * (1 + len(parts)),
        out_specs=VMEM,
        out_shape=jax.ShapeDtypeStruct(raw.shape, jnp.bfloat16),
        compiler_params=params(),
        name="finish_queries",
    )(raw, *parts)


def shards(queries, passages, candidates, teacher):
    query_count, query_tokens, width = queries.shape
    pass_count = passages.shape[0]
    cand_count = candidates.shape[1]
    sources = lax.axis_size("psg")
    slices = lax.axis_size("qry")
    rows = query_count * query_tokens

    received = lax.all_to_all(
        pack(queries.reshape(rows, width), candidates, teacher, sources, pass_count),
        "psg",
        split_axis=0,
        concat_axis=0,
        tiled=True,
    )
    norm, flip, own_raw = prepare_passages(passages, slices)
    soft, qn, score, many, target, ids, zw = forward(
        received, norm, cand_count, query_count, query_tokens
    )
    zw = lax.all_to_all(zw, "psg", split_axis=0, concat_axis=0, tiled=True)
    raised_sum, wanted_sum = attend(flip, soft, ids, score, many, target, query_tokens)
    keep, send, grads = query_backward(zw, score, many, target, raised_sum, wanted_sum)
    bit = 1
    while bit < sources:
        swap = [(i, i ^ bit) for i in range(sources)]
        send = lax.ppermute(send, "psg", swap)
        if bit * 2 < sources:
            total = keep.astype(jnp.float32) + send.astype(jnp.float32)
            half = total.shape[0] // 2
            keep, send = total[:half], total[half:].astype(jnp.bfloat16)
        bit *= 2
    grad_queries = finish_queries(queries.reshape(rows, width), [keep[0], send[0]])

    own, core, far, cross = passage_backward(
        ids, grads, qn, soft, pass_count, query_tokens, slices
    )
    near = [(k, k ^ 1) for k in range(slices)]
    away = [(k, k ^ 2) for k in range(slices)]
    cross = lax.ppermute(cross, "qry", near)
    far = (far.astype(jnp.float32) + cross.astype(jnp.float32)).astype(jnp.bfloat16)
    far = lax.ppermute(far, "qry", away)
    core = lax.ppermute(core, "qry", near)
    grad_passages = finish(own_raw, [own, core, far])

    raised = jnp.exp(teacher)
    raised_sum = jnp.sum(raised, -1, keepdims=True)
    log_target = teacher - jnp.log(raised_sum)
    known = jnp.sum(raised / raised_sum * log_target, -1)
    mine = lax.dynamic_slice_in_dim(
        zw[:, :, :2], lax.axis_index("psg") * query_count, query_count, 1
    )
    mine = jnp.sum(mine, 0)
    pair_loss = known - mine[:, 1] + jnp.log(mine[:, 0])
    return (pair_loss, grad_queries.reshape(queries.shape), grad_passages)


def solution(mesh):
    placed = (
        P(("psg", "qry"), None, None),
        P("psg", None, None),
        P(("psg", "qry"), None),
        P(("psg", "qry"), None),
    )
    return jax.shard_map(
        shards,
        mesh=mesh,
        in_specs=placed,
        out_specs=(P(("psg", "qry")), P(("psg", "qry"), None, None), P("psg", "qry", None)),
        check_vma=False,
    )
```

```python
import math

import jax
import jax.numpy as jnp
from jax import lax
from jax.experimental import pallas as pl
from jax.experimental.pallas import tpu as pltpu
from jax.sharding import PartitionSpec as P

epsilon = 1e-06
softness_scale = 0.05
chunk_pairs = 8
vmem_bytes = 44 << 20
row_pad = 8

VMEM = pl.BlockSpec(memory_space=pltpu.VMEM)
HBM = pl.BlockSpec(memory_space=pltpu.HBM)
chunk_unroll = 8
passage_unroll = 4
copy_parts = 8
meta_rows = 8


def in_hbm(array):
    return pltpu.with_memory_space_constraint(array, pltpu.HBM)


def params():
    return pltpu.CompilerParams(vmem_limit_bytes=vmem_bytes)


def unit_rows(values):
    widened = values.astype(jnp.float32)
    inverse = lax.rsqrt(jnp.sum(widened * widened, -1, keepdims=True) + epsilon)
    return widened * inverse, inverse


def round_bf16(values):
    return values.astype(jnp.bfloat16).astype(jnp.float32)


def pack_kernel(pass_count, *refs):
    sources, targets, out_ref, sems = refs[:3], refs[4:7], refs[3], refs[7]
    copies = [
        pltpu.make_async_copy(source, target, sems.at[i])
        for i, (source, target) in enumerate(zip(sources, targets))
    ]
    for copy in copies:
        copy.start()
    for copy in copies:
        copy.wait()
    queries_ref, candidates_ref, teacher_ref = targets
    query_count, cand_count = teacher_ref.shape
    ids = candidates_ref[...].astype(jnp.float32)
    owner = jnp.floor((ids + 0.5) * (1.0 / pass_count))
    values = teacher_ref[...]
    high = round_bf16(values)
    middle = round_bf16(values - high)
    low = values - high - middle
    main = jnp.concatenate([owner, ids - owner * pass_count, high, middle], 1)
    blank = jnp.zeros((8 - query_count, 128), jnp.float32)
    low = jnp.concatenate([low, jnp.zeros((query_count, 128 - cand_count), jnp.float32)], 1)
    extra = jnp.concatenate([main, blank, low, blank], 0).astype(jnp.bfloat16)
    rows = queries_ref.shape[0]
    for d in range(out_ref.shape[0]):
        out_ref[d, :rows, :] = queries_ref[...]
        out_ref[d, rows:, :] = extra


def pack(queries, candidates, teacher, sources, pass_count):
    rows, width = queries.shape
    return pl.pallas_call(
        lambda *refs: pack_kernel(pass_count, *refs),
        in_specs=[HBM] * 3,
        out_specs=VMEM,
        out_shape=jax.ShapeDtypeStruct((sources, rows + 16, width), jnp.bfloat16),
        scratch_shapes=[
            pltpu.VMEM(queries.shape, queries.dtype),
            pltpu.VMEM(candidates.shape, candidates.dtype),
            pltpu.VMEM(teacher.shape, teacher.dtype),
            pltpu.SemaphoreType.DMA((3,)),
        ],
        compiler_params=params(),
        name="pack",
    )(in_hbm(queries), in_hbm(candidates), in_hbm(teacher))


def lane_ids(shape):
    return lax.broadcasted_iota(jnp.int32, shape, len(shape) - 1)


def tangent(raw, grad):
    unit, inverse = unit_rows(raw)
    return inverse * (grad - unit * jnp.sum(unit * grad, -1, keepdims=True))


def passages_kernel(slices, in_ref, norm_ref, flip_ref, own_ref):
    count, tokens, _ = in_ref.shape
    share = tokens // slices
    me = lax.axis_index("qry")
    for item in range(count):
        for place in range(slices):
            start = pl.multiple_of((me ^ place) * share, share)
            raw = in_ref[item, pl.ds(start, share), :]
            if place == 0:
                own_ref[item] = raw
            norm_ref[item, pl.ds(place * share, share), :] = unit_rows(raw)[0].astype(
                jnp.bfloat16
            )
        flip_ref[item] = jnp.transpose(norm_ref[item], (1, 0))


def prepare_passages(passages, slices):
    count, tokens, width = passages.shape
    step = math.gcd(count, 8)
    share = tokens // slices
    return pl.pallas_call(
        lambda *refs: passages_kernel(slices, *refs),
        grid=(count // step,),
        in_specs=[pl.BlockSpec((step, tokens, width), lambda i: (i, 0, 0))],
        out_specs=[
            pl.BlockSpec((step, tokens, width), lambda i: (i, 0, 0)),
            pl.BlockSpec((step, width, tokens), lambda i: (i, 0, 0)),
            pl.BlockSpec((step, share, width), lambda i: (i, 0, 0)),
        ],
        out_shape=[
            pltpu.HBM((count, tokens, width), jnp.bfloat16),
            pltpu.HBM((count, width, tokens), jnp.bfloat16),
            pltpu.HBM((count, share, width), jnp.bfloat16),
        ],
        compiler_params=params(),
        cost_estimate=pl.CostEstimate(flops=1 << 24, bytes_accessed=6 << 20, transcendentals=0),
        name="prepare_passages",
    )(in_hbm(passages))


def list_layout(group):
    empty = -(-group // chunk_pairs) * chunk_pairs
    return empty, empty + chunk_pairs


def slot_total(pass_count, pairs):
    worst = (pairs + pass_count * (chunk_pairs - 1)) // chunk_pairs
    return -(-(worst + 1) // chunk_unroll) * chunk_unroll


def steps_of(list_smem, tables):
    total = list_smem[tables + 4, 0]
    return jnp.maximum((total + chunk_unroll - 1) // chunk_unroll, 1)


def part_copies(source, target, sems):
    size = source.shape[0] // copy_parts
    return [
        pltpu.make_async_copy(
            source.at[pl.ds(i * size, size)], target.at[pl.ds(i * size, size)], sems.at[i]
        )
        for i in range(copy_parts)
    ]


def query_places(ids, query_tokens):
    return [pl.ds(pl.multiple_of(n * query_tokens, query_tokens), query_tokens) for n in ids]


def forward_kernel(
    cand_count,
    query_count,
    query_tokens,
    recv_ref,
    norm_hbm,
    soft_hbm,
    qn_ref,
    score_ref,
    many_ref,
    target_ref,
    list_ref,
    zw_ref,
    norm_ref,
    soft_ref,
    ext_ref,
    low_ref,
    sums_ref,
    list_smem,
    sem,
    norm_sem,
    soft_sems,
):
    norm_copies = part_copies(norm_hbm, norm_ref, norm_sem)
    for copy in norm_copies:
        copy.start()
    sources = recv_ref.shape[0]
    pass_count, tokens, width = norm_ref.shape
    group = sources * query_count
    rows = query_count * query_tokens
    stride = group + row_pad
    empty, tables = list_layout(group)
    owner = lax.axis_index("psg").astype(jnp.float32)
    for s in range(sources):
        packed = recv_ref[s, rows : rows + 16, :].astype(jnp.float32)
        ext_ref[s * query_count : (s + 1) * query_count, :] = packed[:query_count]
        low_ref[s * query_count : (s + 1) * query_count, :] = packed[8 : 8 + query_count]
        qn_ref[s * rows : (s + 1) * rows, :] = unit_rows(recv_ref[s, :rows, :])[0].astype(
            jnp.bfloat16
        )
    qn_ref[sources * rows :, :] = jnp.zeros((query_tokens, width), jnp.bfloat16)

    main = ext_ref[...]
    lanes = lane_ids(main.shape)
    lanes_float = lanes.astype(jnp.float32)
    live = lanes < cand_count
    local = pltpu.roll(main, 128 - cand_count, 1)
    logits = (
        pltpu.roll(main, 128 - 2 * cand_count, 1)
        + pltpu.roll(main, 128 - 3 * cand_count, 1)
        + low_ref[...]
    )
    raised = jnp.where(live, jnp.exp(logits), 0.0)
    target = raised / jnp.sum(raised, -1, keepdims=True)
    local = jnp.where(main == owner, local, -1.0)
    many = jnp.zeros(main.shape, jnp.float32)
    wanted = jnp.zeros(main.shape, jnp.float32)
    for c in range(cand_count):
        same = local[:, c : c + 1] == lanes_float
        many = many + jnp.where(same, 1.0, 0.0)
        wanted = wanted + jnp.where(same, target[:, c : c + 1], 0.0)
    many_ref[...] = many
    target_ref[...] = wanted
    active = many > 0.0
    lower = (
        lax.broadcasted_iota(jnp.int32, (group, group), 0)
        > lax.broadcasted_iota(jnp.int32, (group, group), 1)
    ).astype(jnp.bfloat16)
    active_value = jnp.where(active, 1.0, 0.0)
    rank = jnp.dot(lower, active_value.astype(jnp.bfloat16), preferred_element_type=jnp.float32)
    rank = jnp.where(active, rank, -1.0)
    less = lax.broadcasted_iota(jnp.int32, main.shape, 0).astype(jnp.float32) - group
    for k in range(empty):
        found = jnp.sum(jnp.where(rank == k, less, 0.0), 0, keepdims=True) + group
        list_ref[k : k + 1, :] = found.astype(jnp.int32)
    list_ref[empty:tables, :] = jnp.full((tables - empty, 128), group, jnp.int32)
    square = (128, 128)
    first_id = lax.broadcasted_iota(jnp.int32, square, 0)
    second_id = lax.broadcasted_iota(jnp.int32, square, 1)
    counts = lax.dot_general(
        active_value, jnp.ones((group, 128), jnp.float32), (((0,), (0,)), ((), ())),
        preferred_element_type=jnp.float32,
    )
    chunks = jnp.floor((counts + (chunk_pairs - 1)) * (1.0 / chunk_pairs))
    ends = jnp.dot(
        (first_id >= second_id).astype(jnp.bfloat16),
        chunks.astype(jnp.bfloat16),
        preferred_element_type=jnp.float32,
    )
    past = ends <= second_id.astype(jnp.float32)
    passage_of = jnp.sum(jnp.where(past, 1.0, 0.0), 0, keepdims=True)
    start_of = jnp.sum(jnp.where(past, chunks, 0.0), 0, keepdims=True)
    chunk_id = lax.broadcasted_iota(jnp.int32, (1, 128), 1).astype(jnp.float32)
    beyond = passage_of > pass_count - 0.5
    passage_of = jnp.where(beyond, 0.0, passage_of)
    first_of = jnp.where(beyond, float(empty), (chunk_id - start_of) * chunk_pairs)
    flat = jnp.sum(active_value, 0, keepdims=True)
    starts = jnp.sum(jnp.where(first_id == second_id, ends - chunks, 0.0), 0, keepdims=True)
    total = jnp.sum(jnp.where(first_id == 127, ends, 0.0), 0, keepdims=True)
    for row, value in enumerate((passage_of, first_of, starts, flat, total)):
        list_ref[tables + row : tables + row + 1, :] = value.astype(jnp.int32)
    copy = pltpu.make_async_copy(list_ref, list_smem, sem)
    copy.start()
    for other in norm_copies:
        other.wait()
    copy.wait()

    def soft_copy(slot):
        return pltpu.make_async_copy(soft_ref.at[slot], soft_hbm.at[slot], soft_sems.at[slot])

    def chunk(slot):
        p = list_smem[tables, slot]
        first = list_smem[tables + 1, slot]
        ids = [list_smem[first + r, p] for r in range(chunk_pairs)]
        tile = jnp.concatenate([qn_ref[place, :] for place in query_places(ids, query_tokens)], 0)
        dots = lax.dot_general(
            norm_ref[p], tile, (((1,), (1,)), ((), ())), preferred_element_type=jnp.float32
        )
        power = jnp.exp2(dots * (math.log2(math.e) / softness_scale))
        sums = jnp.sum(power, 0, keepdims=True)
        soft_ref[slot] = (power * (1.0 / sums)).astype(jnp.bfloat16)
        for r, n in enumerate(ids):
            sums_ref[pl.ds(p * stride + n, 1), :query_tokens] = sums[
                :, r * query_tokens : (r + 1) * query_tokens
            ]

    def step(i, carry):
        for u in range(chunk_unroll):
            chunk(i * chunk_unroll + u)
        for u in range(chunk_unroll):
            soft_copy(i * chunk_unroll + u).start()
        return carry

    steps = steps_of(list_smem, tables)
    lax.fori_loop(0, steps, step, 0)

    scores = jnp.zeros(main.shape, jnp.float32)
    for p in range(pass_count):
        logs = jnp.log(sums_ref[p * stride : p * stride + group, :])
        value = softness_scale * jnp.sum(
            jnp.where(lanes < query_tokens, logs, 0.0), -1, keepdims=True
        )
        scores = jnp.where(lanes == p, value, scores)
    scores = jnp.where(active, scores, 0.0)
    score_ref[...] = scores
    mass = jnp.sum(many * jnp.exp(scores), -1, keepdims=True)
    agreed = jnp.sum(wanted * scores, -1, keepdims=True)
    message = jnp.where(lanes == 0, mass, jnp.where(lanes == 1, agreed, 0.0))
    for s in range(sources):
        zw_ref[s] = message

    def drain(slot, carry):
        soft_copy(slot).wait()
        return carry

    lax.fori_loop(0, steps * chunk_unroll, drain, 0)


def forward(received, norm, cand_count, query_count, query_tokens):
    sources = received.shape[0]
    pass_count, tokens, width = norm.shape
    group = sources * query_count
    capacity = max(2, -(-5 * query_count * cand_count // (2 * sources)))
    slots = slot_total(pass_count, sources * capacity)
    list_rows = list_layout(group)[1] + meta_rows
    rows = query_count * query_tokens
    soft_shape = (slots, tokens, chunk_pairs * query_tokens)
    flops = 2 * slots * chunk_pairs * query_tokens * tokens * width
    return pl.pallas_call(
        lambda *refs: forward_kernel(cand_count, query_count, query_tokens, *refs),
        in_specs=[VMEM, HBM],
        out_specs=[HBM] + [VMEM] * 6,
        out_shape=[
            pltpu.HBM(soft_shape, jnp.bfloat16),
            jax.ShapeDtypeStruct((sources * rows + query_tokens, width), jnp.bfloat16),
            jax.ShapeDtypeStruct((group, 128), jnp.float32),
            jax.ShapeDtypeStruct((group, 128), jnp.float32),
            jax.ShapeDtypeStruct((group, 128), jnp.float32),
            jax.ShapeDtypeStruct((list_rows, 128), jnp.int32),
            jax.ShapeDtypeStruct((sources, group, 128), jnp.float32),
        ],
        scratch_shapes=[
            pltpu.VMEM(norm.shape, jnp.bfloat16),
            pltpu.VMEM(soft_shape, jnp.bfloat16),
            pltpu.VMEM((group, 128), jnp.float32),
            pltpu.VMEM((group, 128), jnp.float32),
            pltpu.VMEM((pass_count * (group + row_pad), 128), jnp.float32),
            pltpu.SMEM((list_rows, 128), jnp.int32),
            pltpu.SemaphoreType.DMA,
            pltpu.SemaphoreType.DMA((copy_parts,)),
            pltpu.SemaphoreType.DMA((slots,)),
        ],
        compiler_params=params(),
        cost_estimate=pl.CostEstimate(flops=flops, bytes_accessed=12 << 20, transcendentals=1 << 22),
        name="forward",
    )(received, in_hbm(norm))


def spread(ref, values, pass_count, stride, start=0):
    group = values.shape[0]
    for p in range(pass_count):
        ref[p * stride : p * stride + group, :] = jnp.broadcast_to(
            values[:, start + p : start + p + 1], (group, 128)
        )
        ref[p * stride + group : (p + 1) * stride, :] = jnp.zeros((stride - group, 128), jnp.float32)


def attend_kernel(
    query_tokens,
    flip_hbm,
    soft_hbm,
    list_ref,
    score_ref,
    many_ref,
    target_ref,
    raised_ref,
    wanted_ref,
    flip_ref,
    soft_ref,
    raised_rows,
    wanted_rows,
    raised_sum,
    wanted_sum,
    list_smem,
    sem,
    flip_sem,
    soft_sems,
):
    pass_count = flip_ref.shape[0]
    group = score_ref.shape[0]
    stride = group + row_pad
    list_copy = pltpu.make_async_copy(list_ref, list_smem, sem)
    list_copy.start()
    flip_copies = part_copies(flip_hbm, flip_ref, flip_sem)
    empty, tables = list_layout(group)

    def soft_copy(slot):
        return pltpu.make_async_copy(soft_hbm.at[slot], soft_ref.at[slot], soft_sems.at[slot])

    def fetch(slot, carry):
        soft_copy(slot).start()
        return carry

    list_copy.wait()
    steps = steps_of(list_smem, tables)
    lax.fori_loop(0, chunk_unroll, fetch, 0)
    for copy in flip_copies:
        copy.start()
    lax.fori_loop(chunk_unroll, steps * chunk_unroll, fetch, 0)
    spread(raised_rows, many_ref[...] * jnp.exp(score_ref[...]), pass_count, stride)
    spread(wanted_rows, target_ref[...], pass_count, stride)
    raised_sum[...] = jnp.zeros(raised_sum.shape, jnp.float32)
    wanted_sum[...] = jnp.zeros(wanted_sum.shape, jnp.float32)
    for copy in flip_copies:
        copy.wait()

    def chunk(slot):
        p = list_smem[tables, slot]
        first = list_smem[tables + 1, slot]
        ids = [list_smem[first + r, p] for r in range(chunk_pairs)]
        places = query_places(ids, query_tokens)
        mixed = jnp.dot(flip_ref[p], soft_ref[slot], preferred_element_type=jnp.float32)
        mixed = jnp.transpose(mixed, (1, 0))
        for total, rows in ((raised_sum, raised_rows), (wanted_sum, wanted_rows)):
            added = [
                total[place, :]
                + mixed[r * query_tokens : (r + 1) * query_tokens]
                * rows[pl.ds(p * stride + ids[r], 1), :]
                for r, place in enumerate(places)
            ]
            for place, value in zip(places, added):
                total[place, :] = value

    def step(i, carry):
        for u in range(chunk_unroll):
            soft_copy(i * chunk_unroll + u).wait()
        for u in range(chunk_unroll):
            chunk(i * chunk_unroll + u)
        return carry

    lax.fori_loop(0, steps, step, 0)
    raised_ref[...] = raised_sum[: group * query_tokens, :]
    wanted_ref[...] = wanted_sum[: group * query_tokens, :]


def attend(flip, soft, ids, score, many, target, query_tokens):
    slots, tokens, columns = soft.shape
    pass_count, width, _ = flip.shape
    group = score.shape[0]
    flops = 2 * slots * columns * tokens * width
    total = jax.ShapeDtypeStruct((group * query_tokens, width), jnp.float32)
    rows = pltpu.VMEM((pass_count * (group + row_pad), 128), jnp.float32)
    padded = pltpu.VMEM(((group + 1) * query_tokens, width), jnp.float32)
    return pl.pallas_call(
        lambda *refs: attend_kernel(query_tokens, *refs),
        in_specs=[HBM, HBM] + [VMEM] * 4,
        out_specs=[VMEM] * 2,
        out_shape=[total, total],
        scratch_shapes=[
            pltpu.VMEM(flip.shape, jnp.bfloat16),
            pltpu.VMEM(soft.shape, jnp.bfloat16),
            rows,
            rows,
            padded,
            padded,
            pltpu.SMEM(ids.shape, jnp.int32),
            pltpu.SemaphoreType.DMA,
            pltpu.SemaphoreType.DMA((copy_parts,)),
            pltpu.SemaphoreType.DMA((slots,)),
        ],
        compiler_params=params(),
        cost_estimate=pl.CostEstimate(flops=flops, bytes_accessed=12 << 20, transcendentals=0),
        name="attend",
    )(in_hbm(flip), in_hbm(soft), ids, score, many, target)


def halving_order(count):
    order = [0]
    bit = count // 2
    while bit:
        order = order + [x | bit for x in order]
        bit //= 2
    return order


def query_kernel(
    query_tokens,
    zw_ref,
    score_ref,
    many_ref,
    target_ref,
    raised_ref,
    wanted_ref,
    keep_ref,
    send_ref,
    grads_ref,
    scale_ref,
    query_ref,
):
    sources, group, _ = zw_ref.shape
    sums = zw_ref[0]
    for s in range(1, sources):
        sums = sums + zw_ref[s]
    inverse = 1.0 / sums[:, :1]
    grads_ref[...] = many_ref[...] * jnp.exp(score_ref[...]) * inverse - target_ref[...]
    scale_ref[...] = jnp.broadcast_to(inverse, scale_ref.shape)
    for n in range(group):
        place = pl.ds(n * query_tokens, query_tokens)
        query_ref[place, :] = (
            raised_ref[place, :] * scale_ref[n : n + 1, :] - wanted_ref[place, :]
        ).astype(jnp.bfloat16)
    me = lax.axis_index("psg")
    rows = group // sources * query_tokens
    half = keep_ref.shape[0]
    for place, d in enumerate(halving_order(sources)):
        start = pl.multiple_of((me ^ d) * rows, rows)
        value = query_ref[pl.ds(start, rows), :]
        if place < half:
            keep_ref[place] = value
        else:
            send_ref[place - half] = value


def query_backward(zw, score, many, target, raised, wanted):
    sources, group, _ = zw.shape
    rows, width = raised.shape
    part = jax.ShapeDtypeStruct((sources // 2, rows // sources, width), jnp.bfloat16)
    return pl.pallas_call(
        lambda *refs: query_kernel(rows // group, *refs),
        in_specs=[VMEM] * 6,
        out_specs=[VMEM] * 3,
        out_shape=[part, part, jax.ShapeDtypeStruct((group, 128), jnp.float32)],
        scratch_shapes=[
            pltpu.VMEM((group, 128), jnp.float32),
            pltpu.VMEM((rows, width), jnp.bfloat16),
        ],
        compiler_params=params(),
        name="query_backward",
    )(zw, score, many, target, raised, wanted)


def passage_kernel(
    query_tokens,
    start,
    list_ref,
    grads_ref,
    qn_ref,
    soft_hbm,
    own_ref,
    core_ref,
    far_ref,
    cross_ref,
    soft_ref,
    grad_ref,
    list_smem,
    sem,
    soft_sems,
):
    list_copy = pltpu.make_async_copy(list_ref, list_smem, sem)
    list_copy.start()
    pass_count, share, width = own_ref.shape
    group = grads_ref.shape[0]
    stride = group + row_pad
    empty, tables = list_layout(group)

    def soft_copy(slot):
        return pltpu.make_async_copy(soft_hbm.at[slot], soft_ref.at[slot], soft_sems.at[slot])

    def fetch(slot, carry):
        soft_copy(slot).start()
        return carry

    def drain(slot, carry):
        soft_copy(slot).wait()
        return carry

    list_copy.wait()
    low = list_smem[tables + 2, start]
    high = jnp.maximum(list_smem[tables + 2, start + pass_count], low + 1)
    lax.fori_loop(low, high, fetch, 0)
    spread(grad_ref, grads_ref[...], pass_count, stride, start)

    def tile(p, first):
        ids = [list_smem[first + r, start + p] for r in range(chunk_pairs)]
        return [
            (qn_ref[place, :].astype(jnp.float32) * grad_ref[pl.ds(p * stride + n, 1), :]).astype(
                jnp.bfloat16
            )
            for n, place in zip(ids, query_places(ids, query_tokens))
        ]

    outs = (own_ref, core_ref, far_ref, cross_ref)

    def passage(p):
        pairs = list_smem[tables + 3, start + p]
        slot = list_smem[tables + 2, start + p]
        tiles, softs = [], []
        for h in range(2):
            some = pairs > h * chunk_pairs
            tiles += tile(p, jnp.where(some, h * chunk_pairs, empty))
            softs.append(soft_ref[jnp.where(some, slot + h, low)])
        value = jnp.dot(
            jnp.concatenate(softs, 1),
            jnp.concatenate(tiles, 0),
            preferred_element_type=jnp.float32,
        ).astype(jnp.bfloat16)
        for place, ref in enumerate(outs):
            ref[p] = value[place * share : (place + 1) * share]

    def step(i, ready):
        last = (i + 1) * passage_unroll
        needed = jnp.maximum(list_smem[tables + 2, start + last], low + 1)
        lax.fori_loop(ready, needed, drain, 0)
        for u in range(passage_unroll):
            passage(i * passage_unroll + u)
        return needed

    lax.fori_loop(0, pass_count // passage_unroll, step, low)

    def rest(p, carry):
        chunks = (list_smem[tables + 3, start + p] + chunk_pairs - 1) // chunk_pairs
        slot = list_smem[tables + 2, start + p]

        def add(b, inner):
            value = jnp.dot(
                soft_ref[slot + b],
                jnp.concatenate(tile(p, b * chunk_pairs), 0),
                preferred_element_type=jnp.float32,
            )
            for place, ref in enumerate(outs):
                piece = value[place * share : (place + 1) * share]
                ref[p] = (ref[p].astype(jnp.float32) + piece).astype(jnp.bfloat16)
            return inner

        lax.fori_loop(2, chunks, add, 0)
        return carry

    lax.fori_loop(0, pass_count, rest, 0)


def passage_backward(ids, grads, qn, soft, start, pass_count, query_tokens, slices):
    slots, tokens, columns = soft.shape
    width = qn.shape[1]
    piece = jax.ShapeDtypeStruct((pass_count, tokens // slices, width), jnp.bfloat16)
    flops = 4 * pass_count * columns * tokens * width
    return pl.pallas_call(
        lambda *refs: passage_kernel(query_tokens, start, *refs),
        in_specs=[VMEM] * 3 + [HBM],
        out_specs=[VMEM] * 4,
        out_shape=[piece] * 4,
        scratch_shapes=[
            pltpu.VMEM(soft.shape, jnp.bfloat16),
            pltpu.VMEM((pass_count * (grads.shape[0] + row_pad), 128), jnp.float32),
            pltpu.SMEM(ids.shape, jnp.int32),
            pltpu.SemaphoreType.DMA,
            pltpu.SemaphoreType.DMA((slots,)),
        ],
        compiler_params=params(),
        cost_estimate=pl.CostEstimate(flops=flops, bytes_accessed=6 << 20, transcendentals=0),
        name="passage_backward",
    )(ids, grads, qn, in_hbm(soft))


def finish_kernel(raw_ref, *refs):
    out_ref = refs[-1]
    grad = refs[0][...].astype(jnp.float32)
    for ref in refs[1:-1]:
        grad = grad + ref[...].astype(jnp.float32)
    out_ref[...] = tangent(raw_ref[...], grad).astype(jnp.bfloat16)


def finish(raw, parts):
    return pl.pallas_call(
        finish_kernel,
        in_specs=[VMEM] * (1 + len(parts)),
        out_specs=VMEM,
        out_shape=jax.ShapeDtypeStruct(raw.shape, jnp.bfloat16),
        compiler_params=params(),
        name="finish",
    )(raw, *parts)


def finish_queries(raw, parts):
    return pl.pallas_call(
        finish_kernel,
        in_specs=[VMEM] * (1 + len(parts)),
        out_specs=VMEM,
        out_shape=jax.ShapeDtypeStruct(raw.shape, jnp.bfloat16),
        compiler_params=params(),
        name="finish_queries",
    )(raw, *parts)


def shards(queries, passages, candidates, teacher):
    query_count, query_tokens, width = queries.shape
    pass_count = passages.shape[0]
    cand_count = candidates.shape[1]
    sources = lax.axis_size("psg")
    slices = lax.axis_size("qry")
    rows = query_count * query_tokens

    received = lax.all_to_all(
        pack(queries.reshape(rows, width), candidates, teacher, sources, pass_count),
        "psg",
        split_axis=0,
        concat_axis=0,
        tiled=True,
    )
    norm, flip, own_raw = prepare_passages(passages, slices)
    soft, qn, score, many, target, ids, zw = forward(
        received, norm, cand_count, query_count, query_tokens
    )
    zw = lax.all_to_all(zw, "psg", split_axis=0, concat_axis=0, tiled=True)
    raised_sum, wanted_sum = attend(flip, soft, ids, score, many, target, query_tokens)
    keep, send, grads = query_backward(zw, score, many, target, raised_sum, wanted_sum)
    near = [(k, k ^ 1) for k in range(slices)]
    away = [(k, k ^ 2) for k in range(slices)]
    own, core, far, cross = passage_backward(
        ids, grads, qn, soft, 0, pass_count, query_tokens, slices
    )
    cross = lax.ppermute(cross, "qry", near)
    far = (far.astype(jnp.float32) + cross.astype(jnp.float32)).astype(jnp.bfloat16)
    far, send = lax.optimization_barrier((far, send))
    far = lax.ppermute(far, "qry", away)
    core = lax.ppermute(core, "qry", near)
    bit = 1
    while bit < sources:
        swap = [(i, i ^ bit) for i in range(sources)]
        send = lax.ppermute(send, "psg", swap)
        if bit * 2 < sources:
            total = keep.astype(jnp.float32) + send.astype(jnp.float32)
            half = total.shape[0] // 2
            keep, send = total[:half], total[half:].astype(jnp.bfloat16)
        bit *= 2
    grad_queries = finish_queries(queries.reshape(rows, width), [keep[0], send[0]])

    grad_passages = finish(own_raw, [own, core, far])

    raised = jnp.exp(teacher)
    raised_sum = jnp.sum(raised, -1, keepdims=True)
    log_target = teacher - jnp.log(raised_sum)
    known = jnp.sum(raised / raised_sum * log_target, -1)
    mine = lax.dynamic_slice_in_dim(
        zw[:, :, :2], lax.axis_index("psg") * query_count, query_count, 1
    )
    mine = jnp.sum(mine, 0)
    pair_loss = known - mine[:, 1] + jnp.log(mine[:, 0])
    return (pair_loss, grad_queries.reshape(queries.shape), grad_passages)


def solution(mesh):
    placed = (
        P(("psg", "qry"), None, None),
        P("psg", None, None),
        P(("psg", "qry"), None),
        P(("psg", "qry"), None),
    )
    return jax.shard_map(
        shards,
        mesh=mesh,
        in_specs=placed,
        out_specs=(P(("psg", "qry")), P(("psg", "qry"), None, None), P("psg", "qry", None)),
        check_vma=False,
    )
```

```python
import math

import jax
import jax.numpy as jnp
from jax import lax
from jax.experimental import pallas as pl
from jax.experimental.pallas import tpu as pltpu
from jax.sharding import PartitionSpec as P

epsilon = 1e-06
softness_scale = 0.05
chunk_pairs = 8
vmem_bytes = 44 << 20
row_pad = 8

VMEM = pl.BlockSpec(memory_space=pltpu.VMEM)
HBM = pl.BlockSpec(memory_space=pltpu.HBM)
chunk_unroll = 8
chunk_tail = 4
passage_unroll = 8
early_slots = 24
copy_parts = 8
meta_rows = 8


def in_hbm(array):
    return pltpu.with_memory_space_constraint(array, pltpu.HBM)


def params():
    return pltpu.CompilerParams(vmem_limit_bytes=vmem_bytes)


def unit_rows(values):
    widened = values.astype(jnp.float32)
    inverse = lax.rsqrt(jnp.sum(widened * widened, -1, keepdims=True) + epsilon)
    return widened * inverse, inverse


def round_bf16(values):
    return values.astype(jnp.bfloat16).astype(jnp.float32)


def pack_kernel(pass_count, *refs):
    sources, targets, out_ref, sems = refs[:3], refs[4:7], refs[3], refs[7]
    copies = [
        pltpu.make_async_copy(source, target, sems.at[i])
        for i, (source, target) in enumerate(zip(sources, targets))
    ]
    for copy in copies:
        copy.start()
    for copy in copies:
        copy.wait()
    queries_ref, candidates_ref, teacher_ref = targets
    query_count, cand_count = teacher_ref.shape
    ids = candidates_ref[...].astype(jnp.float32)
    owner = jnp.floor((ids + 0.5) * (1.0 / pass_count))
    values = teacher_ref[...]
    high = round_bf16(values)
    middle = round_bf16(values - high)
    low = values - high - middle
    main = jnp.concatenate([owner, ids - owner * pass_count, high, middle], 1)
    blank = jnp.zeros((8 - query_count, 128), jnp.float32)
    low = jnp.concatenate([low, jnp.zeros((query_count, 128 - cand_count), jnp.float32)], 1)
    extra = jnp.concatenate([main, blank, low, blank], 0).astype(jnp.bfloat16)
    rows = queries_ref.shape[0]
    for d in range(out_ref.shape[0]):
        out_ref[d, :rows, :] = queries_ref[...]
        out_ref[d, rows:, :] = extra


def pack(queries, candidates, teacher, sources, pass_count):
    rows, width = queries.shape
    return pl.pallas_call(
        lambda *refs: pack_kernel(pass_count, *refs),
        in_specs=[HBM] * 3,
        out_specs=VMEM,
        out_shape=jax.ShapeDtypeStruct((sources, rows + 16, width), jnp.bfloat16),
        scratch_shapes=[
            pltpu.VMEM(queries.shape, queries.dtype),
            pltpu.VMEM(candidates.shape, candidates.dtype),
            pltpu.VMEM(teacher.shape, teacher.dtype),
            pltpu.SemaphoreType.DMA((3,)),
        ],
        compiler_params=params(),
        name="pack",
    )(in_hbm(queries), in_hbm(candidates), in_hbm(teacher))


def lane_ids(shape):
    return lax.broadcasted_iota(jnp.int32, shape, len(shape) - 1)


def tangent(raw, grad):
    unit, inverse = unit_rows(raw)
    return inverse * (grad - unit * jnp.sum(unit * grad, -1, keepdims=True))


def passages_kernel(slices, in_ref, norm_ref, flip_ref, own_ref):
    count, tokens, _ = in_ref.shape
    share = tokens // slices
    me = lax.axis_index("qry")
    for item in range(count):
        for place in range(slices):
            start = pl.multiple_of((me ^ place) * share, share)
            raw = in_ref[item, pl.ds(start, share), :]
            if place == 0:
                own_ref[item] = raw
            norm_ref[item, pl.ds(place * share, share), :] = unit_rows(raw)[0].astype(
                jnp.bfloat16
            )
        flip_ref[item] = jnp.transpose(norm_ref[item], (1, 0))


def prepare_passages(passages, slices):
    count, tokens, width = passages.shape
    step = math.gcd(count, 8)
    share = tokens // slices
    return pl.pallas_call(
        lambda *refs: passages_kernel(slices, *refs),
        grid=(count // step,),
        in_specs=[pl.BlockSpec((step, tokens, width), lambda i: (i, 0, 0))],
        out_specs=[
            pl.BlockSpec((step, tokens, width), lambda i: (i, 0, 0)),
            pl.BlockSpec((step, width, tokens), lambda i: (i, 0, 0)),
            pl.BlockSpec((step, share, width), lambda i: (i, 0, 0)),
        ],
        out_shape=[
            pltpu.HBM((count, tokens, width), jnp.bfloat16),
            pltpu.HBM((count, width, tokens), jnp.bfloat16),
            pltpu.HBM((count, share, width), jnp.bfloat16),
        ],
        compiler_params=params(),
        cost_estimate=pl.CostEstimate(flops=1 << 24, bytes_accessed=6 << 20, transcendentals=0),
        name="prepare_passages",
    )(in_hbm(passages))


def list_layout(group):
    empty = -(-group // chunk_pairs) * chunk_pairs // 4
    return empty, empty + chunk_pairs // 4


def slot_total(pass_count, pairs):
    worst = (pairs + pass_count * (chunk_pairs - 1)) // chunk_pairs
    return -(-max(worst, early_slots) // chunk_unroll) * chunk_unroll


def list_ids(list_smem, row, p):
    words = [list_smem[row + w, p] for w in range(chunk_pairs // 4)]
    return [(words[r // 4] >> (8 * (r % 4))) & 255 for r in range(chunk_pairs)]


def each_chunk(list_smem, tables, visit):
    total = jnp.maximum(list_smem[tables + 4, 0], 1)
    full = total // chunk_unroll
    tail = (total - full * chunk_unroll + chunk_tail - 1) // chunk_tail

    def step(i, carry):
        visit(i * chunk_unroll, chunk_unroll)
        return carry

    def tail_step(i, carry):
        visit(full * chunk_unroll + i * chunk_tail, chunk_tail)
        return carry

    lax.fori_loop(0, full, step, 0)
    lax.fori_loop(0, tail, tail_step, 0)
    return full * chunk_unroll + tail * chunk_tail


def slots_used(list_smem, tables):
    total = jnp.maximum(list_smem[tables + 4, 0], 1)
    return (total + chunk_tail - 1) // chunk_tail * chunk_tail


def part_copies(source, target, sems):
    size = source.shape[0] // copy_parts
    return [
        pltpu.make_async_copy(
            source.at[pl.ds(i * size, size)], target.at[pl.ds(i * size, size)], sems.at[i]
        )
        for i in range(copy_parts)
    ]


def query_places(ids, query_tokens):
    return [pl.ds(pl.multiple_of(n * query_tokens, query_tokens), query_tokens) for n in ids]


def forward_kernel(
    cand_count,
    query_count,
    query_tokens,
    recv_ref,
    norm_hbm,
    soft_hbm,
    qn_ref,
    score_ref,
    many_ref,
    target_ref,
    list_ref,
    zw_ref,
    inverse_ref,
    norm_ref,
    soft_ref,
    ext_ref,
    low_ref,
    sums_ref,
    list_smem,
    sem,
    norm_sem,
    soft_sems,
):
    norm_copies = part_copies(norm_hbm, norm_ref, norm_sem)
    for copy in norm_copies:
        copy.start()
    sources = recv_ref.shape[0]
    pass_count, tokens, width = norm_ref.shape
    group = sources * query_count
    rows = query_count * query_tokens
    stride = group + row_pad
    empty, tables = list_layout(group)
    owner = lax.axis_index("psg").astype(jnp.float32)
    for s in range(sources):
        packed = recv_ref[s, rows : rows + 16, :].astype(jnp.float32)
        ext_ref[s * query_count : (s + 1) * query_count, :] = packed[:query_count]
        low_ref[s * query_count : (s + 1) * query_count, :] = packed[8 : 8 + query_count]
        qn_ref[s * rows : (s + 1) * rows, :] = unit_rows(recv_ref[s, :rows, :])[0].astype(
            jnp.bfloat16
        )
    qn_ref[sources * rows :, :] = jnp.zeros((query_tokens, width), jnp.bfloat16)

    main = ext_ref[...]
    lanes = lane_ids(main.shape)
    lanes_float = lanes.astype(jnp.float32)
    live = lanes < cand_count
    local = pltpu.roll(main, 128 - cand_count, 1)
    logits = (
        pltpu.roll(main, 128 - 2 * cand_count, 1)
        + pltpu.roll(main, 128 - 3 * cand_count, 1)
        + low_ref[...]
    )
    raised = jnp.where(live, jnp.exp(logits), 0.0)
    target = raised / jnp.sum(raised, -1, keepdims=True)
    local = jnp.where(main == owner, local, -1.0)
    many = jnp.zeros(main.shape, jnp.float32)
    wanted = jnp.zeros(main.shape, jnp.float32)
    for c in range(cand_count):
        same = local[:, c : c + 1] == lanes_float
        many = many + jnp.where(same, 1.0, 0.0)
        wanted = wanted + jnp.where(same, target[:, c : c + 1], 0.0)
    many_ref[...] = many
    target_ref[...] = wanted
    active = many > 0.0
    lower = (
        lax.broadcasted_iota(jnp.int32, (group, group), 0)
        > lax.broadcasted_iota(jnp.int32, (group, group), 1)
    ).astype(jnp.bfloat16)
    active_value = jnp.where(active, 1.0, 0.0)
    rank = jnp.dot(lower, active_value.astype(jnp.bfloat16), preferred_element_type=jnp.float32)
    rank = jnp.where(active, rank, -1.0)
    less = lax.broadcasted_iota(jnp.int32, main.shape, 0).astype(jnp.float32) - group
    for w in range(empty):
        word = jnp.zeros((1, 128), jnp.int32)
        for b in range(4):
            found = jnp.sum(jnp.where(rank == 4 * w + b, less, 0.0), 0, keepdims=True) + group
            word = word | (found.astype(jnp.int32) << (8 * b))
        list_ref[w : w + 1, :] = word
    blank = jnp.full((tables - empty, 128), group, jnp.int32)
    list_ref[empty:tables, :] = blank | (blank << 8) | (blank << 16) | (blank << 24)
    square = (128, 128)
    first_id = lax.broadcasted_iota(jnp.int32, square, 0)
    second_id = lax.broadcasted_iota(jnp.int32, square, 1)
    counts = lax.dot_general(
        active_value.astype(jnp.bfloat16),
        jnp.ones((group, 128), jnp.bfloat16),
        (((0,), (0,)), ((), ())),
        preferred_element_type=jnp.float32,
    )
    chunks = jnp.floor((counts + (chunk_pairs - 1)) * (1.0 / chunk_pairs))
    more = jnp.maximum(chunks - 2.0, 0.0)
    lower_square = (first_id >= second_id).astype(jnp.bfloat16)
    ends = jnp.dot(lower_square, chunks.astype(jnp.bfloat16), preferred_element_type=jnp.float32)
    more_ends = jnp.dot(lower_square, more.astype(jnp.bfloat16), preferred_element_type=jnp.float32)
    chunk_id = lax.broadcasted_iota(jnp.int32, (1, 128), 1).astype(jnp.float32)

    def places_of(chunk_ends, chunk_counts):
        past = chunk_ends <= second_id.astype(jnp.float32)
        passage_of = jnp.sum(jnp.where(past, 1.0, 0.0), 0, keepdims=True)
        start_of = jnp.sum(jnp.where(past, chunk_counts, 0.0), 0, keepdims=True)
        return passage_of, chunk_id - start_of

    def last_row(values):
        return jnp.sum(jnp.where(first_id == 127, values, 0.0), 0, keepdims=True)

    passage_of, chunk_of = places_of(ends, chunks)
    more_passage, more_chunk = places_of(more_ends, more)
    beyond = passage_of > pass_count - 0.5
    rows_of = (
        jnp.where(beyond, 0.0, passage_of),
        jnp.where(beyond, float(empty), chunk_of * (chunk_pairs // 4)),
        jnp.sum(jnp.where(first_id == second_id, ends - chunks, 0.0), 0, keepdims=True),
        jnp.sum(active_value, 0, keepdims=True),
        last_row(ends),
        more_passage,
        more_chunk + 2.0,
        last_row(more_ends),
    )
    for row, value in enumerate(rows_of):
        list_ref[tables + row : tables + row + 1, :] = value.astype(jnp.int32)
    copy = pltpu.make_async_copy(list_ref, list_smem, sem)
    copy.start()
    for other in norm_copies:
        other.wait()
    copy.wait()

    def soft_copy(slot):
        return pltpu.make_async_copy(soft_ref.at[slot], soft_hbm.at[slot], soft_sems.at[slot])

    def chunk(slot):
        p = list_smem[tables, slot]
        ids = list_ids(list_smem, list_smem[tables + 1, slot], p)
        tile = jnp.concatenate([qn_ref[place, :] for place in query_places(ids, query_tokens)], 0)
        dots = lax.dot_general(
            norm_ref[p], tile, (((1,), (1,)), ((), ())), preferred_element_type=jnp.float32
        )
        power = jnp.exp2(dots * (math.log2(math.e) / softness_scale))
        sums = jnp.sum(power, 0, keepdims=True)
        soft_ref[slot] = power.astype(jnp.bfloat16)
        inverse_ref[pl.ds(slot, 1), :] = 1.0 / sums
        for r, n in enumerate(ids):
            sums_ref[pl.ds(p * stride + n, 1), :query_tokens] = sums[
                :, r * query_tokens : (r + 1) * query_tokens
            ]

    def visit(first, count):
        for u in range(count):
            chunk(first + u)
        for u in range(count):
            soft_copy(first + u).start()

    used = each_chunk(list_smem, tables, visit)

    scores = jnp.zeros(main.shape, jnp.float32)
    for p in range(pass_count):
        logs = jnp.log(sums_ref[p * stride : p * stride + group, :])
        value = softness_scale * jnp.sum(
            jnp.where(lanes < query_tokens, logs, 0.0), -1, keepdims=True
        )
        scores = jnp.where(lanes == p, value, scores)
    scores = jnp.where(active, scores, 0.0)
    score_ref[...] = scores
    mass = jnp.sum(many * jnp.exp(scores), -1, keepdims=True)
    agreed = jnp.sum(wanted * scores, -1, keepdims=True)
    message = jnp.where(lanes == 0, mass, jnp.where(lanes == 1, agreed, 0.0))
    for s in range(sources):
        zw_ref[s] = message

    def drain(slot, carry):
        soft_copy(slot).wait()
        return carry

    lax.fori_loop(0, used, drain, 0)


def forward(received, norm, cand_count, query_count, query_tokens):
    sources = received.shape[0]
    pass_count, tokens, width = norm.shape
    group = sources * query_count
    capacity = max(2, -(-5 * query_count * cand_count // (2 * sources)))
    slots = slot_total(pass_count, sources * capacity)
    list_rows = -(-(list_layout(group)[1] + meta_rows) // 8) * 8
    rows = query_count * query_tokens
    soft_shape = (slots, tokens, chunk_pairs * query_tokens)
    flops = 2 * slots * chunk_pairs * query_tokens * tokens * width
    return pl.pallas_call(
        lambda *refs: forward_kernel(cand_count, query_count, query_tokens, *refs),
        in_specs=[VMEM, HBM],
        out_specs=[HBM] + [VMEM] * 7,
        out_shape=[
            pltpu.HBM(soft_shape, jnp.bfloat16),
            jax.ShapeDtypeStruct((sources * rows + query_tokens, width), jnp.bfloat16),
            jax.ShapeDtypeStruct((group, 128), jnp.float32),
            jax.ShapeDtypeStruct((group, 128), jnp.float32),
            jax.ShapeDtypeStruct((group, 128), jnp.float32),
            jax.ShapeDtypeStruct((list_rows, 128), jnp.int32),
            jax.ShapeDtypeStruct((sources, group, 128), jnp.float32),
            jax.ShapeDtypeStruct((slots, chunk_pairs * query_tokens), jnp.float32),
        ],
        scratch_shapes=[
            pltpu.VMEM(norm.shape, jnp.bfloat16),
            pltpu.VMEM(soft_shape, jnp.bfloat16),
            pltpu.VMEM((group, 128), jnp.float32),
            pltpu.VMEM((group, 128), jnp.float32),
            pltpu.VMEM((pass_count * (group + row_pad), 128), jnp.float32),
            pltpu.SMEM((list_rows, 128), jnp.int32),
            pltpu.SemaphoreType.DMA,
            pltpu.SemaphoreType.DMA((copy_parts,)),
            pltpu.SemaphoreType.DMA((slots,)),
        ],
        compiler_params=params(),
        cost_estimate=pl.CostEstimate(flops=flops, bytes_accessed=12 << 20, transcendentals=1 << 22),
        name="forward",
    )(received, in_hbm(norm))


def spread(ref, values, pass_count, stride, start=0):
    group = values.shape[0]
    for p in range(pass_count):
        ref[p * stride : p * stride + group, :] = jnp.broadcast_to(
            values[:, start + p : start + p + 1], (group, 128)
        )
        ref[p * stride + group : (p + 1) * stride, :] = jnp.zeros((stride - group, 128), jnp.float32)


def attend_kernel(
    query_tokens,
    flip_hbm,
    soft_hbm,
    list_ref,
    score_ref,
    many_ref,
    target_ref,
    inverse_ref,
    raised_ref,
    wanted_ref,
    flip_ref,
    soft_ref,
    raised_rows,
    wanted_rows,
    raised_sum,
    wanted_sum,
    list_smem,
    sem,
    flip_sem,
    soft_sems,
):
    pass_count = flip_ref.shape[0]
    group = score_ref.shape[0]
    stride = group + row_pad
    list_copy = pltpu.make_async_copy(list_ref, list_smem, sem)
    list_copy.start()
    flip_copies = part_copies(flip_hbm, flip_ref, flip_sem)
    empty, tables = list_layout(group)

    def soft_copy(slot):
        return pltpu.make_async_copy(soft_hbm.at[slot], soft_ref.at[slot], soft_sems.at[slot])

    def fetch(slot, carry):
        soft_copy(slot).start()
        return carry

    lax.fori_loop(0, chunk_unroll, fetch, 0)
    for copy in flip_copies:
        copy.start()
    lax.fori_loop(chunk_unroll, early_slots, fetch, 0)
    list_copy.wait()
    used = slots_used(list_smem, tables)
    lax.fori_loop(early_slots, used, fetch, 0)
    spread(raised_rows, many_ref[...] * jnp.exp(score_ref[...]), pass_count, stride)
    spread(wanted_rows, target_ref[...], pass_count, stride)
    raised_sum[...] = jnp.zeros(raised_sum.shape, jnp.float32)
    wanted_sum[...] = jnp.zeros(wanted_sum.shape, jnp.float32)
    for copy in flip_copies:
        copy.wait()

    def chunk(slot):
        p = list_smem[tables, slot]
        ids = list_ids(list_smem, list_smem[tables + 1, slot], p)
        places = query_places(ids, query_tokens)
        mixed = jnp.dot(flip_ref[p], soft_ref[slot], preferred_element_type=jnp.float32)
        mixed = jnp.transpose(mixed * inverse_ref[pl.ds(slot, 1), :], (1, 0))
        for total, rows in ((raised_sum, raised_rows), (wanted_sum, wanted_rows)):
            added = [
                total[place, :]
                + mixed[r * query_tokens : (r + 1) * query_tokens]
                * rows[pl.ds(p * stride + ids[r], 1), :]
                for r, place in enumerate(places)
            ]
            for place, value in zip(places, added):
                total[place, :] = value

    def visit(first, count):
        for u in range(count):
            soft_copy(first + u).wait()
        for u in range(count):
            chunk(first + u)

    each_chunk(list_smem, tables, visit)

    def drain(slot, carry):
        soft_copy(slot).wait()
        return carry

    lax.fori_loop(used, early_slots, drain, 0)
    raised_ref[...] = raised_sum[: group * query_tokens, :]
    wanted_ref[...] = wanted_sum[: group * query_tokens, :]


def attend(flip, soft, ids, score, many, target, inverse, query_tokens):
    slots, tokens, columns = soft.shape
    pass_count, width, _ = flip.shape
    group = score.shape[0]
    flops = 2 * slots * columns * tokens * width
    total = jax.ShapeDtypeStruct((group * query_tokens, width), jnp.float32)
    rows = pltpu.VMEM((pass_count * (group + row_pad), 128), jnp.float32)
    padded = pltpu.VMEM(((group + 1) * query_tokens, width), jnp.float32)
    return pl.pallas_call(
        lambda *refs: attend_kernel(query_tokens, *refs),
        in_specs=[HBM, HBM] + [VMEM] * 5,
        out_specs=[VMEM] * 2,
        out_shape=[total, total],
        scratch_shapes=[
            pltpu.VMEM(flip.shape, jnp.bfloat16),
            pltpu.VMEM(soft.shape, jnp.bfloat16),
            rows,
            rows,
            padded,
            padded,
            pltpu.SMEM(ids.shape, jnp.int32),
            pltpu.SemaphoreType.DMA,
            pltpu.SemaphoreType.DMA((copy_parts,)),
            pltpu.SemaphoreType.DMA((slots,)),
        ],
        compiler_params=params(),
        cost_estimate=pl.CostEstimate(flops=flops, bytes_accessed=12 << 20, transcendentals=0),
        name="attend",
    )(in_hbm(flip), in_hbm(soft), ids, score, many, target, inverse)


def halving_order(count):
    order = [0]
    bit = count // 2
    while bit:
        order = order + [x | bit for x in order]
        bit //= 2
    return order


def query_kernel(
    query_tokens,
    zw_ref,
    score_ref,
    many_ref,
    target_ref,
    raised_ref,
    wanted_ref,
    keep_ref,
    send_ref,
    grads_ref,
    scale_ref,
    query_ref,
):
    sources, group, _ = zw_ref.shape
    sums = zw_ref[0]
    for s in range(1, sources):
        sums = sums + zw_ref[s]
    inverse = 1.0 / sums[:, :1]
    grads_ref[...] = many_ref[...] * jnp.exp(score_ref[...]) * inverse - target_ref[...]
    scale_ref[...] = jnp.broadcast_to(inverse, scale_ref.shape)
    for n in range(group):
        place = pl.ds(n * query_tokens, query_tokens)
        query_ref[place, :] = (
            raised_ref[place, :] * scale_ref[n : n + 1, :] - wanted_ref[place, :]
        ).astype(jnp.bfloat16)
    me = lax.axis_index("psg")
    rows = group // sources * query_tokens
    half = keep_ref.shape[0]
    for place, d in enumerate(halving_order(sources)):
        start = pl.multiple_of((me ^ d) * rows, rows)
        value = query_ref[pl.ds(start, rows), :]
        if place < half:
            keep_ref[place] = value
        else:
            send_ref[place - half] = value


def query_backward(zw, score, many, target, raised, wanted):
    sources, group, _ = zw.shape
    rows, width = raised.shape
    part = jax.ShapeDtypeStruct((sources // 2, rows // sources, width), jnp.bfloat16)
    return pl.pallas_call(
        lambda *refs: query_kernel(rows // group, *refs),
        in_specs=[VMEM] * 6,
        out_specs=[VMEM] * 3,
        out_shape=[part, part, jax.ShapeDtypeStruct((group, 128), jnp.float32)],
        scratch_shapes=[
            pltpu.VMEM((group, 128), jnp.float32),
            pltpu.VMEM((rows, width), jnp.bfloat16),
        ],
        compiler_params=params(),
        name="query_backward",
    )(zw, score, many, target, raised, wanted)


def passage_kernel(
    query_tokens,
    list_ref,
    grads_ref,
    qn_ref,
    inverse_ref,
    soft_hbm,
    own_ref,
    core_ref,
    far_ref,
    cross_ref,
    soft_ref,
    grad_ref,
    list_smem,
    sem,
    soft_sems,
):
    list_copy = pltpu.make_async_copy(list_ref, list_smem, sem)
    list_copy.start()
    pass_count, share, width = own_ref.shape
    group = grads_ref.shape[0]
    stride = group + row_pad
    empty, tables = list_layout(group)

    def soft_copy(slot):
        return pltpu.make_async_copy(soft_hbm.at[slot], soft_ref.at[slot], soft_sems.at[slot])

    def fetch(slot, carry):
        soft_copy(slot).start()
        return carry

    def drain(slot, carry):
        soft_copy(slot).wait()
        return carry

    lax.fori_loop(0, early_slots, fetch, 0)
    spread(grad_ref, grads_ref[...], pass_count, stride)
    list_copy.wait()
    total = list_smem[tables + 4, 0]
    lax.fori_loop(early_slots, total, fetch, 0)

    def tile(p, row):
        ids = list_ids(list_smem, row, p)
        return [
            (qn_ref[place, :].astype(jnp.float32) * grad_ref[pl.ds(p * stride + n, 1), :]).astype(
                jnp.bfloat16
            )
            for n, place in zip(ids, query_places(ids, query_tokens))
        ]

    def weights(slot):
        value = soft_ref[slot]
        tokens, columns = value.shape
        scale = jnp.broadcast_to(inverse_ref[pl.ds(slot, 1), :], (16, columns)).astype(jnp.bfloat16)
        return (value.reshape(tokens // 16, 16, columns) * scale[None]).reshape(tokens, columns)

    outs = (own_ref, core_ref, far_ref, cross_ref)

    def passage(p):
        pairs = list_smem[tables + 3, p]
        slot = list_smem[tables + 2, p]
        tiles, softs = [], []
        for h in range(2):
            some = pairs > h * chunk_pairs
            tiles += tile(p, jnp.where(some, h * (chunk_pairs // 4), empty))
            softs.append(weights(jnp.where(some, slot + h, 0)))
        value = jnp.dot(
            jnp.concatenate(softs, 1),
            jnp.concatenate(tiles, 0),
            preferred_element_type=jnp.float32,
        ).astype(jnp.bfloat16)
        for place, ref in enumerate(outs):
            ref[p] = value[place * share : (place + 1) * share]

    def step(i, ready):
        needed = jnp.maximum(list_smem[tables + 2, (i + 1) * passage_unroll], 1)
        lax.fori_loop(ready, needed, drain, 0)
        for u in range(passage_unroll):
            passage(i * passage_unroll + u)
        return needed

    ready = lax.fori_loop(0, pass_count // passage_unroll, step, jnp.int32(0))
    lax.fori_loop(ready, early_slots, drain, 0)

    def rest(i, carry):
        p = list_smem[tables + 5, i]
        b = list_smem[tables + 6, i]
        value = jnp.dot(
            weights(list_smem[tables + 2, p] + b),
            jnp.concatenate(tile(p, b * (chunk_pairs // 4)), 0),
            preferred_element_type=jnp.float32,
        )
        for place, ref in enumerate(outs):
            piece = value[place * share : (place + 1) * share]
            ref[p] = (ref[p].astype(jnp.float32) + piece).astype(jnp.bfloat16)
        return carry

    lax.fori_loop(0, list_smem[tables + 7, 0], rest, 0)


def passage_backward(ids, grads, qn, inverse, soft, pass_count, query_tokens, slices):
    slots, tokens, columns = soft.shape
    width = qn.shape[1]
    piece = jax.ShapeDtypeStruct((pass_count, tokens // slices, width), jnp.bfloat16)
    flops = 4 * pass_count * columns * tokens * width
    return pl.pallas_call(
        lambda *refs: passage_kernel(query_tokens, *refs),
        in_specs=[VMEM] * 4 + [HBM],
        out_specs=[VMEM] * 4,
        out_shape=[piece] * 4,
        scratch_shapes=[
            pltpu.VMEM(soft.shape, jnp.bfloat16),
            pltpu.VMEM((pass_count * (grads.shape[0] + row_pad), 128), jnp.float32),
            pltpu.SMEM(ids.shape, jnp.int32),
            pltpu.SemaphoreType.DMA,
            pltpu.SemaphoreType.DMA((slots,)),
        ],
        compiler_params=params(),
        cost_estimate=pl.CostEstimate(flops=flops, bytes_accessed=6 << 20, transcendentals=0),
        name="passage_backward",
    )(ids, grads, qn, inverse, in_hbm(soft))


def finish_kernel(raw_ref, *refs):
    out_ref = refs[-1]
    grad = refs[0][...].astype(jnp.float32)
    for ref in refs[1:-1]:
        grad = grad + ref[...].astype(jnp.float32)
    out_ref[...] = tangent(raw_ref[...], grad).astype(jnp.bfloat16)


def finish(raw, parts):
    return pl.pallas_call(
        finish_kernel,
        in_specs=[VMEM] * (1 + len(parts)),
        out_specs=VMEM,
        out_shape=jax.ShapeDtypeStruct(raw.shape, jnp.bfloat16),
        compiler_params=params(),
        name="finish",
    )(raw, *parts)


def finish_queries(raw, parts):
    return pl.pallas_call(
        finish_kernel,
        in_specs=[VMEM] * (1 + len(parts)),
        out_specs=VMEM,
        out_shape=jax.ShapeDtypeStruct(raw.shape, jnp.bfloat16),
        compiler_params=params(),
        name="finish_queries",
    )(raw, *parts)


def shards(queries, passages, candidates, teacher):
    query_count, query_tokens, width = queries.shape
    pass_count = passages.shape[0]
    cand_count = candidates.shape[1]
    sources = lax.axis_size("psg")
    slices = lax.axis_size("qry")
    rows = query_count * query_tokens

    received = lax.all_to_all(
        pack(queries.reshape(rows, width), candidates, teacher, sources, pass_count),
        "psg",
        split_axis=0,
        concat_axis=0,
        tiled=True,
    )
    norm, flip, own_raw = prepare_passages(passages, slices)
    soft, qn, score, many, target, ids, zw, inverse = forward(
        received, norm, cand_count, query_count, query_tokens
    )
    zw = lax.all_to_all(zw, "psg", split_axis=0, concat_axis=0, tiled=True)
    raised_sum, wanted_sum = attend(
        flip, soft, ids, score, many, target, inverse, query_tokens
    )
    keep, send, grads = query_backward(zw, score, many, target, raised_sum, wanted_sum)
    near = [(k, k ^ 1) for k in range(slices)]
    away = [(k, k ^ 2) for k in range(slices)]
    own, core, far, cross = passage_backward(
        ids, grads, qn, inverse, soft, pass_count, query_tokens, slices
    )
    cross = lax.ppermute(cross, "qry", near)
    far = (far.astype(jnp.float32) + cross.astype(jnp.float32)).astype(jnp.bfloat16)
    far, send, core = lax.optimization_barrier((far, send, core))
    far = lax.ppermute(far, "qry", away)
    core = lax.ppermute(core, "qry", near)
    bit = 1
    while sources // bit > 4:
        send = lax.ppermute(send, "psg", [(i, i ^ bit) for i in range(sources)])
        send, zw = lax.optimization_barrier((send, zw))
        total = keep.astype(jnp.float32) + send.astype(jnp.float32)
        half = total.shape[0] // 2
        bit *= 2
        if sources // bit > 4:
            keep, send = total[:half], total[half:].astype(jnp.bfloat16)
    query_parts = [total[0]]
    for place, d in enumerate(halving_order(sources)[: total.shape[0]]):
        if place:
            piece = total[place].astype(jnp.bfloat16)
            query_parts.append(lax.ppermute(piece, "psg", [(i, i ^ d) for i in range(sources)]))
    grad_queries = finish_queries(queries.reshape(rows, width), query_parts)

    grad_passages = finish(own_raw, [own, core, far])

    raised = jnp.exp(teacher)
    raised_sum = jnp.sum(raised, -1, keepdims=True)
    log_target = teacher - jnp.log(raised_sum)
    known = jnp.sum(raised / raised_sum * log_target, -1)
    mine = lax.dynamic_slice_in_dim(
        zw[:, :, :2], lax.axis_index("psg") * query_count, query_count, 1
    )
    mine = jnp.sum(mine, 0)
    pair_loss = known - mine[:, 1] + jnp.log(mine[:, 0])
    return (pair_loss, grad_queries.reshape(queries.shape), grad_passages)


def solution(mesh):
    placed = (
        P(("psg", "qry"), None, None),
        P("psg", None, None),
        P(("psg", "qry"), None),
        P(("psg", "qry"), None),
    )
    return jax.shard_map(
        shards,
        mesh=mesh,
        in_specs=placed,
        out_specs=(P(("psg", "qry")), P(("psg", "qry"), None, None), P("psg", "qry", None)),
        check_vma=False,
    )
```

```python
import math

import jax
import jax.numpy as jnp
from jax import lax
from jax.experimental import pallas as pl
from jax.experimental.pallas import tpu as pltpu
from jax.sharding import PartitionSpec as P

epsilon = 1e-06
softness_scale = 0.05
chunk_pairs = 8
vmem_bytes = 44 << 20
row_pad = 8

VMEM = pl.BlockSpec(memory_space=pltpu.VMEM)
HBM = pl.BlockSpec(memory_space=pltpu.HBM)
chunk_unroll = 8
chunk_tail = 4
passage_unroll = 8
early_slots = 24
copy_parts = 8
meta_rows = 8


def in_hbm(array):
    return pltpu.with_memory_space_constraint(array, pltpu.HBM)


def params():
    return pltpu.CompilerParams(vmem_limit_bytes=vmem_bytes)


def unit_rows(values):
    widened = values.astype(jnp.float32)
    inverse = lax.rsqrt(jnp.sum(widened * widened, -1, keepdims=True) + epsilon)
    return widened * inverse, inverse


def round_bf16(values):
    return values.astype(jnp.bfloat16).astype(jnp.float32)


def pack_kernel(pass_count, *refs):
    sources, targets, out_ref, sems = refs[:3], refs[4:7], refs[3], refs[7]
    copies = [
        pltpu.make_async_copy(source, target, sems.at[i])
        for i, (source, target) in enumerate(zip(sources, targets))
    ]
    for copy in copies:
        copy.start()
    for copy in copies:
        copy.wait()
    queries_ref, candidates_ref, teacher_ref = targets
    query_count, cand_count = teacher_ref.shape
    ids = candidates_ref[...].astype(jnp.float32)
    owner = jnp.floor((ids + 0.5) * (1.0 / pass_count))
    values = teacher_ref[...]
    high = round_bf16(values)
    middle = round_bf16(values - high)
    low = values - high - middle
    main = jnp.concatenate([owner, ids - owner * pass_count, high, middle], 1)
    blank = jnp.zeros((8 - query_count, 128), jnp.float32)
    low = jnp.concatenate([low, jnp.zeros((query_count, 128 - cand_count), jnp.float32)], 1)
    extra = jnp.concatenate([main, blank, low, blank], 0).astype(jnp.bfloat16)
    rows = queries_ref.shape[0]
    out_ref[:rows, :] = queries_ref[...]
    out_ref[rows:, :] = extra


def pack(queries, candidates, teacher, pass_count):
    rows, width = queries.shape
    return pl.pallas_call(
        lambda *refs: pack_kernel(pass_count, *refs),
        in_specs=[HBM] * 3,
        out_specs=VMEM,
        out_shape=jax.ShapeDtypeStruct((rows + 16, width), jnp.bfloat16),
        scratch_shapes=[
            pltpu.VMEM(queries.shape, queries.dtype),
            pltpu.VMEM(candidates.shape, candidates.dtype),
            pltpu.VMEM(teacher.shape, teacher.dtype),
            pltpu.SemaphoreType.DMA((3,)),
        ],
        compiler_params=params(),
        name="pack",
    )(in_hbm(queries), in_hbm(candidates), in_hbm(teacher))


def lane_ids(shape):
    return lax.broadcasted_iota(jnp.int32, shape, len(shape) - 1)


def tangent(raw, grad):
    unit, inverse = unit_rows(raw)
    return inverse * (grad - unit * jnp.sum(unit * grad, -1, keepdims=True))


def passages_kernel(
    slices, in_hbm_ref, norm_ref, flip_hbm, own_ref, in_ref, flip_ref, in_sems, flip_sems
):
    total, tokens, _ = norm_ref.shape
    parts = in_sems.shape[0]
    count = total // parts
    share = tokens // slices
    me = lax.axis_index("qry")

    def in_copy(part):
        place = pl.ds(part * count, count)
        return pltpu.make_async_copy(in_hbm_ref.at[place], in_ref.at[place], in_sems.at[part])

    def flip_copy(part):
        place = pl.ds(part * count, count)
        return pltpu.make_async_copy(flip_ref.at[place], flip_hbm.at[place], flip_sems.at[part])

    for part in range(parts):
        in_copy(part).start()
    for part in range(parts):
        in_copy(part).wait()
        for item in range(part * count, (part + 1) * count):
            for place in range(slices):
                start = pl.multiple_of((me ^ place) * share, share)
                raw = in_ref[item, pl.ds(start, share), :]
                if place == 0:
                    own_ref[item] = raw
                norm_ref[item, pl.ds(place * share, share), :] = unit_rows(raw)[0].astype(
                    jnp.bfloat16
                )
            flip_ref[item] = jnp.transpose(norm_ref[item], (1, 0))
        flip_copy(part).start()
    for part in range(parts):
        flip_copy(part).wait()


def prepare_passages(passages, slices):
    count, tokens, width = passages.shape
    parts = math.gcd(count, 4)
    share = tokens // slices
    return pl.pallas_call(
        lambda *refs: passages_kernel(slices, *refs),
        in_specs=[HBM],
        out_specs=[VMEM, HBM, VMEM],
        out_shape=[
            jax.ShapeDtypeStruct((count, tokens, width), jnp.bfloat16),
            pltpu.HBM((count, width, tokens), jnp.bfloat16),
            jax.ShapeDtypeStruct((count, share, width), jnp.bfloat16),
        ],
        scratch_shapes=[
            pltpu.VMEM((count, tokens, width), jnp.bfloat16),
            pltpu.VMEM((count, width, tokens), jnp.bfloat16),
            pltpu.SemaphoreType.DMA((parts,)),
            pltpu.SemaphoreType.DMA((parts,)),
        ],
        compiler_params=params(),
        cost_estimate=pl.CostEstimate(flops=1 << 24, bytes_accessed=6 << 20, transcendentals=0),
        name="prepare_passages",
    )(in_hbm(passages))


def list_layout(group):
    empty = -(-group // chunk_pairs) * chunk_pairs // 4
    return empty, empty + chunk_pairs // 4


def slot_total(pass_count, pairs):
    worst = (pairs + pass_count * (chunk_pairs - 1)) // chunk_pairs
    return -(-max(worst, early_slots) // chunk_unroll) * chunk_unroll


def list_ids(list_smem, row, p):
    words = [list_smem[row + w, p] for w in range(chunk_pairs // 4)]
    return [(words[r // 4] >> (8 * (r % 4))) & 255 for r in range(chunk_pairs)]


def each_chunk(list_smem, tables, visit):
    total = jnp.maximum(list_smem[tables + 4, 0], 1)
    full = total // chunk_unroll
    tail = (total - full * chunk_unroll + chunk_tail - 1) // chunk_tail

    def step(i, carry):
        visit(i * chunk_unroll, chunk_unroll)
        return carry

    def tail_step(i, carry):
        visit(full * chunk_unroll + i * chunk_tail, chunk_tail)
        return carry

    lax.fori_loop(0, full, step, 0)
    lax.fori_loop(0, tail, tail_step, 0)
    return full * chunk_unroll + tail * chunk_tail


def slots_used(list_smem, tables):
    total = jnp.maximum(list_smem[tables + 4, 0], 1)
    return (total + chunk_tail - 1) // chunk_tail * chunk_tail


def part_copies(source, target, sems):
    size = source.shape[0] // copy_parts
    return [
        pltpu.make_async_copy(
            source.at[pl.ds(i * size, size)], target.at[pl.ds(i * size, size)], sems.at[i]
        )
        for i in range(copy_parts)
    ]


def query_places(ids, query_tokens):
    return [pl.ds(pl.multiple_of(n * query_tokens, query_tokens), query_tokens) for n in ids]


def forward_kernel(
    cand_count,
    query_count,
    query_tokens,
    recv_refs,
    norm_ref,
    soft_hbm,
    qn_ref,
    score_ref,
    many_ref,
    target_ref,
    list_ref,
    zw_ref,
    inverse_ref,
    soft_ref,
    ext_ref,
    low_ref,
    sums_ref,
    list_smem,
    sem,
    soft_sems,
):
    near = recv_refs[0].shape[0]
    sources = near * len(recv_refs)
    pass_count, tokens, width = norm_ref.shape
    group = sources * query_count
    rows = query_count * query_tokens
    stride = group + row_pad
    empty, tables = list_layout(group)
    me = lax.axis_index("psg")
    owner = me.astype(jnp.float32)
    for d in range(sources):
        recv_ref = recv_refs[d // near].at[d % near]
        source = me ^ d
        packed = recv_ref[rows : rows + 16, :].astype(jnp.float32)
        place = pl.ds(pl.multiple_of(source * query_count, query_count), query_count)
        ext_ref[place, :] = packed[:query_count]
        low_ref[place, :] = packed[8 : 8 + query_count]
        qn_ref[pl.ds(pl.multiple_of(source * rows, rows), rows), :] = unit_rows(
            recv_ref[:rows, :]
        )[0].astype(jnp.bfloat16)
    qn_ref[sources * rows :, :] = jnp.zeros((query_tokens, width), jnp.bfloat16)

    main = ext_ref[...]
    lanes = lane_ids(main.shape)
    lanes_float = lanes.astype(jnp.float32)
    live = lanes < cand_count
    local = pltpu.roll(main, 128 - cand_count, 1)
    logits = (
        pltpu.roll(main, 128 - 2 * cand_count, 1)
        + pltpu.roll(main, 128 - 3 * cand_count, 1)
        + low_ref[...]
    )
    raised = jnp.where(live, jnp.exp(logits), 0.0)
    target = raised / jnp.sum(raised, -1, keepdims=True)
    local = jnp.where(main == owner, local, -1.0)
    many = jnp.zeros(main.shape, jnp.float32)
    wanted = jnp.zeros(main.shape, jnp.float32)
    for c in range(cand_count):
        same = local[:, c : c + 1] == lanes_float
        many = many + jnp.where(same, 1.0, 0.0)
        wanted = wanted + jnp.where(same, target[:, c : c + 1], 0.0)
    many_ref[...] = many
    target_ref[...] = wanted
    active = many > 0.0
    lower = (
        lax.broadcasted_iota(jnp.int32, (group, group), 0)
        > lax.broadcasted_iota(jnp.int32, (group, group), 1)
    ).astype(jnp.bfloat16)
    active_value = jnp.where(active, 1.0, 0.0)
    rank = jnp.dot(lower, active_value.astype(jnp.bfloat16), preferred_element_type=jnp.float32)
    rank = jnp.where(active, rank, -1.0)
    less = lax.broadcasted_iota(jnp.int32, main.shape, 0).astype(jnp.float32) - group
    for w in range(empty):
        word = jnp.zeros((1, 128), jnp.int32)
        for b in range(4):
            found = jnp.sum(jnp.where(rank == 4 * w + b, less, 0.0), 0, keepdims=True) + group
            word = word | (found.astype(jnp.int32) << (8 * b))
        list_ref[w : w + 1, :] = word
    blank = jnp.full((tables - empty, 128), group, jnp.int32)
    list_ref[empty:tables, :] = blank | (blank << 8) | (blank << 16) | (blank << 24)
    square = (128, 128)
    first_id = lax.broadcasted_iota(jnp.int32, square, 0)
    second_id = lax.broadcasted_iota(jnp.int32, square, 1)
    counts = lax.dot_general(
        active_value.astype(jnp.bfloat16),
        jnp.ones((group, 128), jnp.bfloat16),
        (((0,), (0,)), ((), ())),
        preferred_element_type=jnp.float32,
    )
    chunks = jnp.floor((counts + (chunk_pairs - 1)) * (1.0 / chunk_pairs))
    more = jnp.maximum(chunks - 2.0, 0.0)
    lower_square = (first_id >= second_id).astype(jnp.bfloat16)
    ends = jnp.dot(lower_square, chunks.astype(jnp.bfloat16), preferred_element_type=jnp.float32)
    more_ends = jnp.dot(lower_square, more.astype(jnp.bfloat16), preferred_element_type=jnp.float32)
    chunk_id = lax.broadcasted_iota(jnp.int32, (1, 128), 1).astype(jnp.float32)

    def places_of(chunk_ends, chunk_counts):
        past = chunk_ends <= second_id.astype(jnp.float32)
        passage_of = jnp.sum(jnp.where(past, 1.0, 0.0), 0, keepdims=True)
        start_of = jnp.sum(jnp.where(past, chunk_counts, 0.0), 0, keepdims=True)
        return passage_of, chunk_id - start_of

    def last_row(values):
        return jnp.sum(jnp.where(first_id == 127, values, 0.0), 0, keepdims=True)

    passage_of, chunk_of = places_of(ends, chunks)
    more_passage, more_chunk = places_of(more_ends, more)
    beyond = passage_of > pass_count - 0.5
    rows_of = (
        jnp.where(beyond, 0.0, passage_of),
        jnp.where(beyond, float(empty), chunk_of * (chunk_pairs // 4)),
        jnp.sum(jnp.where(first_id == second_id, ends - chunks, 0.0), 0, keepdims=True),
        jnp.sum(active_value, 0, keepdims=True),
        last_row(ends),
        more_passage,
        more_chunk + 2.0,
        last_row(more_ends),
    )
    for row, value in enumerate(rows_of):
        list_ref[tables + row : tables + row + 1, :] = value.astype(jnp.int32)
    copy = pltpu.make_async_copy(list_ref, list_smem, sem)
    copy.start()
    copy.wait()

    def soft_copy(slot):
        return pltpu.make_async_copy(soft_ref.at[slot], soft_hbm.at[slot], soft_sems.at[slot])

    def chunk(slot):
        p = list_smem[tables, slot]
        ids = list_ids(list_smem, list_smem[tables + 1, slot], p)
        tile = jnp.concatenate([qn_ref[place, :] for place in query_places(ids, query_tokens)], 0)
        dots = lax.dot_general(
            norm_ref[p], tile, (((1,), (1,)), ((), ())), preferred_element_type=jnp.float32
        )
        power = jnp.exp2(dots * (math.log2(math.e) / softness_scale))
        sums = jnp.sum(power, 0, keepdims=True)
        soft_ref[slot] = power.astype(jnp.bfloat16)
        inverse_ref[pl.ds(slot, 1), :] = 1.0 / sums
        for r, n in enumerate(ids):
            sums_ref[pl.ds(p * stride + n, 1), :query_tokens] = sums[
                :, r * query_tokens : (r + 1) * query_tokens
            ]

    def visit(first, count):
        for u in range(count):
            chunk(first + u)
        for u in range(count):
            soft_copy(first + u).start()

    used = each_chunk(list_smem, tables, visit)

    scores = jnp.zeros(main.shape, jnp.float32)
    for p in range(pass_count):
        logs = jnp.log(sums_ref[p * stride : p * stride + group, :])
        value = softness_scale * jnp.sum(
            jnp.where(lanes < query_tokens, logs, 0.0), -1, keepdims=True
        )
        scores = jnp.where(lanes == p, value, scores)
    scores = jnp.where(active, scores, 0.0)
    score_ref[...] = scores
    mass = jnp.sum(many * jnp.exp(scores), -1, keepdims=True)
    agreed = jnp.sum(wanted * scores, -1, keepdims=True)
    same_id = lax.broadcasted_iota(jnp.int32, main.shape, 0) == lanes
    message = jnp.concatenate(
        [
            jnp.sum(jnp.where(same_id, value, 0.0), 0, keepdims=True) for value in (mass, agreed)
        ]
        + [jnp.zeros((6, 128), jnp.float32)],
        0,
    )
    for s in range(sources):
        zw_ref[s] = message

    def drain(slot, carry):
        soft_copy(slot).wait()
        return carry

    lax.fori_loop(0, used, drain, 0)


def forward(received, norm, cand_count, query_count, query_tokens):
    sources = received[0].shape[0] * len(received)
    pass_count, tokens, width = norm.shape
    group = sources * query_count
    capacity = max(2, -(-5 * query_count * cand_count // (2 * sources)))
    slots = slot_total(pass_count, sources * capacity)
    list_rows = -(-(list_layout(group)[1] + meta_rows) // 8) * 8
    rows = query_count * query_tokens
    soft_shape = (slots, tokens, chunk_pairs * query_tokens)
    flops = 2 * slots * chunk_pairs * query_tokens * tokens * width
    return pl.pallas_call(
        lambda *refs: forward_kernel(
            cand_count, query_count, query_tokens, refs[: len(received)], *refs[len(received) :]
        ),
        in_specs=[VMEM] * (len(received) + 1),
        out_specs=[HBM] + [VMEM] * 7,
        out_shape=[
            pltpu.HBM(soft_shape, jnp.bfloat16),
            jax.ShapeDtypeStruct((sources * rows + query_tokens, width), jnp.bfloat16),
            jax.ShapeDtypeStruct((group, 128), jnp.float32),
            jax.ShapeDtypeStruct((group, 128), jnp.float32),
            jax.ShapeDtypeStruct((group, 128), jnp.float32),
            jax.ShapeDtypeStruct((list_rows, 128), jnp.int32),
            jax.ShapeDtypeStruct((sources, 8, 128), jnp.float32),
            jax.ShapeDtypeStruct((slots, chunk_pairs * query_tokens), jnp.float32),
        ],
        scratch_shapes=[
            pltpu.VMEM(soft_shape, jnp.bfloat16),
            pltpu.VMEM((group, 128), jnp.float32),
            pltpu.VMEM((group, 128), jnp.float32),
            pltpu.VMEM((pass_count * (group + row_pad), 128), jnp.float32),
            pltpu.SMEM((list_rows, 128), jnp.int32),
            pltpu.SemaphoreType.DMA,
            pltpu.SemaphoreType.DMA((slots,)),
        ],
        compiler_params=params(),
        cost_estimate=pl.CostEstimate(flops=flops, bytes_accessed=12 << 20, transcendentals=1 << 22),
        name="forward",
    )(*received, norm)


def spread(ref, values, pass_count, stride, start=0):
    group = values.shape[0]
    for p in range(pass_count):
        ref[p * stride : p * stride + group, :] = jnp.broadcast_to(
            values[:, start + p : start + p + 1], (group, 128)
        )
        ref[p * stride + group : (p + 1) * stride, :] = jnp.zeros((stride - group, 128), jnp.float32)


def attend_kernel(
    query_tokens,
    flip_hbm,
    soft_hbm,
    list_ref,
    score_ref,
    many_ref,
    target_ref,
    inverse_ref,
    raised_ref,
    wanted_ref,
    flip_ref,
    soft_ref,
    raised_rows,
    wanted_rows,
    raised_sum,
    wanted_sum,
    list_smem,
    sem,
    flip_sem,
    soft_sems,
):
    pass_count = flip_ref.shape[0]
    group = score_ref.shape[0]
    stride = group + row_pad
    list_copy = pltpu.make_async_copy(list_ref, list_smem, sem)
    list_copy.start()
    flip_copies = part_copies(flip_hbm, flip_ref, flip_sem)
    empty, tables = list_layout(group)

    def soft_copy(slot):
        return pltpu.make_async_copy(soft_hbm.at[slot], soft_ref.at[slot], soft_sems.at[slot])

    def fetch(slot, carry):
        soft_copy(slot).start()
        return carry

    lax.fori_loop(0, chunk_unroll, fetch, 0)
    for copy in flip_copies:
        copy.start()
    lax.fori_loop(chunk_unroll, early_slots, fetch, 0)
    list_copy.wait()
    used = slots_used(list_smem, tables)
    lax.fori_loop(early_slots, used, fetch, 0)
    spread(raised_rows, many_ref[...] * jnp.exp(score_ref[...]), pass_count, stride)
    spread(wanted_rows, target_ref[...], pass_count, stride)
    raised_sum[...] = jnp.zeros(raised_sum.shape, jnp.float32)
    wanted_sum[...] = jnp.zeros(wanted_sum.shape, jnp.float32)
    for copy in flip_copies:
        copy.wait()

    def chunk(slot):
        p = list_smem[tables, slot]
        ids = list_ids(list_smem, list_smem[tables + 1, slot], p)
        places = query_places(ids, query_tokens)
        mixed = jnp.dot(flip_ref[p], soft_ref[slot], preferred_element_type=jnp.float32)
        mixed = (mixed * inverse_ref[pl.ds(slot, 1), :]).astype(jnp.bfloat16)
        mixed = jnp.transpose(mixed, (1, 0)).astype(jnp.float32)
        for total, rows in ((raised_sum, raised_rows), (wanted_sum, wanted_rows)):
            added = [
                total[place, :]
                + mixed[r * query_tokens : (r + 1) * query_tokens]
                * rows[pl.ds(p * stride + ids[r], 1), :]
                for r, place in enumerate(places)
            ]
            for place, value in zip(places, added):
                total[place, :] = value

    def visit(first, count):
        for u in range(count):
            soft_copy(first + u).wait()
        for u in range(count):
            chunk(first + u)

    each_chunk(list_smem, tables, visit)

    def drain(slot, carry):
        soft_copy(slot).wait()
        return carry

    lax.fori_loop(used, early_slots, drain, 0)
    raised_ref[...] = raised_sum[: group * query_tokens, :]
    wanted_ref[...] = wanted_sum[: group * query_tokens, :]


def attend(flip, soft, ids, score, many, target, inverse, query_tokens):
    slots, tokens, columns = soft.shape
    pass_count, width, _ = flip.shape
    group = score.shape[0]
    flops = 2 * slots * columns * tokens * width
    total = jax.ShapeDtypeStruct((group * query_tokens, width), jnp.float32)
    rows = pltpu.VMEM((pass_count * (group + row_pad), 128), jnp.float32)
    padded = pltpu.VMEM(((group + 1) * query_tokens, width), jnp.float32)
    return pl.pallas_call(
        lambda *refs: attend_kernel(query_tokens, *refs),
        in_specs=[HBM, HBM] + [VMEM] * 5,
        out_specs=[VMEM] * 2,
        out_shape=[total, total],
        scratch_shapes=[
            pltpu.VMEM(flip.shape, jnp.bfloat16),
            pltpu.VMEM(soft.shape, jnp.bfloat16),
            rows,
            rows,
            padded,
            padded,
            pltpu.SMEM(ids.shape, jnp.int32),
            pltpu.SemaphoreType.DMA,
            pltpu.SemaphoreType.DMA((copy_parts,)),
            pltpu.SemaphoreType.DMA((slots,)),
        ],
        compiler_params=params(),
        cost_estimate=pl.CostEstimate(flops=flops, bytes_accessed=12 << 20, transcendentals=0),
        name="attend",
    )(in_hbm(flip), in_hbm(soft), ids, score, many, target, inverse)


def halving_order(count):
    order = [0]
    bit = count // 2
    while bit:
        order = order + [x | bit for x in order]
        bit //= 2
    return order


def query_kernel(
    query_tokens,
    zw_ref,
    score_ref,
    many_ref,
    target_ref,
    raised_ref,
    wanted_ref,
    keep_ref,
    send_ref,
    grads_ref,
    scale_ref,
    query_ref,
):
    sources, group = zw_ref.shape[0], score_ref.shape[0]
    sums = zw_ref[0]
    for s in range(1, sources):
        sums = sums + zw_ref[s]
    lanes = lane_ids((group, 128))
    same_id = lax.broadcasted_iota(jnp.int32, (group, 128), 0) == lanes
    inverse = 1.0 / jnp.sum(jnp.where(same_id, sums[:1], 0.0), -1, keepdims=True)
    grads_ref[...] = many_ref[...] * jnp.exp(score_ref[...]) * inverse - target_ref[...]
    scale_ref[...] = jnp.broadcast_to(inverse, scale_ref.shape)
    for n in range(group):
        place = pl.ds(n * query_tokens, query_tokens)
        query_ref[place, :] = (
            raised_ref[place, :] * scale_ref[n : n + 1, :] - wanted_ref[place, :]
        ).astype(jnp.bfloat16)
    me = lax.axis_index("psg")
    rows = group // sources * query_tokens
    half = keep_ref.shape[0]
    for place, d in enumerate(halving_order(sources)):
        start = pl.multiple_of((me ^ d) * rows, rows)
        value = query_ref[pl.ds(start, rows), :]
        if place < half:
            keep_ref[place] = value
        else:
            send_ref[place - half] = value


def query_backward(zw, score, many, target, raised, wanted):
    sources, group = zw.shape[0], score.shape[0]
    rows, width = raised.shape
    part = jax.ShapeDtypeStruct((sources // 2, rows // sources, width), jnp.bfloat16)
    return pl.pallas_call(
        lambda *refs: query_kernel(rows // group, *refs),
        in_specs=[VMEM] * 6,
        out_specs=[VMEM] * 3,
        out_shape=[part, part, jax.ShapeDtypeStruct((group, 128), jnp.float32)],
        scratch_shapes=[
            pltpu.VMEM((group, 128), jnp.float32),
            pltpu.VMEM((rows, width), jnp.bfloat16),
        ],
        compiler_params=params(),
        name="query_backward",
    )(zw, score, many, target, raised, wanted)


def passage_kernel(
    query_tokens,
    list_ref,
    grads_ref,
    qn_ref,
    inverse_ref,
    soft_hbm,
    own_ref,
    core_ref,
    far_ref,
    cross_ref,
    soft_ref,
    grad_ref,
    list_smem,
    sem,
    soft_sems,
):
    list_copy = pltpu.make_async_copy(list_ref, list_smem, sem)
    list_copy.start()
    pass_count, share, width = own_ref.shape
    group = grads_ref.shape[0]
    stride = group + row_pad
    empty, tables = list_layout(group)

    def soft_copy(slot):
        return pltpu.make_async_copy(soft_hbm.at[slot], soft_ref.at[slot], soft_sems.at[slot])

    def fetch(slot, carry):
        soft_copy(slot).start()
        return carry

    def drain(slot, carry):
        soft_copy(slot).wait()
        return carry

    lax.fori_loop(0, early_slots, fetch, 0)
    spread(grad_ref, grads_ref[...], pass_count, stride)
    list_copy.wait()
    total = list_smem[tables + 4, 0]
    lax.fori_loop(early_slots, total, fetch, 0)

    def tile(p, row):
        ids = list_ids(list_smem, row, p)
        return [
            (qn_ref[place, :].astype(jnp.float32) * grad_ref[pl.ds(p * stride + n, 1), :]).astype(
                jnp.bfloat16
            )
            for n, place in zip(ids, query_places(ids, query_tokens))
        ]

    def weights(slot):
        value = soft_ref[slot]
        tokens, columns = value.shape
        scale = jnp.broadcast_to(inverse_ref[pl.ds(slot, 1), :], (16, columns)).astype(jnp.bfloat16)
        return (value.reshape(tokens // 16, 16, columns) * scale[None]).reshape(tokens, columns)

    outs = (own_ref, core_ref, far_ref, cross_ref)

    def passage(p):
        pairs = list_smem[tables + 3, p]
        slot = list_smem[tables + 2, p]
        tiles, softs = [], []
        for h in range(2):
            some = pairs > h * chunk_pairs
            tiles += tile(p, jnp.where(some, h * (chunk_pairs // 4), empty))
            softs.append(weights(jnp.where(some, slot + h, 0)))
        value = jnp.dot(
            jnp.concatenate(softs, 1),
            jnp.concatenate(tiles, 0),
            preferred_element_type=jnp.float32,
        ).astype(jnp.bfloat16)
        for place, ref in enumerate(outs):
            ref[p] = value[place * share : (place + 1) * share]

    def step(i, ready):
        needed = jnp.maximum(list_smem[tables + 2, (i + 1) * passage_unroll], 1)
        lax.fori_loop(ready, needed, drain, 0)
        for u in range(passage_unroll):
            passage(i * passage_unroll + u)
        return needed

    ready = lax.fori_loop(0, pass_count // passage_unroll, step, jnp.int32(0))
    lax.fori_loop(ready, early_slots, drain, 0)

    def rest(i, carry):
        p = list_smem[tables + 5, i]
        b = list_smem[tables + 6, i]
        value = jnp.dot(
            weights(list_smem[tables + 2, p] + b),
            jnp.concatenate(tile(p, b * (chunk_pairs // 4)), 0),
            preferred_element_type=jnp.float32,
        )
        for place, ref in enumerate(outs):
            piece = value[place * share : (place + 1) * share]
            ref[p] = (ref[p].astype(jnp.float32) + piece).astype(jnp.bfloat16)
        return carry

    lax.fori_loop(0, list_smem[tables + 7, 0], rest, 0)


def passage_backward(ids, grads, qn, inverse, soft, pass_count, query_tokens, slices):
    slots, tokens, columns = soft.shape
    width = qn.shape[1]
    piece = jax.ShapeDtypeStruct((pass_count, tokens // slices, width), jnp.bfloat16)
    flops = 4 * pass_count * columns * tokens * width
    return pl.pallas_call(
        lambda *refs: passage_kernel(query_tokens, *refs),
        in_specs=[VMEM] * 4 + [HBM],
        out_specs=[VMEM] * 4,
        out_shape=[piece] * 4,
        scratch_shapes=[
            pltpu.VMEM(soft.shape, jnp.bfloat16),
            pltpu.VMEM((pass_count * (grads.shape[0] + row_pad), 128), jnp.float32),
            pltpu.SMEM(ids.shape, jnp.int32),
            pltpu.SemaphoreType.DMA,
            pltpu.SemaphoreType.DMA((slots,)),
        ],
        compiler_params=params(),
        cost_estimate=pl.CostEstimate(flops=flops, bytes_accessed=6 << 20, transcendentals=0),
        name="passage_backward",
    )(ids, grads, qn, inverse, in_hbm(soft))


def finish_kernel(raw_ref, *refs):
    out_ref = refs[-1]
    grad = refs[0][...].astype(jnp.float32)
    for ref in refs[1:-1]:
        grad = grad + ref[...].astype(jnp.float32)
    out_ref[...] = tangent(raw_ref[...], grad).astype(jnp.bfloat16)


def finish(raw, parts):
    return pl.pallas_call(
        finish_kernel,
        in_specs=[VMEM] * (1 + len(parts)),
        out_specs=VMEM,
        out_shape=jax.ShapeDtypeStruct(raw.shape, jnp.bfloat16),
        compiler_params=params(),
        name="finish",
    )(raw, *parts)


def finish_queries(raw, parts):
    return pl.pallas_call(
        finish_kernel,
        in_specs=[VMEM] * (1 + len(parts)),
        out_specs=VMEM,
        out_shape=jax.ShapeDtypeStruct(raw.shape, jnp.bfloat16),
        compiler_params=params(),
        name="finish_queries",
    )(raw, *parts)


def shards(queries, passages, candidates, teacher):
    query_count, query_tokens, width = queries.shape
    pass_count = passages.shape[0]
    cand_count = candidates.shape[1]
    sources = lax.axis_size("psg")
    slices = lax.axis_size("qry")
    rows = query_count * query_tokens

    received = pack(queries.reshape(rows, width), candidates, teacher, pass_count)[None]
    while received.shape[0] * 4 < sources:
        bit = received.shape[0]
        swap = [(i, i ^ bit) for i in range(sources)]
        received = jnp.concatenate([received, lax.ppermute(received, "psg", swap)], 0)
    stride = received.shape[0]
    received = [received] + [
        lax.ppermute(received, "psg", [(i, i ^ d) for i in range(sources)])
        for d in range(stride, sources, stride)
    ]
    norm, flip, own_raw = prepare_passages(passages, slices)
    soft, qn, score, many, target, ids, zw, inverse = forward(
        received, norm, cand_count, query_count, query_tokens
    )
    zw = lax.all_to_all(zw, "psg", split_axis=0, concat_axis=0, tiled=True)
    raised_sum, wanted_sum = attend(
        flip, soft, ids, score, many, target, inverse, query_tokens
    )
    keep, send, grads = query_backward(zw, score, many, target, raised_sum, wanted_sum)
    near = [(k, k ^ 1) for k in range(slices)]
    away = [(k, k ^ 2) for k in range(slices)]
    own, core, far, cross = passage_backward(
        ids, grads, qn, inverse, soft, pass_count, query_tokens, slices
    )
    cross = lax.ppermute(cross, "qry", near)
    far = (far.astype(jnp.float32) + cross.astype(jnp.float32)).astype(jnp.bfloat16)
    far, send, core = lax.optimization_barrier((far, send, core))
    far = lax.ppermute(far, "qry", away)
    core = lax.ppermute(core, "qry", near)
    bit = 1
    while sources // bit > 4:
        send = lax.ppermute(send, "psg", [(i, i ^ bit) for i in range(sources)])
        send, zw = lax.optimization_barrier((send, zw))
        total = keep.astype(jnp.float32) + send.astype(jnp.float32)
        half = total.shape[0] // 2
        bit *= 2
        if sources // bit > 4:
            keep, send = total[:half], total[half:].astype(jnp.bfloat16)
    query_parts = [total[0]]
    for place, d in enumerate(halving_order(sources)[: total.shape[0]]):
        if place:
            piece = total[place].astype(jnp.bfloat16)
            query_parts.append(lax.ppermute(piece, "psg", [(i, i ^ d) for i in range(sources)]))
    grad_queries = finish_queries(queries.reshape(rows, width), query_parts)

    grad_passages = finish(own_raw, [own, core, far])

    raised = jnp.exp(teacher)
    raised_sum = jnp.sum(raised, -1, keepdims=True)
    log_target = teacher - jnp.log(raised_sum)
    known = jnp.sum(raised / raised_sum * log_target, -1)
    mine = lax.dynamic_slice_in_dim(
        jnp.sum(zw[:, :2], 0), lax.axis_index("psg") * query_count, query_count, 1
    )
    pair_loss = known - mine[1] + jnp.log(mine[0])
    return (pair_loss, grad_queries.reshape(queries.shape), grad_passages)


def solution(mesh):
    placed = (
        P(("psg", "qry"), None, None),
        P("psg", None, None),
        P(("psg", "qry"), None),
        P(("psg", "qry"), None),
    )
    return jax.shard_map(
        shards,
        mesh=mesh,
        in_specs=placed,
        out_specs=(P(("psg", "qry")), P(("psg", "qry"), None, None), P("psg", "qry", None)),
        check_vma=False,
    )
```

```python
import math

import jax
import jax.numpy as jnp
from jax import lax
from jax.experimental import pallas as pl
from jax.experimental.pallas import tpu as pltpu
from jax.sharding import PartitionSpec as P

epsilon = 1e-06
softness_scale = 0.05
chunk_pairs = 8
vmem_bytes = 20 << 20
row_pad = 8

VMEM = pl.BlockSpec(memory_space=pltpu.VMEM)
HBM = pl.BlockSpec(memory_space=pltpu.HBM)
chunk_unroll = 8
chunk_tail = 4
passage_unroll = 8
meta_rows = 8


def in_hbm(array):
    return pltpu.with_memory_space_constraint(array, pltpu.HBM)


def params():
    return pltpu.CompilerParams(vmem_limit_bytes=vmem_bytes)


def unit_rows(values):
    widened = values.astype(jnp.float32)
    inverse = lax.rsqrt(jnp.sum(widened * widened, -1, keepdims=True) + epsilon)
    return widened * inverse, inverse


def round_bf16(values):
    return values.astype(jnp.bfloat16).astype(jnp.float32)


def pack_kernel(pass_count, *refs):
    sources, targets, out_ref, sems = refs[:3], refs[4:7], refs[3], refs[7]
    copies = [
        pltpu.make_async_copy(source, target, sems.at[i])
        for i, (source, target) in enumerate(zip(sources, targets))
    ]
    for copy in copies:
        copy.start()
    for copy in copies:
        copy.wait()
    queries_ref, candidates_ref, teacher_ref = targets
    query_count, cand_count = teacher_ref.shape
    ids = candidates_ref[...].astype(jnp.float32)
    owner = jnp.floor((ids + 0.5) * (1.0 / pass_count))
    values = teacher_ref[...]
    high = round_bf16(values)
    middle = round_bf16(values - high)
    low = values - high - middle
    main = jnp.concatenate([owner, ids - owner * pass_count, high, middle], 1)
    blank = jnp.zeros((8 - query_count, 128), jnp.float32)
    low = jnp.concatenate([low, jnp.zeros((query_count, 128 - cand_count), jnp.float32)], 1)
    extra = jnp.concatenate([main, blank, low, blank], 0).astype(jnp.bfloat16)
    rows = queries_ref.shape[0]
    out_ref[:rows, :] = queries_ref[...]
    out_ref[rows:, :] = extra


def pack(queries, candidates, teacher, pass_count):
    rows, width = queries.shape
    return pl.pallas_call(
        lambda *refs: pack_kernel(pass_count, *refs),
        in_specs=[HBM] * 3,
        out_specs=VMEM,
        out_shape=jax.ShapeDtypeStruct((rows + 16, width), jnp.bfloat16),
        scratch_shapes=[
            pltpu.VMEM(queries.shape, queries.dtype),
            pltpu.VMEM(candidates.shape, candidates.dtype),
            pltpu.VMEM(teacher.shape, teacher.dtype),
            pltpu.SemaphoreType.DMA((3,)),
        ],
        compiler_params=params(),
        name="pack",
    )(in_hbm(queries), in_hbm(candidates), in_hbm(teacher))


def lane_ids(shape):
    return lax.broadcasted_iota(jnp.int32, shape, len(shape) - 1)


def tangent(raw, grad):
    unit, inverse = unit_rows(raw)
    return inverse * (grad - unit * jnp.sum(unit * grad, -1, keepdims=True))


def passages_kernel(
    slices, in_hbm_ref, norm_ref, flip_ref, own_ref, in_ref, in_sems
):
    total, tokens, _ = norm_ref.shape
    parts = in_sems.shape[0]
    count = total // parts
    share = tokens // slices
    me = lax.axis_index("qry")

    def in_copy(part):
        place = pl.ds(part * count, count)
        return pltpu.make_async_copy(in_hbm_ref.at[place], in_ref.at[place], in_sems.at[part])

    for part in range(parts):
        in_copy(part).start()
    for part in range(parts):
        in_copy(part).wait()
        for item in range(part * count, (part + 1) * count):
            for place in range(slices):
                start = pl.multiple_of((me ^ place) * share, share)
                raw = in_ref[item, pl.ds(start, share), :]
                if place == 0:
                    own_ref[item] = raw
                norm_ref[item, pl.ds(place * share, share), :] = unit_rows(raw)[0].astype(
                    jnp.bfloat16
                )
            flip_ref[item] = jnp.transpose(norm_ref[item], (1, 0))


def prepare_passages(passages, slices):
    count, tokens, width = passages.shape
    parts = math.gcd(count, 4)
    share = tokens // slices
    return pl.pallas_call(
        lambda *refs: passages_kernel(slices, *refs),
        in_specs=[HBM],
        out_specs=[VMEM] * 3,
        out_shape=[
            jax.ShapeDtypeStruct((count, tokens, width), jnp.bfloat16),
            jax.ShapeDtypeStruct((count, width, tokens), jnp.bfloat16),
            jax.ShapeDtypeStruct((count, share, width), jnp.bfloat16),
        ],
        scratch_shapes=[
            pltpu.VMEM((count, tokens, width), jnp.bfloat16),
            pltpu.SemaphoreType.DMA((parts,)),
        ],
        compiler_params=params(),
        cost_estimate=pl.CostEstimate(flops=1 << 24, bytes_accessed=6 << 20, transcendentals=0),
        name="prepare_passages",
    )(in_hbm(passages))


def list_layout(group):
    empty = -(-group // chunk_pairs) * chunk_pairs // 4
    return empty, empty + chunk_pairs // 4


def slot_total(pass_count, pairs):
    worst = (pairs + pass_count * (chunk_pairs - 1)) // chunk_pairs
    return -(-worst // chunk_unroll) * chunk_unroll


def list_ids(list_smem, row, p):
    words = [list_smem[row + w, p] for w in range(chunk_pairs // 4)]
    return [(words[r // 4] >> (8 * (r % 4))) & 255 for r in range(chunk_pairs)]


def each_chunk(list_smem, tables, visit):
    total = jnp.maximum(list_smem[tables + 4, 0], 1)
    full = total // chunk_unroll
    tail = (total - full * chunk_unroll + chunk_tail - 1) // chunk_tail

    def step(i, carry):
        visit(i * chunk_unroll, chunk_unroll)
        return carry

    def tail_step(i, carry):
        visit(full * chunk_unroll + i * chunk_tail, chunk_tail)
        return carry

    lax.fori_loop(0, full, step, 0)
    lax.fori_loop(0, tail, tail_step, 0)


def query_places(ids, query_tokens):
    return [pl.ds(pl.multiple_of(n * query_tokens, query_tokens), query_tokens) for n in ids]


def forward_kernel(
    cand_count,
    query_count,
    query_tokens,
    recv_refs,
    norm_ref,
    soft_ref,
    qn_ref,
    score_ref,
    many_ref,
    target_ref,
    list_ref,
    zw_ref,
    inverse_ref,
    ext_ref,
    low_ref,
    sums_ref,
    list_smem,
    sem,
):
    near = recv_refs[0].shape[0]
    sources = near * len(recv_refs)
    pass_count, tokens, width = norm_ref.shape
    group = sources * query_count
    rows = query_count * query_tokens
    stride = group + row_pad
    empty, tables = list_layout(group)
    me = lax.axis_index("psg")
    owner = me.astype(jnp.float32)
    for d in range(sources):
        recv_ref = recv_refs[d // near].at[d % near]
        source = me ^ d
        packed = recv_ref[rows : rows + 16, :].astype(jnp.float32)
        place = pl.ds(pl.multiple_of(source * query_count, query_count), query_count)
        ext_ref[place, :] = packed[:query_count]
        low_ref[place, :] = packed[8 : 8 + query_count]

    main = ext_ref[...]
    lanes = lane_ids(main.shape)
    lanes_float = lanes.astype(jnp.float32)
    live = lanes < cand_count
    local = pltpu.roll(main, 128 - cand_count, 1)
    logits = (
        pltpu.roll(main, 128 - 2 * cand_count, 1)
        + pltpu.roll(main, 128 - 3 * cand_count, 1)
        + low_ref[...]
    )
    raised = jnp.where(live, jnp.exp(logits), 0.0)
    target = raised / jnp.sum(raised, -1, keepdims=True)
    local = jnp.where(main == owner, local, -1.0)
    many = jnp.zeros(main.shape, jnp.float32)
    wanted = jnp.zeros(main.shape, jnp.float32)
    for c in range(cand_count):
        same = local[:, c : c + 1] == lanes_float
        many = many + jnp.where(same, 1.0, 0.0)
        wanted = wanted + jnp.where(same, target[:, c : c + 1], 0.0)
    many_ref[...] = many
    target_ref[...] = wanted
    active = many > 0.0
    lower = (
        lax.broadcasted_iota(jnp.int32, (group, group), 0)
        > lax.broadcasted_iota(jnp.int32, (group, group), 1)
    ).astype(jnp.bfloat16)
    active_value = jnp.where(active, 1.0, 0.0)
    rank = jnp.dot(lower, active_value.astype(jnp.bfloat16), preferred_element_type=jnp.float32)
    rank = jnp.where(active, rank, -1.0)
    less = lax.broadcasted_iota(jnp.int32, main.shape, 0).astype(jnp.float32) - group
    for w in range(empty):
        word = jnp.zeros((1, 128), jnp.int32)
        for b in range(4):
            found = jnp.sum(jnp.where(rank == 4 * w + b, less, 0.0), 0, keepdims=True) + group
            word = word | (found.astype(jnp.int32) << (8 * b))
        list_ref[w : w + 1, :] = word
    blank = jnp.full((tables - empty, 128), group, jnp.int32)
    list_ref[empty:tables, :] = blank | (blank << 8) | (blank << 16) | (blank << 24)
    square = (128, 128)
    first_id = lax.broadcasted_iota(jnp.int32, square, 0)
    second_id = lax.broadcasted_iota(jnp.int32, square, 1)
    counts = lax.dot_general(
        active_value.astype(jnp.bfloat16),
        jnp.ones((group, 128), jnp.bfloat16),
        (((0,), (0,)), ((), ())),
        preferred_element_type=jnp.float32,
    )
    chunks = jnp.floor((counts + (chunk_pairs - 1)) * (1.0 / chunk_pairs))
    more = jnp.maximum(chunks - 2.0, 0.0)
    lower_square = (first_id >= second_id).astype(jnp.bfloat16)
    ends = jnp.dot(lower_square, chunks.astype(jnp.bfloat16), preferred_element_type=jnp.float32)
    more_ends = jnp.dot(lower_square, more.astype(jnp.bfloat16), preferred_element_type=jnp.float32)
    chunk_id = lax.broadcasted_iota(jnp.int32, (1, 128), 1).astype(jnp.float32)

    def places_of(chunk_ends, chunk_counts):
        past = chunk_ends <= second_id.astype(jnp.float32)
        passage_of = jnp.sum(jnp.where(past, 1.0, 0.0), 0, keepdims=True)
        start_of = jnp.sum(jnp.where(past, chunk_counts, 0.0), 0, keepdims=True)
        return passage_of, chunk_id - start_of

    def last_row(values):
        return jnp.sum(jnp.where(first_id == 127, values, 0.0), 0, keepdims=True)

    passage_of, chunk_of = places_of(ends, chunks)
    more_passage, more_chunk = places_of(more_ends, more)
    beyond = passage_of > pass_count - 0.5
    rows_of = (
        jnp.where(beyond, 0.0, passage_of),
        jnp.where(beyond, float(empty), chunk_of * (chunk_pairs // 4)),
        jnp.sum(jnp.where(first_id == second_id, ends - chunks, 0.0), 0, keepdims=True),
        jnp.sum(active_value, 0, keepdims=True),
        last_row(ends),
        more_passage,
        more_chunk + 2.0,
        last_row(more_ends),
    )
    for row, value in enumerate(rows_of):
        list_ref[tables + row : tables + row + 1, :] = value.astype(jnp.int32)
    copy = pltpu.make_async_copy(list_ref, list_smem, sem)
    copy.start()
    for d in range(sources):
        recv_ref = recv_refs[d // near].at[d % near]
        place = pl.ds(pl.multiple_of((me ^ d) * rows, rows), rows)
        qn_ref[place, :] = unit_rows(recv_ref[:rows, :])[0].astype(jnp.bfloat16)
    qn_ref[sources * rows :, :] = jnp.zeros((query_tokens, width), jnp.bfloat16)
    copy.wait()

    def chunk(slot):
        p = list_smem[tables, slot]
        ids = list_ids(list_smem, list_smem[tables + 1, slot], p)
        tile = jnp.concatenate([qn_ref[place, :] for place in query_places(ids, query_tokens)], 0)
        dots = lax.dot_general(
            norm_ref[p], tile, (((1,), (1,)), ((), ())), preferred_element_type=jnp.float32
        )
        power = jnp.exp2(dots * (math.log2(math.e) / softness_scale))
        sums = jnp.sum(power, 0, keepdims=True)
        soft_ref[slot] = power.astype(jnp.bfloat16)
        inverse_ref[pl.ds(slot, 1), :] = 1.0 / sums
        for r, n in enumerate(ids):
            sums_ref[pl.ds(p * stride + n, 1), :query_tokens] = sums[
                :, r * query_tokens : (r + 1) * query_tokens
            ]

    def visit(first, count):
        for u in range(count):
            chunk(first + u)

    each_chunk(list_smem, tables, visit)

    scores = jnp.zeros(main.shape, jnp.float32)
    for p in range(pass_count):
        logs = jnp.log(sums_ref[p * stride : p * stride + group, :])
        value = softness_scale * jnp.sum(
            jnp.where(lanes < query_tokens, logs, 0.0), -1, keepdims=True
        )
        scores = jnp.where(lanes == p, value, scores)
    scores = jnp.where(active, scores, 0.0)
    score_ref[...] = scores
    mass = jnp.sum(many * jnp.exp(scores), -1, keepdims=True)
    agreed = jnp.sum(wanted * scores, -1, keepdims=True)
    same_id = lax.broadcasted_iota(jnp.int32, main.shape, 0) == lanes
    message = jnp.concatenate(
        [
            jnp.sum(jnp.where(same_id, value, 0.0), 0, keepdims=True) for value in (mass, agreed)
        ]
        + [jnp.zeros((6, 128), jnp.float32)],
        0,
    )
    zw_ref[...] = message


def forward(received, norm, cand_count, query_count, query_tokens):
    sources = received[0].shape[0] * len(received)
    pass_count, tokens, width = norm.shape
    group = sources * query_count
    capacity = max(2, -(-5 * query_count * cand_count // (2 * sources)))
    slots = slot_total(pass_count, sources * capacity)
    list_rows = -(-(list_layout(group)[1] + meta_rows) // 8) * 8
    rows = query_count * query_tokens
    soft_shape = (slots, tokens, chunk_pairs * query_tokens)
    flops = 2 * slots * chunk_pairs * query_tokens * tokens * width
    return pl.pallas_call(
        lambda *refs: forward_kernel(
            cand_count, query_count, query_tokens, refs[: len(received)], *refs[len(received) :]
        ),
        in_specs=[VMEM] * (len(received) + 1),
        out_specs=[VMEM] * 8,
        out_shape=[
            jax.ShapeDtypeStruct(soft_shape, jnp.bfloat16),
            jax.ShapeDtypeStruct((sources * rows + query_tokens, width), jnp.bfloat16),
            jax.ShapeDtypeStruct((group, 128), jnp.float32),
            jax.ShapeDtypeStruct((group, 128), jnp.float32),
            jax.ShapeDtypeStruct((group, 128), jnp.float32),
            jax.ShapeDtypeStruct((list_rows, 128), jnp.int32),
            jax.ShapeDtypeStruct((8, 128), jnp.float32),
            jax.ShapeDtypeStruct((slots, chunk_pairs * query_tokens), jnp.float32),
        ],
        scratch_shapes=[
            pltpu.VMEM((group, 128), jnp.float32),
            pltpu.VMEM((group, 128), jnp.float32),
            pltpu.VMEM((pass_count * (group + row_pad), 128), jnp.float32),
            pltpu.SMEM((list_rows, 128), jnp.int32),
            pltpu.SemaphoreType.DMA,
        ],
        compiler_params=params(),
        cost_estimate=pl.CostEstimate(flops=flops, bytes_accessed=12 << 20, transcendentals=1 << 22),
        name="forward",
    )(*received, norm)


def spread(ref, values, pass_count, stride, start=0):
    group = values.shape[0]
    for p in range(pass_count):
        ref[p * stride : p * stride + group, :] = jnp.broadcast_to(
            values[:, start + p : start + p + 1], (group, 128)
        )
        ref[p * stride + group : (p + 1) * stride, :] = jnp.zeros((stride - group, 128), jnp.float32)


def attend_kernel(
    query_tokens,
    flip_ref,
    soft_ref,
    list_ref,
    score_ref,
    many_ref,
    target_ref,
    inverse_ref,
    raised_ref,
    wanted_ref,
    raised_rows,
    wanted_rows,
    list_smem,
    sem,
):
    pass_count = flip_ref.shape[0]
    group = score_ref.shape[0]
    stride = group + row_pad
    list_copy = pltpu.make_async_copy(list_ref, list_smem, sem)
    list_copy.start()
    empty, tables = list_layout(group)

    spread(raised_rows, many_ref[...] * jnp.exp(score_ref[...]), pass_count, stride)
    spread(wanted_rows, target_ref[...], pass_count, stride)
    raised_ref[...] = jnp.zeros(raised_ref.shape, jnp.float32)
    wanted_ref[...] = jnp.zeros(wanted_ref.shape, jnp.float32)
    list_copy.wait()

    def chunk(slot):
        p = list_smem[tables, slot]
        ids = list_ids(list_smem, list_smem[tables + 1, slot], p)
        places = query_places(ids, query_tokens)
        mixed = jnp.dot(flip_ref[p], soft_ref[slot], preferred_element_type=jnp.float32)
        mixed = (mixed * inverse_ref[pl.ds(slot, 1), :]).astype(jnp.bfloat16)
        mixed = jnp.transpose(mixed, (1, 0)).astype(jnp.float32)
        for total, rows in ((raised_ref, raised_rows), (wanted_ref, wanted_rows)):
            added = [
                total[place, :]
                + mixed[r * query_tokens : (r + 1) * query_tokens]
                * rows[pl.ds(p * stride + ids[r], 1), :]
                for r, place in enumerate(places)
            ]
            for place, value in zip(places, added):
                total[place, :] = value

    def visit(first, count):
        for u in range(count):
            chunk(first + u)

    each_chunk(list_smem, tables, visit)


def attend(flip, soft, ids, score, many, target, inverse, query_tokens):
    slots, tokens, columns = soft.shape
    pass_count, width, _ = flip.shape
    group = score.shape[0]
    flops = 2 * slots * columns * tokens * width
    total = jax.ShapeDtypeStruct(((group + 1) * query_tokens, width), jnp.float32)
    rows = pltpu.VMEM((pass_count * (group + row_pad), 128), jnp.float32)
    return pl.pallas_call(
        lambda *refs: attend_kernel(query_tokens, *refs),
        in_specs=[VMEM] * 7,
        out_specs=[VMEM] * 2,
        out_shape=[total, total],
        scratch_shapes=[
            rows,
            rows,
            pltpu.SMEM(ids.shape, jnp.int32),
            pltpu.SemaphoreType.DMA,
        ],
        compiler_params=params(),
        cost_estimate=pl.CostEstimate(flops=flops, bytes_accessed=12 << 20, transcendentals=0),
        name="attend",
    )(flip, soft, ids, score, many, target, inverse)


def halving_order(count):
    order = [0]
    bit = count // 2
    while bit:
        order = order + [x | bit for x in order]
        bit //= 2
    return order


def query_kernel(
    query_tokens,
    sources,
    zw_refs,
    score_ref,
    many_ref,
    target_ref,
    raised_ref,
    wanted_ref,
    keep_ref,
    send_ref,
    grads_ref,
    scale_ref,
    query_ref,
):
    group = score_ref.shape[0]
    sums = sum(ref[...] for ref in zw_refs)
    lanes = lane_ids((group, 128))
    same_id = lax.broadcasted_iota(jnp.int32, (group, 128), 0) == lanes
    inverse = 1.0 / jnp.sum(jnp.where(same_id, sums[:1], 0.0), -1, keepdims=True)
    grads_ref[...] = many_ref[...] * jnp.exp(score_ref[...]) * inverse - target_ref[...]
    scale_ref[...] = jnp.broadcast_to(inverse, scale_ref.shape)
    for n in range(group):
        place = pl.ds(n * query_tokens, query_tokens)
        query_ref[place, :] = (
            raised_ref[place, :] * scale_ref[n : n + 1, :] - wanted_ref[place, :]
        ).astype(jnp.bfloat16)
    me = lax.axis_index("psg")
    rows = group // sources * query_tokens
    half = keep_ref.shape[0]
    for place, d in enumerate(halving_order(sources)):
        start = pl.multiple_of((me ^ d) * rows, rows)
        value = query_ref[pl.ds(start, rows), :]
        if place < half:
            keep_ref[place] = value
        else:
            send_ref[place - half] = value


def query_backward(zw, score, many, target, raised, wanted, sources):
    group = score.shape[0]
    width = raised.shape[1]
    rows = raised.shape[0] // (group + 1) * group
    part = jax.ShapeDtypeStruct((sources // 2, rows // sources, width), jnp.bfloat16)
    return pl.pallas_call(
        lambda *refs: query_kernel(
            rows // group, sources, refs[: len(zw)], *refs[len(zw) :]
        ),
        in_specs=[VMEM] * (len(zw) + 5),
        out_specs=[VMEM] * 3,
        out_shape=[part, part, jax.ShapeDtypeStruct((group, 128), jnp.float32)],
        scratch_shapes=[
            pltpu.VMEM((group, 128), jnp.float32),
            pltpu.VMEM((rows, width), jnp.bfloat16),
        ],
        compiler_params=params(),
        name="query_backward",
    )(*zw, score, many, target, raised, wanted)


def passage_kernel(
    query_tokens,
    list_ref,
    grads_ref,
    qn_ref,
    inverse_ref,
    soft_ref,
    own_ref,
    core_ref,
    far_ref,
    cross_ref,
    grad_ref,
    list_smem,
    sem,
):
    list_copy = pltpu.make_async_copy(list_ref, list_smem, sem)
    list_copy.start()
    pass_count, share, width = own_ref.shape
    group = grads_ref.shape[0]
    stride = group + row_pad
    empty, tables = list_layout(group)
    spread(grad_ref, grads_ref[...], pass_count, stride)
    list_copy.wait()

    def tile(p, row):
        ids = list_ids(list_smem, row, p)
        return [
            (qn_ref[place, :].astype(jnp.float32) * grad_ref[pl.ds(p * stride + n, 1), :]).astype(
                jnp.bfloat16
            )
            for n, place in zip(ids, query_places(ids, query_tokens))
        ]

    def weights(slot):
        value = soft_ref[slot]
        tokens, columns = value.shape
        scale = jnp.broadcast_to(inverse_ref[pl.ds(slot, 1), :], (16, columns)).astype(jnp.bfloat16)
        return (value.reshape(tokens // 16, 16, columns) * scale[None]).reshape(tokens, columns)

    outs = (own_ref, core_ref, far_ref, cross_ref)

    def passage(p):
        pairs = list_smem[tables + 3, p]
        slot = list_smem[tables + 2, p]
        tiles, softs = [], []
        for h in range(2):
            some = pairs > h * chunk_pairs
            tiles += tile(p, jnp.where(some, h * (chunk_pairs // 4), empty))
            softs.append(weights(jnp.where(some, slot + h, 0)))
        value = jnp.dot(
            jnp.concatenate(softs, 1),
            jnp.concatenate(tiles, 0),
            preferred_element_type=jnp.float32,
        ).astype(jnp.bfloat16)
        for place, ref in enumerate(outs):
            ref[p] = value[place * share : (place + 1) * share]

    def step(i, carry):
        for u in range(passage_unroll):
            passage(i * passage_unroll + u)
        return carry

    lax.fori_loop(0, pass_count // passage_unroll, step, 0)

    def rest(i, carry):
        p = list_smem[tables + 5, i]
        b = list_smem[tables + 6, i]
        value = jnp.dot(
            weights(list_smem[tables + 2, p] + b),
            jnp.concatenate(tile(p, b * (chunk_pairs // 4)), 0),
            preferred_element_type=jnp.float32,
        )
        for place, ref in enumerate(outs):
            piece = value[place * share : (place + 1) * share]
            ref[p] = (ref[p].astype(jnp.float32) + piece).astype(jnp.bfloat16)
        return carry

    lax.fori_loop(0, list_smem[tables + 7, 0], rest, 0)


def passage_backward(ids, grads, qn, inverse, soft, pass_count, query_tokens, slices):
    _, tokens, columns = soft.shape
    width = qn.shape[1]
    piece = jax.ShapeDtypeStruct((pass_count, tokens // slices, width), jnp.bfloat16)
    flops = 4 * pass_count * columns * tokens * width
    return pl.pallas_call(
        lambda *refs: passage_kernel(query_tokens, *refs),
        in_specs=[VMEM] * 5,
        out_specs=[VMEM] * 4,
        out_shape=[piece] * 4,
        scratch_shapes=[
            pltpu.VMEM((pass_count * (grads.shape[0] + row_pad), 128), jnp.float32),
            pltpu.SMEM(ids.shape, jnp.int32),
            pltpu.SemaphoreType.DMA,
        ],
        compiler_params=params(),
        cost_estimate=pl.CostEstimate(flops=flops, bytes_accessed=6 << 20, transcendentals=0),
        name="passage_backward",
    )(ids, grads, qn, inverse, soft)


def finish_kernel(query_parts, *refs):
    raw_query, raw_passage = refs[:2]
    query_out, passage_out = refs[-2:]
    queries, passages = refs[2 : 2 + query_parts], refs[2 + query_parts : -2]
    for raw, parts, out in ((raw_query, queries, query_out), (raw_passage, passages, passage_out)):
        grad = sum(ref[...].astype(jnp.float32) for ref in parts)
        out[...] = tangent(raw[...], grad).astype(jnp.bfloat16)


def finish(raw_query, raw_passage, query_parts, passage_parts):
    count = 2 + len(query_parts) + len(passage_parts)
    return pl.pallas_call(
        lambda *refs: finish_kernel(len(query_parts), *refs),
        in_specs=[VMEM] * count,
        out_specs=[VMEM] * 2,
        out_shape=[
            jax.ShapeDtypeStruct(raw_query.shape, jnp.bfloat16),
            jax.ShapeDtypeStruct(raw_passage.shape, jnp.bfloat16),
        ],
        compiler_params=params(),
        name="finish",
    )(raw_query, raw_passage, *query_parts, *passage_parts)


def shards(queries, passages, candidates, teacher):
    query_count, query_tokens, width = queries.shape
    pass_count = passages.shape[0]
    cand_count = candidates.shape[1]
    sources = lax.axis_size("psg")
    slices = lax.axis_size("qry")
    rows = query_count * query_tokens

    received = pack(queries.reshape(rows, width), candidates, teacher, pass_count)[None]
    while received.shape[0] * 4 < sources:
        bit = received.shape[0]
        pairs = [(i, i ^ bit) for i in range(sources)]
        received = jnp.concatenate([received, lax.ppermute(received, "psg", pairs)], 0)
    stride = received.shape[0]
    received = [received] + [
        lax.ppermute(received, "psg", [(i, i ^ d) for i in range(sources)])
        for d in range(stride, sources, stride)
    ]
    norm, flip, own_raw = prepare_passages(passages, slices)
    soft, qn, score, many, target, ids, zw, inverse = forward(
        received, norm, cand_count, query_count, query_tokens
    )

    def swap(values, bit):
        return lax.ppermute(values, "psg", [(i, i ^ bit) for i in range(sources)])

    bit = 1
    while sources // bit > 4:
        zw = zw + swap(zw, bit)
        bit *= 2
    raised_sum, wanted_sum = attend(
        flip, soft, ids, score, many, target, inverse, query_tokens
    )
    zw, raised_sum = lax.optimization_barrier((zw, raised_sum))
    zw = [zw] + [swap(zw, d) for d in range(bit, sources, bit)]
    keep, send, grads = query_backward(
        zw, score, many, target, raised_sum, wanted_sum, sources
    )
    near = [(k, k ^ 1) for k in range(slices)]
    away = [(k, k ^ 2) for k in range(slices)]
    own, core, far, cross = passage_backward(
        ids, grads, qn, inverse, soft, pass_count, query_tokens, slices
    )
    cross = lax.ppermute(cross, "qry", near)
    far = (far.astype(jnp.float32) + cross.astype(jnp.float32)).astype(jnp.bfloat16)
    far, core, send = lax.optimization_barrier((far, core, send))
    core = lax.ppermute(core, "qry", near)
    far = lax.ppermute(far, "qry", away)
    bit = 1
    while sources // bit > 4:
        send = lax.ppermute(send, "psg", [(i, i ^ bit) for i in range(sources)])
        send, zw = lax.optimization_barrier((send, zw))
        total = keep.astype(jnp.float32) + send.astype(jnp.float32)
        half = total.shape[0] // 2
        bit *= 2
        if sources // bit > 4:
            keep, send = total[:half], total[half:].astype(jnp.bfloat16)
    query_parts = [total[0]]
    for place, d in enumerate(halving_order(sources)[: total.shape[0]]):
        if place:
            piece = total[place].astype(jnp.bfloat16)
            query_parts.append(lax.ppermute(piece, "psg", [(i, i ^ d) for i in range(sources)]))
    grad_queries, grad_passages = finish(
        queries.reshape(rows, width), own_raw, query_parts, [own, core, far]
    )

    raised = jnp.exp(teacher)
    raised_sum = jnp.sum(raised, -1, keepdims=True)
    log_target = teacher - jnp.log(raised_sum)
    known = jnp.sum(raised / raised_sum * log_target, -1)
    mine = lax.dynamic_slice_in_dim(
        sum(zw)[:2], lax.axis_index("psg") * query_count, query_count, 1
    )
    pair_loss = known - mine[1] + jnp.log(mine[0])
    return (pair_loss, grad_queries.reshape(queries.shape), grad_passages)


def solution(mesh):
    placed = (
        P(("psg", "qry"), None, None),
        P("psg", None, None),
        P(("psg", "qry"), None),
        P(("psg", "qry"), None),
    )
    return jax.shard_map(
        shards,
        mesh=mesh,
        in_specs=placed,
        out_specs=(P(("psg", "qry")), P(("psg", "qry"), None, None), P("psg", "qry", None)),
        check_vma=False,
    )
```

```python
import math

import jax
import jax.numpy as jnp
from jax import lax
from jax.experimental import pallas as pl
from jax.experimental.pallas import tpu as pltpu
from jax.sharding import PartitionSpec as P

epsilon = 1e-06
softness_scale = 0.05
chunk_pairs = 8
vmem_bytes = 20 << 20
row_pad = 8

VMEM = pl.BlockSpec(memory_space=pltpu.VMEM)
HBM = pl.BlockSpec(memory_space=pltpu.HBM)
chunk_unroll = 8
chunk_tail = 4
passage_unroll = 8
meta_rows = 8


def in_hbm(array):
    return pltpu.with_memory_space_constraint(array, pltpu.HBM)


def params():
    return pltpu.CompilerParams(vmem_limit_bytes=vmem_bytes)


def unit_rows(values):
    widened = values.astype(jnp.float32)
    inverse = lax.rsqrt(jnp.sum(widened * widened, -1, keepdims=True) + epsilon)
    return widened * inverse, inverse


def round_bf16(values):
    return values.astype(jnp.bfloat16).astype(jnp.float32)


def pack_kernel(pass_count, *refs):
    sources, targets, out_ref, sems = refs[:3], refs[4:7], refs[3], refs[7]
    copies = [
        pltpu.make_async_copy(source, target, sems.at[i])
        for i, (source, target) in enumerate(zip(sources, targets))
    ]
    for copy in copies:
        copy.start()
    for copy in copies:
        copy.wait()
    queries_ref, candidates_ref, teacher_ref = targets
    query_count, cand_count = teacher_ref.shape
    ids = candidates_ref[...].astype(jnp.float32)
    owner = jnp.floor((ids + 0.5) * (1.0 / pass_count))
    values = teacher_ref[...]
    high = round_bf16(values)
    middle = round_bf16(values - high)
    low = values - high - middle
    main = jnp.concatenate([owner, ids - owner * pass_count, high, middle], 1)
    blank = jnp.zeros((8 - query_count, 128), jnp.float32)
    low = jnp.concatenate([low, jnp.zeros((query_count, 128 - cand_count), jnp.float32)], 1)
    extra = jnp.concatenate([main, blank, low, blank], 0).astype(jnp.bfloat16)
    rows = queries_ref.shape[0]
    out_ref[:rows, :] = queries_ref[...]
    out_ref[rows:, :] = extra


def pack(queries, candidates, teacher, pass_count):
    rows, width = queries.shape
    return pl.pallas_call(
        lambda *refs: pack_kernel(pass_count, *refs),
        in_specs=[HBM] * 3,
        out_specs=VMEM,
        out_shape=jax.ShapeDtypeStruct((rows + 16, width), jnp.bfloat16),
        scratch_shapes=[
            pltpu.VMEM(queries.shape, queries.dtype),
            pltpu.VMEM(candidates.shape, candidates.dtype),
            pltpu.VMEM(teacher.shape, teacher.dtype),
            pltpu.SemaphoreType.DMA((3,)),
        ],
        compiler_params=params(),
        name="pack",
    )(in_hbm(queries), in_hbm(candidates), in_hbm(teacher))


def lane_ids(shape):
    return lax.broadcasted_iota(jnp.int32, shape, len(shape) - 1)


def tangent(raw, grad):
    unit, inverse = unit_rows(raw)
    return inverse * (grad - unit * jnp.sum(unit * grad, -1, keepdims=True))


def passages_kernel(
    slices, in_hbm_ref, norm_ref, flip_ref, own_ref, in_ref, in_sems
):
    total, tokens, _ = norm_ref.shape
    parts = in_sems.shape[0]
    count = total // parts
    share = tokens // slices
    me = lax.axis_index("qry")

    def in_copy(part):
        place = pl.ds(part * count, count)
        return pltpu.make_async_copy(in_hbm_ref.at[place], in_ref.at[place], in_sems.at[part])

    for part in range(parts):
        in_copy(part).start()
    for part in range(parts):
        in_copy(part).wait()
        for item in range(part * count, (part + 1) * count):
            for place in range(slices):
                start = pl.multiple_of((me ^ place) * share, share)
                raw = in_ref[item, pl.ds(start, share), :]
                if place == 0:
                    own_ref[item] = raw
                norm_ref[item, pl.ds(place * share, share), :] = unit_rows(raw)[0].astype(
                    jnp.bfloat16
                )
            flip_ref[item] = jnp.transpose(norm_ref[item], (1, 0))


def prepare_passages(passages, slices):
    count, tokens, width = passages.shape
    parts = math.gcd(count, 4)
    share = tokens // slices
    return pl.pallas_call(
        lambda *refs: passages_kernel(slices, *refs),
        in_specs=[HBM],
        out_specs=[VMEM] * 3,
        out_shape=[
            jax.ShapeDtypeStruct((count, tokens, width), jnp.bfloat16),
            jax.ShapeDtypeStruct((count, width, tokens), jnp.bfloat16),
            jax.ShapeDtypeStruct((count, share, width), jnp.bfloat16),
        ],
        scratch_shapes=[
            pltpu.VMEM((count, tokens, width), jnp.bfloat16),
            pltpu.SemaphoreType.DMA((parts,)),
        ],
        compiler_params=params(),
        cost_estimate=pl.CostEstimate(flops=1 << 24, bytes_accessed=6 << 20, transcendentals=0),
        name="prepare_passages",
    )(in_hbm(passages))


def list_layout(group):
    empty = -(-group // chunk_pairs) * chunk_pairs // 4
    return empty, empty + chunk_pairs // 4


def slot_total(pass_count, pairs):
    worst = (pairs + pass_count * (chunk_pairs - 1)) // chunk_pairs
    return -(-worst // chunk_unroll) * chunk_unroll


def list_ids(list_smem, row, p):
    words = [list_smem[row + w, p] for w in range(chunk_pairs // 4)]
    return [(words[r // 4] >> (8 * (r % 4))) & 255 for r in range(chunk_pairs)]


def each_chunk(list_smem, tables, visit):
    total = jnp.maximum(list_smem[tables + 4, 0], 1)
    full = total // chunk_unroll
    tail = (total - full * chunk_unroll + chunk_tail - 1) // chunk_tail

    def step(i, carry):
        visit(i * chunk_unroll, chunk_unroll)
        return carry

    def tail_step(i, carry):
        visit(full * chunk_unroll + i * chunk_tail, chunk_tail)
        return carry

    lax.fori_loop(0, full, step, 0)
    lax.fori_loop(0, tail, tail_step, 0)


def query_places(ids, query_tokens):
    return [pl.ds(pl.multiple_of(n * query_tokens, query_tokens), query_tokens) for n in ids]


def forward_kernel(
    cand_count,
    query_count,
    query_tokens,
    recv_refs,
    norm_ref,
    soft_ref,
    qn_ref,
    score_ref,
    many_ref,
    target_ref,
    list_ref,
    zw_ref,
    inverse_ref,
    ext_ref,
    low_ref,
    sums_ref,
    list_smem,
    sem,
):
    near = recv_refs[0].shape[0]
    sources = near * len(recv_refs)
    pass_count, tokens, width = norm_ref.shape
    group = sources * query_count
    rows = query_count * query_tokens
    stride = group + row_pad
    empty, tables = list_layout(group)
    me = lax.axis_index("psg")
    owner = me.astype(jnp.float32)
    for d in range(sources):
        recv_ref = recv_refs[d // near].at[d % near]
        source = me ^ d
        packed = recv_ref[rows : rows + 16, :].astype(jnp.float32)
        place = pl.ds(pl.multiple_of(source * query_count, query_count), query_count)
        ext_ref[place, :] = packed[:query_count]
        low_ref[place, :] = packed[8 : 8 + query_count]

    main = ext_ref[...]
    lanes = lane_ids(main.shape)
    lanes_float = lanes.astype(jnp.float32)
    live = lanes < cand_count
    local = pltpu.roll(main, 128 - cand_count, 1)
    logits = (
        pltpu.roll(main, 128 - 2 * cand_count, 1)
        + pltpu.roll(main, 128 - 3 * cand_count, 1)
        + low_ref[...]
    )
    raised = jnp.where(live, jnp.exp(logits), 0.0)
    target = raised / jnp.sum(raised, -1, keepdims=True)
    local = jnp.where(main == owner, local, -1.0)
    many = jnp.zeros(main.shape, jnp.float32)
    wanted = jnp.zeros(main.shape, jnp.float32)
    for c in range(cand_count):
        same = local[:, c : c + 1] == lanes_float
        many = many + jnp.where(same, 1.0, 0.0)
        wanted = wanted + jnp.where(same, target[:, c : c + 1], 0.0)
    many_ref[...] = many
    target_ref[...] = wanted
    active = many > 0.0
    lower = (
        lax.broadcasted_iota(jnp.int32, (group, group), 0)
        > lax.broadcasted_iota(jnp.int32, (group, group), 1)
    ).astype(jnp.bfloat16)
    active_value = jnp.where(active, 1.0, 0.0)
    rank = jnp.dot(lower, active_value.astype(jnp.bfloat16), preferred_element_type=jnp.float32)
    rank = jnp.where(active, rank, -1.0)
    less = lax.broadcasted_iota(jnp.int32, main.shape, 0).astype(jnp.float32) - group
    for w in range(empty):
        word = jnp.zeros((1, 128), jnp.int32)
        for b in range(4):
            found = jnp.sum(jnp.where(rank == 4 * w + b, less, 0.0), 0, keepdims=True) + group
            word = word | (found.astype(jnp.int32) << (8 * b))
        list_ref[w : w + 1, :] = word
    blank = jnp.full((tables - empty, 128), group, jnp.int32)
    list_ref[empty:tables, :] = blank | (blank << 8) | (blank << 16) | (blank << 24)
    square = (128, 128)
    first_id = lax.broadcasted_iota(jnp.int32, square, 0)
    second_id = lax.broadcasted_iota(jnp.int32, square, 1)
    counts = lax.dot_general(
        active_value.astype(jnp.bfloat16),
        jnp.ones((group, 128), jnp.bfloat16),
        (((0,), (0,)), ((), ())),
        preferred_element_type=jnp.float32,
    )
    chunks = jnp.floor((counts + (chunk_pairs - 1)) * (1.0 / chunk_pairs))
    more = jnp.maximum(chunks - 2.0, 0.0)
    lower_square = (first_id >= second_id).astype(jnp.bfloat16)
    ends = jnp.dot(lower_square, chunks.astype(jnp.bfloat16), preferred_element_type=jnp.float32)
    more_ends = jnp.dot(lower_square, more.astype(jnp.bfloat16), preferred_element_type=jnp.float32)
    chunk_id = lax.broadcasted_iota(jnp.int32, (1, 128), 1).astype(jnp.float32)

    def places_of(chunk_ends, chunk_counts):
        past = chunk_ends <= second_id.astype(jnp.float32)
        passage_of = jnp.sum(jnp.where(past, 1.0, 0.0), 0, keepdims=True)
        start_of = jnp.sum(jnp.where(past, chunk_counts, 0.0), 0, keepdims=True)
        return passage_of, chunk_id - start_of

    def last_row(values):
        return jnp.sum(jnp.where(first_id == 127, values, 0.0), 0, keepdims=True)

    passage_of, chunk_of = places_of(ends, chunks)
    more_passage, more_chunk = places_of(more_ends, more)
    beyond = passage_of > pass_count - 0.5
    rows_of = (
        jnp.where(beyond, 0.0, passage_of),
        jnp.where(beyond, float(empty), chunk_of * (chunk_pairs // 4)),
        jnp.sum(jnp.where(first_id == second_id, ends - chunks, 0.0), 0, keepdims=True),
        jnp.sum(active_value, 0, keepdims=True),
        last_row(ends),
        more_passage,
        more_chunk + 2.0,
        last_row(more_ends),
    )
    for row, value in enumerate(rows_of):
        list_ref[tables + row : tables + row + 1, :] = value.astype(jnp.int32)
    copy = pltpu.make_async_copy(list_ref, list_smem, sem)
    copy.start()
    for d in range(sources):
        recv_ref = recv_refs[d // near].at[d % near]
        place = pl.ds(pl.multiple_of((me ^ d) * rows, rows), rows)
        qn_ref[place, :] = unit_rows(recv_ref[:rows, :])[0].astype(jnp.bfloat16)
    qn_ref[sources * rows :, :] = jnp.zeros((query_tokens, width), jnp.bfloat16)
    copy.wait()

    def chunk(slot):
        p = list_smem[tables, slot]
        ids = list_ids(list_smem, list_smem[tables + 1, slot], p)
        tile = jnp.concatenate([qn_ref[place, :] for place in query_places(ids, query_tokens)], 0)
        dots = lax.dot_general(
            norm_ref[p], tile, (((1,), (1,)), ((), ())), preferred_element_type=jnp.float32
        )
        power = jnp.exp2(dots * (math.log2(math.e) / softness_scale))
        sums = jnp.sum(power, 0, keepdims=True)
        soft_ref[slot] = power.astype(jnp.bfloat16)
        inverse_ref[pl.ds(slot, 1), :] = 1.0 / sums
        for r, n in enumerate(ids):
            sums_ref[pl.ds(p * stride + n, 1), :query_tokens] = sums[
                :, r * query_tokens : (r + 1) * query_tokens
            ]

    def visit(first, count):
        for u in range(count):
            chunk(first + u)

    each_chunk(list_smem, tables, visit)

    scores = jnp.zeros(main.shape, jnp.float32)
    for p in range(pass_count):
        logs = jnp.log(sums_ref[p * stride : p * stride + group, :])
        value = softness_scale * jnp.sum(
            jnp.where(lanes < query_tokens, logs, 0.0), -1, keepdims=True
        )
        scores = jnp.where(lanes == p, value, scores)
    scores = jnp.where(active, scores, 0.0)
    score_ref[...] = scores
    mass = jnp.sum(many * jnp.exp(scores), -1, keepdims=True)
    agreed = jnp.sum(wanted * scores, -1, keepdims=True)
    same_id = lax.broadcasted_iota(jnp.int32, main.shape, 0) == lanes
    message = jnp.concatenate(
        [
            jnp.sum(jnp.where(same_id, value, 0.0), 0, keepdims=True) for value in (mass, agreed)
        ]
        + [jnp.zeros((6, 128), jnp.float32)],
        0,
    )
    zw_ref[...] = message


def forward(received, norm, cand_count, query_count, query_tokens):
    sources = received[0].shape[0] * len(received)
    pass_count, tokens, width = norm.shape
    group = sources * query_count
    capacity = max(2, -(-5 * query_count * cand_count // (2 * sources)))
    slots = slot_total(pass_count, sources * capacity)
    list_rows = -(-(list_layout(group)[1] + meta_rows) // 8) * 8
    rows = query_count * query_tokens
    soft_shape = (slots, tokens, chunk_pairs * query_tokens)
    flops = 2 * slots * chunk_pairs * query_tokens * tokens * width
    return pl.pallas_call(
        lambda *refs: forward_kernel(
            cand_count, query_count, query_tokens, refs[: len(received)], *refs[len(received) :]
        ),
        in_specs=[VMEM] * (len(received) + 1),
        out_specs=[VMEM] * 8,
        out_shape=[
            jax.ShapeDtypeStruct(soft_shape, jnp.bfloat16),
            jax.ShapeDtypeStruct((sources * rows + query_tokens, width), jnp.bfloat16),
            jax.ShapeDtypeStruct((group, 128), jnp.float32),
            jax.ShapeDtypeStruct((group, 128), jnp.float32),
            jax.ShapeDtypeStruct((group, 128), jnp.float32),
            jax.ShapeDtypeStruct((list_rows, 128), jnp.int32),
            jax.ShapeDtypeStruct((8, 128), jnp.float32),
            jax.ShapeDtypeStruct((slots, chunk_pairs * query_tokens), jnp.float32),
        ],
        scratch_shapes=[
            pltpu.VMEM((group, 128), jnp.float32),
            pltpu.VMEM((group, 128), jnp.float32),
            pltpu.VMEM((pass_count * (group + row_pad), 128), jnp.float32),
            pltpu.SMEM((list_rows, 128), jnp.int32),
            pltpu.SemaphoreType.DMA,
        ],
        compiler_params=params(),
        cost_estimate=pl.CostEstimate(flops=flops, bytes_accessed=12 << 20, transcendentals=1 << 22),
        name="forward",
    )(*received, norm)


def spread(ref, values, pass_count, stride, start=0):
    group = values.shape[0]
    for p in range(pass_count):
        ref[p * stride : p * stride + group, :] = jnp.broadcast_to(
            values[:, start + p : start + p + 1], (group, 128)
        )
        ref[p * stride + group : (p + 1) * stride, :] = jnp.zeros((stride - group, 128), jnp.float32)


def attend_kernel(
    query_tokens,
    flip_ref,
    soft_ref,
    list_ref,
    score_ref,
    many_ref,
    target_ref,
    inverse_ref,
    raised_ref,
    wanted_ref,
    raised_rows,
    wanted_rows,
    list_smem,
    sem,
):
    pass_count = flip_ref.shape[0]
    group = score_ref.shape[0]
    stride = group + row_pad
    list_copy = pltpu.make_async_copy(list_ref, list_smem, sem)
    list_copy.start()
    empty, tables = list_layout(group)

    spread(raised_rows, many_ref[...] * jnp.exp(score_ref[...]), pass_count, stride)
    spread(wanted_rows, target_ref[...], pass_count, stride)
    raised_ref[...] = jnp.zeros(raised_ref.shape, jnp.float32)
    wanted_ref[...] = jnp.zeros(wanted_ref.shape, jnp.float32)
    list_copy.wait()

    def chunk(slot):
        p = list_smem[tables, slot]
        ids = list_ids(list_smem, list_smem[tables + 1, slot], p)
        places = query_places(ids, query_tokens)
        mixed = jnp.dot(flip_ref[p], soft_ref[slot], preferred_element_type=jnp.float32)
        mixed = (mixed * inverse_ref[pl.ds(slot, 1), :]).astype(jnp.bfloat16)
        mixed = jnp.transpose(mixed, (1, 0)).astype(jnp.float32)
        for total, rows in ((raised_ref, raised_rows), (wanted_ref, wanted_rows)):
            added = [
                total[place, :]
                + mixed[r * query_tokens : (r + 1) * query_tokens]
                * rows[pl.ds(p * stride + ids[r], 1), :]
                for r, place in enumerate(places)
            ]
            for place, value in zip(places, added):
                total[place, :] = value

    def visit(first, count):
        for u in range(count):
            chunk(first + u)

    each_chunk(list_smem, tables, visit)


def attend(flip, soft, ids, score, many, target, inverse, query_tokens):
    slots, tokens, columns = soft.shape
    pass_count, width, _ = flip.shape
    group = score.shape[0]
    flops = 2 * slots * columns * tokens * width
    total = jax.ShapeDtypeStruct(((group + 1) * query_tokens, width), jnp.float32)
    rows = pltpu.VMEM((pass_count * (group + row_pad), 128), jnp.float32)
    return pl.pallas_call(
        lambda *refs: attend_kernel(query_tokens, *refs),
        in_specs=[VMEM] * 7,
        out_specs=[VMEM] * 2,
        out_shape=[total, total],
        scratch_shapes=[
            rows,
            rows,
            pltpu.SMEM(ids.shape, jnp.int32),
            pltpu.SemaphoreType.DMA,
        ],
        compiler_params=params(),
        cost_estimate=pl.CostEstimate(flops=flops, bytes_accessed=12 << 20, transcendentals=0),
        name="attend",
    )(flip, soft, ids, score, many, target, inverse)


def halving_order(count):
    order = [0]
    bit = count // 2
    while bit:
        order = order + [x | bit for x in order]
        bit //= 2
    return order


def query_kernel(
    query_tokens,
    sources,
    zw_refs,
    score_ref,
    many_ref,
    target_ref,
    raised_ref,
    wanted_ref,
    keep_ref,
    send_ref,
    grads_ref,
    scale_ref,
    query_ref,
):
    group = score_ref.shape[0]
    sums = sum(ref[...] for ref in zw_refs)
    lanes = lane_ids((group, 128))
    same_id = lax.broadcasted_iota(jnp.int32, (group, 128), 0) == lanes
    inverse = 1.0 / jnp.sum(jnp.where(same_id, sums[:1], 0.0), -1, keepdims=True)
    grads_ref[...] = many_ref[...] * jnp.exp(score_ref[...]) * inverse - target_ref[...]
    scale_ref[...] = jnp.broadcast_to(inverse, scale_ref.shape)
    for n in range(group):
        place = pl.ds(n * query_tokens, query_tokens)
        query_ref[place, :] = (
            raised_ref[place, :] * scale_ref[n : n + 1, :] - wanted_ref[place, :]
        ).astype(jnp.bfloat16)
    me = lax.axis_index("psg")
    rows = group // sources * query_tokens
    half = keep_ref.shape[0]
    for place, d in enumerate(halving_order(sources)):
        start = pl.multiple_of((me ^ d) * rows, rows)
        value = query_ref[pl.ds(start, rows), :]
        if place < half:
            keep_ref[place] = value
        else:
            send_ref[place - half] = value


def query_backward(zw, score, many, target, raised, wanted, sources):
    group = score.shape[0]
    width = raised.shape[1]
    rows = raised.shape[0] // (group + 1) * group
    part = jax.ShapeDtypeStruct((sources // 2, rows // sources, width), jnp.bfloat16)
    return pl.pallas_call(
        lambda *refs: query_kernel(
            rows // group, sources, refs[: len(zw)], *refs[len(zw) :]
        ),
        in_specs=[VMEM] * (len(zw) + 5),
        out_specs=[VMEM] * 3,
        out_shape=[part, part, jax.ShapeDtypeStruct((group, 128), jnp.float32)],
        scratch_shapes=[
            pltpu.VMEM((group, 128), jnp.float32),
            pltpu.VMEM((rows, width), jnp.bfloat16),
        ],
        compiler_params=params(),
        name="query_backward",
    )(*zw, score, many, target, raised, wanted)


def passage_kernel(
    query_tokens,
    list_ref,
    grads_ref,
    qn_ref,
    inverse_ref,
    soft_ref,
    own_ref,
    core_ref,
    far_ref,
    cross_ref,
    grad_ref,
    list_smem,
    sem,
):
    list_copy = pltpu.make_async_copy(list_ref, list_smem, sem)
    list_copy.start()
    pass_count, share, width = own_ref.shape
    group = grads_ref.shape[0]
    stride = group + row_pad
    empty, tables = list_layout(group)
    spread(grad_ref, grads_ref[...], pass_count, stride)
    list_copy.wait()

    def tile(p, row):
        ids = list_ids(list_smem, row, p)
        return [
            (qn_ref[place, :].astype(jnp.float32) * grad_ref[pl.ds(p * stride + n, 1), :]).astype(
                jnp.bfloat16
            )
            for n, place in zip(ids, query_places(ids, query_tokens))
        ]

    def weights(slot):
        value = soft_ref[slot]
        tokens, columns = value.shape
        scale = jnp.broadcast_to(inverse_ref[pl.ds(slot, 1), :], (16, columns)).astype(jnp.bfloat16)
        return (value.reshape(tokens // 16, 16, columns) * scale[None]).reshape(tokens, columns)

    outs = (own_ref, core_ref, far_ref, cross_ref)

    def passage(p):
        pairs = list_smem[tables + 3, p]
        slot = list_smem[tables + 2, p]
        tiles, softs = [], []
        for h in range(2):
            some = pairs > h * chunk_pairs
            tiles += tile(p, jnp.where(some, h * (chunk_pairs // 4), empty))
            softs.append(weights(jnp.where(some, slot + h, 0)))
        value = jnp.dot(
            jnp.concatenate(softs, 1),
            jnp.concatenate(tiles, 0),
            preferred_element_type=jnp.float32,
        ).astype(jnp.bfloat16)
        for place, ref in enumerate(outs):
            ref[p] = value[place * share : (place + 1) * share]

    def step(i, carry):
        for u in range(passage_unroll):
            passage(i * passage_unroll + u)
        return carry

    lax.fori_loop(0, pass_count // passage_unroll, step, 0)

    def rest(i, carry):
        p = list_smem[tables + 5, i]
        b = list_smem[tables + 6, i]
        value = jnp.dot(
            weights(list_smem[tables + 2, p] + b),
            jnp.concatenate(tile(p, b * (chunk_pairs // 4)), 0),
            preferred_element_type=jnp.float32,
        )
        for place, ref in enumerate(outs):
            piece = value[place * share : (place + 1) * share]
            ref[p] = (ref[p].astype(jnp.float32) + piece).astype(jnp.bfloat16)
        return carry

    lax.fori_loop(0, list_smem[tables + 7, 0], rest, 0)


def passage_backward(ids, grads, qn, inverse, soft, pass_count, query_tokens, slices):
    _, tokens, columns = soft.shape
    width = qn.shape[1]
    piece = jax.ShapeDtypeStruct((pass_count, tokens // slices, width), jnp.bfloat16)
    flops = 4 * pass_count * columns * tokens * width
    return pl.pallas_call(
        lambda *refs: passage_kernel(query_tokens, *refs),
        in_specs=[VMEM] * 5,
        out_specs=[VMEM] * 4,
        out_shape=[piece] * 4,
        scratch_shapes=[
            pltpu.VMEM((pass_count * (grads.shape[0] + row_pad), 128), jnp.float32),
            pltpu.SMEM(ids.shape, jnp.int32),
            pltpu.SemaphoreType.DMA,
        ],
        compiler_params=params(),
        cost_estimate=pl.CostEstimate(flops=flops, bytes_accessed=6 << 20, transcendentals=0),
        name="passage_backward",
    )(ids, grads, qn, inverse, soft)


def finish_kernel(query_parts, *refs):
    raw_query, raw_passage = refs[:2]
    query_out, passage_out = refs[-2:]
    queries, passages = refs[2 : 2 + query_parts], refs[2 + query_parts : -3]
    for raw, parts, out in ((raw_query, queries, query_out), (raw_passage, passages, passage_out)):
        grad = sum(ref[...].astype(jnp.float32) for ref in parts)
        out[...] = tangent(raw[...], grad).astype(jnp.bfloat16)


def finish(raw_query, raw_passage, query_parts, passage_parts, ready):
    count = 2 + len(query_parts) + len(passage_parts)
    return pl.pallas_call(
        lambda *refs: finish_kernel(len(query_parts), *refs),
        in_specs=[VMEM] * count + [pl.BlockSpec(memory_space=pl.ANY)],
        out_specs=[VMEM] * 2,
        out_shape=[
            jax.ShapeDtypeStruct(raw_query.shape, jnp.bfloat16),
            jax.ShapeDtypeStruct(raw_passage.shape, jnp.bfloat16),
        ],
        compiler_params=params(),
        name="finish",
    )(raw_query, raw_passage, *query_parts, *passage_parts, ready)


def shards(queries, passages, candidates, teacher):
    query_count, query_tokens, width = queries.shape
    pass_count = passages.shape[0]
    cand_count = candidates.shape[1]
    sources = lax.axis_size("psg")
    slices = lax.axis_size("qry")
    rows = query_count * query_tokens

    received = pack(queries.reshape(rows, width), candidates, teacher, pass_count)[None]
    while received.shape[0] * 4 < sources:
        bit = received.shape[0]
        pairs = [(i, i ^ bit) for i in range(sources)]
        received = jnp.concatenate([received, lax.ppermute(received, "psg", pairs)], 0)
    stride = received.shape[0]
    received = [received] + [
        lax.ppermute(received, "psg", [(i, i ^ d) for i in range(sources)])
        for d in range(stride, sources, stride)
    ]
    norm, flip, own_raw = prepare_passages(passages, slices)
    soft, qn, score, many, target, ids, zw, inverse = forward(
        received, norm, cand_count, query_count, query_tokens
    )

    def swap(values, bit):
        return lax.ppermute(values, "psg", [(i, i ^ bit) for i in range(sources)])

    bit = 1
    while sources // bit > 4:
        zw = zw + swap(zw, bit)
        bit *= 2
    raised_sum, wanted_sum = attend(
        flip, soft, ids, score, many, target, inverse, query_tokens
    )
    zw, raised_sum = lax.optimization_barrier((zw, raised_sum))
    zw = [zw] + [swap(zw, d) for d in range(bit, sources, bit)]
    keep, send, grads = query_backward(
        zw, score, many, target, raised_sum, wanted_sum, sources
    )
    near = [(k, k ^ 1) for k in range(slices)]
    away = [(k, k ^ 2) for k in range(slices)]
    own, core, far, cross = passage_backward(
        ids, grads, qn, inverse, soft, pass_count, query_tokens, slices
    )
    cross = lax.ppermute(cross, "qry", near)
    far = (far.astype(jnp.float32) + cross.astype(jnp.float32)).astype(jnp.bfloat16)
    send, own = lax.optimization_barrier((send, own))
    ready = far
    far = lax.ppermute(far, "qry", away)
    core = lax.ppermute(core, "qry", near)
    bit = 1
    while bit < sources:
        send = lax.ppermute(send, "psg", [(i, i ^ bit) for i in range(sources)])
        if bit == 1:
            send, zw, ready = lax.optimization_barrier((send, zw, ready))
        bit *= 2
        if bit < sources:
            total = keep.astype(jnp.float32) + send.astype(jnp.float32)
            half = total.shape[0] // 2
            keep, send = total[:half], total[half:].astype(jnp.bfloat16)
    query_parts = [keep[0], send[0]]
    grad_queries, grad_passages = finish(
        queries.reshape(rows, width), own_raw, query_parts, [own, core, far], ready
    )

    raised = jnp.exp(teacher)
    raised_sum = jnp.sum(raised, -1, keepdims=True)
    log_target = teacher - jnp.log(raised_sum)
    known = jnp.sum(raised / raised_sum * log_target, -1)
    mine = lax.dynamic_slice_in_dim(
        sum(zw)[:2], lax.axis_index("psg") * query_count, query_count, 1
    )
    pair_loss = known - mine[1] + jnp.log(mine[0])
    return (pair_loss, grad_queries.reshape(queries.shape), grad_passages)


def solution(mesh):
    placed = (
        P(("psg", "qry"), None, None),
        P("psg", None, None),
        P(("psg", "qry"), None),
        P(("psg", "qry"), None),
    )
    return jax.shard_map(
        shards,
        mesh=mesh,
        in_specs=placed,
        out_specs=(P(("psg", "qry")), P(("psg", "qry"), None, None), P("psg", "qry", None)),
        check_vma=False,
    )
```

```python
import math

import jax
import jax.numpy as jnp
from jax import lax
from jax.experimental import pallas as pl
from jax.experimental.pallas import tpu as pltpu
from jax.sharding import PartitionSpec as P

epsilon = 1e-06
softness_scale = 0.05
chunk_pairs = 8
vmem_bytes = 20 << 20
row_pad = 8

VMEM = pl.BlockSpec(memory_space=pltpu.VMEM)
HBM = pl.BlockSpec(memory_space=pltpu.HBM)
chunk_unroll = 16
chunk_tail = 4
passage_unroll = 8
meta_rows = 8


def in_hbm(array):
    return pltpu.with_memory_space_constraint(array, pltpu.HBM)


def params():
    return pltpu.CompilerParams(vmem_limit_bytes=vmem_bytes)


def unit_rows(values):
    widened = values.astype(jnp.float32)
    inverse = lax.rsqrt(jnp.sum(widened * widened, -1, keepdims=True) + epsilon)
    return widened * inverse, inverse


def round_bf16(values):
    return values.astype(jnp.bfloat16).astype(jnp.float32)


def pack_kernel(pass_count, *refs):
    sources, targets, out_ref, sems = refs[:3], refs[4:7], refs[3], refs[7]
    copies = [
        pltpu.make_async_copy(source, target, sems.at[i])
        for i, (source, target) in enumerate(zip(sources, targets))
    ]
    for copy in copies:
        copy.start()
    for copy in copies:
        copy.wait()
    queries_ref, candidates_ref, teacher_ref = targets
    query_count, cand_count = teacher_ref.shape
    ids = candidates_ref[...].astype(jnp.float32)
    owner = jnp.floor((ids + 0.5) * (1.0 / pass_count))
    values = teacher_ref[...]
    high = round_bf16(values)
    middle = round_bf16(values - high)
    low = values - high - middle
    main = jnp.concatenate([owner, ids - owner * pass_count, high, middle], 1)
    blank = jnp.zeros((8 - query_count, 128), jnp.float32)
    low = jnp.concatenate([low, jnp.zeros((query_count, 128 - cand_count), jnp.float32)], 1)
    extra = jnp.concatenate([main, blank, low, blank], 0).astype(jnp.bfloat16)
    rows = queries_ref.shape[0]
    out_ref[:rows, :] = queries_ref[...]
    out_ref[rows:, :] = extra


def pack(queries, candidates, teacher, pass_count):
    rows, width = queries.shape
    return pl.pallas_call(
        lambda *refs: pack_kernel(pass_count, *refs),
        in_specs=[HBM] * 3,
        out_specs=VMEM,
        out_shape=jax.ShapeDtypeStruct((rows + 16, width), jnp.bfloat16),
        scratch_shapes=[
            pltpu.VMEM(queries.shape, queries.dtype),
            pltpu.VMEM(candidates.shape, candidates.dtype),
            pltpu.VMEM(teacher.shape, teacher.dtype),
            pltpu.SemaphoreType.DMA((3,)),
        ],
        compiler_params=params(),
        name="pack",
    )(in_hbm(queries), in_hbm(candidates), in_hbm(teacher))


def lane_ids(shape):
    return lax.broadcasted_iota(jnp.int32, shape, len(shape) - 1)


def tangent(raw, grad):
    unit, inverse = unit_rows(raw)
    return inverse * (grad - unit * jnp.sum(unit * grad, -1, keepdims=True))


def passages_kernel(
    slices, in_hbm_ref, norm_ref, flip_ref, own_ref, in_ref, in_sems
):
    total, tokens, _ = norm_ref.shape
    parts = in_sems.shape[0]
    count = total // parts
    share = tokens // slices
    me = lax.axis_index("qry")

    def in_copy(part):
        place = pl.ds(part * count, count)
        return pltpu.make_async_copy(in_hbm_ref.at[place], in_ref.at[place], in_sems.at[part])

    for part in range(parts):
        in_copy(part).start()
    for part in range(parts):
        in_copy(part).wait()
        for item in range(part * count, (part + 1) * count):
            for place in range(slices):
                start = pl.multiple_of((me ^ place) * share, share)
                raw = in_ref[item, pl.ds(start, share), :]
                if place == 0:
                    own_ref[item] = raw
                norm_ref[item, pl.ds(place * share, share), :] = unit_rows(raw)[0].astype(
                    jnp.bfloat16
                )
            flip_ref[item] = jnp.transpose(norm_ref[item], (1, 0))


def prepare_passages(passages, slices):
    count, tokens, width = passages.shape
    parts = math.gcd(count, 4)
    share = tokens // slices
    return pl.pallas_call(
        lambda *refs: passages_kernel(slices, *refs),
        in_specs=[HBM],
        out_specs=[VMEM] * 3,
        out_shape=[
            jax.ShapeDtypeStruct((count, tokens, width), jnp.bfloat16),
            jax.ShapeDtypeStruct((count, width, tokens), jnp.bfloat16),
            jax.ShapeDtypeStruct((count, share, width), jnp.bfloat16),
        ],
        scratch_shapes=[
            pltpu.VMEM((count, tokens, width), jnp.bfloat16),
            pltpu.SemaphoreType.DMA((parts,)),
        ],
        compiler_params=params(),
        cost_estimate=pl.CostEstimate(flops=1 << 24, bytes_accessed=6 << 20, transcendentals=0),
        name="prepare_passages",
    )(in_hbm(passages))


def list_layout(group):
    empty = -(-group // chunk_pairs) * chunk_pairs // 4
    return empty, empty + chunk_pairs // 4


def slot_total(pass_count, pairs):
    worst = (pairs + pass_count * (chunk_pairs - 1)) // chunk_pairs
    return -(-worst // chunk_tail) * chunk_tail


def list_ids(list_smem, row, p):
    words = [list_smem[row + w, p] for w in range(chunk_pairs // 4)]
    return [(words[r // 4] >> (8 * (r % 4))) & 255 for r in range(chunk_pairs)]


def each_chunk(list_smem, tables, visit):
    total = jnp.maximum(list_smem[tables + 4, 0], 1)
    full = total // chunk_unroll
    tail = (total - full * chunk_unroll + chunk_tail - 1) // chunk_tail

    def step(i, carry):
        visit(i * chunk_unroll, chunk_unroll)
        return carry

    def tail_step(i, carry):
        visit(full * chunk_unroll + i * chunk_tail, chunk_tail)
        return carry

    lax.fori_loop(0, full, step, 0)
    lax.fori_loop(0, tail, tail_step, 0)


def query_places(ids, query_tokens):
    return [pl.ds(pl.multiple_of(n * query_tokens, query_tokens), query_tokens) for n in ids]


def forward_kernel(
    cand_count,
    query_count,
    query_tokens,
    recv_refs,
    norm_ref,
    soft_ref,
    qn_ref,
    score_ref,
    many_ref,
    target_ref,
    list_ref,
    zw_ref,
    inverse_ref,
    ext_ref,
    low_ref,
    sums_ref,
    list_smem,
    sem,
):
    near = recv_refs[0].shape[0]
    sources = near * len(recv_refs)
    pass_count, tokens, width = norm_ref.shape
    group = sources * query_count
    rows = query_count * query_tokens
    stride = group + row_pad
    empty, tables = list_layout(group)
    me = lax.axis_index("psg")
    owner = me.astype(jnp.float32)
    for d in range(sources):
        recv_ref = recv_refs[d // near].at[d % near]
        source = me ^ d
        packed = recv_ref[rows : rows + 16, :].astype(jnp.float32)
        place = pl.ds(pl.multiple_of(source * query_count, query_count), query_count)
        ext_ref[place, :] = packed[:query_count]
        low_ref[place, :] = packed[8 : 8 + query_count]

    main = ext_ref[...]
    lanes = lane_ids(main.shape)
    lanes_float = lanes.astype(jnp.float32)
    live = lanes < cand_count
    local = pltpu.roll(main, 128 - cand_count, 1)
    logits = (
        pltpu.roll(main, 128 - 2 * cand_count, 1)
        + pltpu.roll(main, 128 - 3 * cand_count, 1)
        + low_ref[...]
    )
    raised = jnp.where(live, jnp.exp(logits), 0.0)
    target = raised / jnp.sum(raised, -1, keepdims=True)
    local = jnp.where(main == owner, local, -1.0)
    many = jnp.zeros(main.shape, jnp.float32)
    wanted = jnp.zeros(main.shape, jnp.float32)
    for c in range(cand_count):
        same = local[:, c : c + 1] == lanes_float
        many = many + jnp.where(same, 1.0, 0.0)
        wanted = wanted + jnp.where(same, target[:, c : c + 1], 0.0)
    many_ref[...] = many
    target_ref[...] = wanted
    active = many > 0.0
    lower = (
        lax.broadcasted_iota(jnp.int32, (group, group), 0)
        > lax.broadcasted_iota(jnp.int32, (group, group), 1)
    ).astype(jnp.bfloat16)
    active_value = jnp.where(active, 1.0, 0.0)
    rank = jnp.dot(lower, active_value.astype(jnp.bfloat16), preferred_element_type=jnp.float32)
    rank = jnp.where(active, rank, -1.0)
    less = lax.broadcasted_iota(jnp.int32, main.shape, 0).astype(jnp.float32) - group
    for w in range(empty):
        word = jnp.zeros((1, 128), jnp.int32)
        for b in range(4):
            found = jnp.sum(jnp.where(rank == 4 * w + b, less, 0.0), 0, keepdims=True) + group
            word = word | (found.astype(jnp.int32) << (8 * b))
        list_ref[w : w + 1, :] = word
    blank = jnp.full((tables - empty, 128), group, jnp.int32)
    list_ref[empty:tables, :] = blank | (blank << 8) | (blank << 16) | (blank << 24)
    square = (128, 128)
    first_id = lax.broadcasted_iota(jnp.int32, square, 0)
    second_id = lax.broadcasted_iota(jnp.int32, square, 1)
    counts = lax.dot_general(
        active_value.astype(jnp.bfloat16),
        jnp.ones((group, 128), jnp.bfloat16),
        (((0,), (0,)), ((), ())),
        preferred_element_type=jnp.float32,
    )
    chunks = jnp.floor((counts + (chunk_pairs - 1)) * (1.0 / chunk_pairs))
    more = jnp.maximum(chunks - 2.0, 0.0)
    lower_square = (first_id >= second_id).astype(jnp.bfloat16)
    ends = jnp.dot(lower_square, chunks.astype(jnp.bfloat16), preferred_element_type=jnp.float32)
    more_ends = jnp.dot(lower_square, more.astype(jnp.bfloat16), preferred_element_type=jnp.float32)
    chunk_id = lax.broadcasted_iota(jnp.int32, (1, 128), 1).astype(jnp.float32)

    def places_of(chunk_ends, chunk_counts):
        past = chunk_ends <= second_id.astype(jnp.float32)
        passage_of = jnp.sum(jnp.where(past, 1.0, 0.0), 0, keepdims=True)
        start_of = jnp.sum(jnp.where(past, chunk_counts, 0.0), 0, keepdims=True)
        return passage_of, chunk_id - start_of

    def last_row(values):
        return jnp.sum(jnp.where(first_id == 127, values, 0.0), 0, keepdims=True)

    passage_of, chunk_of = places_of(ends, chunks)
    more_passage, more_chunk = places_of(more_ends, more)
    beyond = passage_of > pass_count - 0.5
    rows_of = (
        jnp.where(beyond, 0.0, passage_of),
        jnp.where(beyond, float(empty), chunk_of * (chunk_pairs // 4)),
        jnp.sum(jnp.where(first_id == second_id, ends - chunks, 0.0), 0, keepdims=True),
        jnp.sum(active_value, 0, keepdims=True),
        last_row(ends),
        more_passage,
        more_chunk + 2.0,
        last_row(more_ends),
    )
    for row, value in enumerate(rows_of):
        list_ref[tables + row : tables + row + 1, :] = value.astype(jnp.int32)
    copy = pltpu.make_async_copy(list_ref, list_smem, sem)
    copy.start()
    for d in range(sources):
        recv_ref = recv_refs[d // near].at[d % near]
        place = pl.ds(pl.multiple_of((me ^ d) * rows, rows), rows)
        qn_ref[place, :] = unit_rows(recv_ref[:rows, :])[0].astype(jnp.bfloat16)
    qn_ref[sources * rows :, :] = jnp.zeros((query_tokens, width), jnp.bfloat16)
    copy.wait()

    def chunk(slot):
        p = list_smem[tables, slot]
        ids = list_ids(list_smem, list_smem[tables + 1, slot], p)
        tile = jnp.concatenate([qn_ref[place, :] for place in query_places(ids, query_tokens)], 0)
        dots = lax.dot_general(
            norm_ref[p], tile, (((1,), (1,)), ((), ())), preferred_element_type=jnp.float32
        )
        power = jnp.exp2(dots * (math.log2(math.e) / softness_scale))
        sums = jnp.sum(power, 0, keepdims=True)
        soft_ref[slot] = power.astype(jnp.bfloat16)
        inverse_ref[pl.ds(slot, 1), :] = 1.0 / sums
        for r, n in enumerate(ids):
            sums_ref[pl.ds(p * stride + n, 1), :query_tokens] = sums[
                :, r * query_tokens : (r + 1) * query_tokens
            ]

    def visit(first, count):
        for u in range(count):
            chunk(first + u)

    each_chunk(list_smem, tables, visit)

    scores = jnp.zeros(main.shape, jnp.float32)
    for p in range(pass_count):
        logs = jnp.log(sums_ref[p * stride : p * stride + group, :])
        value = softness_scale * jnp.sum(
            jnp.where(lanes < query_tokens, logs, 0.0), -1, keepdims=True
        )
        scores = jnp.where(lanes == p, value, scores)
    scores = jnp.where(active, scores, 0.0)
    score_ref[...] = scores
    mass = jnp.sum(many * jnp.exp(scores), -1, keepdims=True)
    agreed = jnp.sum(wanted * scores, -1, keepdims=True)
    same_id = lax.broadcasted_iota(jnp.int32, main.shape, 0) == lanes
    message = jnp.concatenate(
        [
            jnp.sum(jnp.where(same_id, value, 0.0), 0, keepdims=True) for value in (mass, agreed)
        ]
        + [jnp.zeros((6, 128), jnp.float32)],
        0,
    )
    zw_ref[...] = message


def forward(received, norm, cand_count, query_count, query_tokens):
    sources = received[0].shape[0] * len(received)
    pass_count, tokens, width = norm.shape
    group = sources * query_count
    capacity = max(2, -(-5 * query_count * cand_count // (2 * sources)))
    slots = slot_total(pass_count, sources * capacity)
    list_rows = -(-(list_layout(group)[1] + meta_rows) // 8) * 8
    rows = query_count * query_tokens
    soft_shape = (slots, tokens, chunk_pairs * query_tokens)
    flops = 2 * slots * chunk_pairs * query_tokens * tokens * width
    return pl.pallas_call(
        lambda *refs: forward_kernel(
            cand_count, query_count, query_tokens, refs[: len(received)], *refs[len(received) :]
        ),
        in_specs=[VMEM] * (len(received) + 1),
        out_specs=[VMEM] * 8,
        out_shape=[
            jax.ShapeDtypeStruct(soft_shape, jnp.bfloat16),
            jax.ShapeDtypeStruct((sources * rows + query_tokens, width), jnp.bfloat16),
            jax.ShapeDtypeStruct((group, 128), jnp.float32),
            jax.ShapeDtypeStruct((group, 128), jnp.float32),
            jax.ShapeDtypeStruct((group, 128), jnp.float32),
            jax.ShapeDtypeStruct((list_rows, 128), jnp.int32),
            jax.ShapeDtypeStruct((8, 128), jnp.float32),
            jax.ShapeDtypeStruct((slots, chunk_pairs * query_tokens), jnp.float32),
        ],
        scratch_shapes=[
            pltpu.VMEM((group, 128), jnp.float32),
            pltpu.VMEM((group, 128), jnp.float32),
            pltpu.VMEM((pass_count * (group + row_pad), 128), jnp.float32),
            pltpu.SMEM((list_rows, 128), jnp.int32),
            pltpu.SemaphoreType.DMA,
        ],
        compiler_params=params(),
        cost_estimate=pl.CostEstimate(flops=flops, bytes_accessed=12 << 20, transcendentals=1 << 22),
        name="forward",
    )(*received, norm)


def spread(ref, values, pass_count, stride, start=0):
    group = values.shape[0]
    for p in range(pass_count):
        ref[p * stride : p * stride + group, :] = jnp.broadcast_to(
            values[:, start + p : start + p + 1], (group, 128)
        )
        ref[p * stride + group : (p + 1) * stride, :] = jnp.zeros((stride - group, 128), jnp.float32)


def attend_kernel(
    query_tokens,
    flip_ref,
    soft_ref,
    list_ref,
    score_ref,
    many_ref,
    target_ref,
    inverse_ref,
    raised_ref,
    wanted_ref,
    raised_rows,
    wanted_rows,
    list_smem,
    sem,
):
    pass_count = flip_ref.shape[0]
    group = score_ref.shape[0]
    stride = group + row_pad
    list_copy = pltpu.make_async_copy(list_ref, list_smem, sem)
    list_copy.start()
    empty, tables = list_layout(group)

    spread(raised_rows, many_ref[...] * jnp.exp(score_ref[...]), pass_count, stride)
    spread(wanted_rows, target_ref[...], pass_count, stride)
    raised_ref[...] = jnp.zeros(raised_ref.shape, jnp.float32)
    wanted_ref[...] = jnp.zeros(wanted_ref.shape, jnp.float32)
    list_copy.wait()

    def chunk(slot):
        p = list_smem[tables, slot]
        ids = list_ids(list_smem, list_smem[tables + 1, slot], p)
        places = query_places(ids, query_tokens)
        mixed = jnp.dot(flip_ref[p], soft_ref[slot], preferred_element_type=jnp.float32)
        mixed = (mixed * inverse_ref[pl.ds(slot, 1), :]).astype(jnp.bfloat16)
        mixed = jnp.transpose(mixed, (1, 0)).astype(jnp.float32)
        for total, rows in ((raised_ref, raised_rows), (wanted_ref, wanted_rows)):
            added = [
                total[place, :]
                + mixed[r * query_tokens : (r + 1) * query_tokens]
                * rows[pl.ds(p * stride + ids[r], 1), :]
                for r, place in enumerate(places)
            ]
            for place, value in zip(places, added):
                total[place, :] = value

    def visit(first, count):
        for u in range(count):
            chunk(first + u)

    each_chunk(list_smem, tables, visit)


def attend(flip, soft, ids, score, many, target, inverse, query_tokens):
    slots, tokens, columns = soft.shape
    pass_count, width, _ = flip.shape
    group = score.shape[0]
    flops = 2 * slots * columns * tokens * width
    total = jax.ShapeDtypeStruct(((group + 1) * query_tokens, width), jnp.float32)
    rows = pltpu.VMEM((pass_count * (group + row_pad), 128), jnp.float32)
    return pl.pallas_call(
        lambda *refs: attend_kernel(query_tokens, *refs),
        in_specs=[VMEM] * 7,
        out_specs=[VMEM] * 2,
        out_shape=[total, total],
        scratch_shapes=[
            rows,
            rows,
            pltpu.SMEM(ids.shape, jnp.int32),
            pltpu.SemaphoreType.DMA,
        ],
        compiler_params=params(),
        cost_estimate=pl.CostEstimate(flops=flops, bytes_accessed=12 << 20, transcendentals=0),
        name="attend",
    )(flip, soft, ids, score, many, target, inverse)


def halving_order(count):
    order = [0]
    bit = count // 2
    while bit:
        order = order + [x | bit for x in order]
        bit //= 2
    return order


def query_kernel(
    query_tokens,
    sources,
    zw_refs,
    score_ref,
    many_ref,
    target_ref,
    raised_ref,
    wanted_ref,
    keep_ref,
    send_ref,
    grads_ref,
    scale_ref,
    query_ref,
):
    group = score_ref.shape[0]
    sums = sum(ref[...] for ref in zw_refs)
    lanes = lane_ids((group, 128))
    same_id = lax.broadcasted_iota(jnp.int32, (group, 128), 0) == lanes
    inverse = 1.0 / jnp.sum(jnp.where(same_id, sums[:1], 0.0), -1, keepdims=True)
    grads_ref[...] = many_ref[...] * jnp.exp(score_ref[...]) * inverse - target_ref[...]
    scale_ref[...] = jnp.broadcast_to(inverse, scale_ref.shape)
    for n in range(group):
        place = pl.ds(n * query_tokens, query_tokens)
        query_ref[place, :] = (
            raised_ref[place, :] * scale_ref[n : n + 1, :] - wanted_ref[place, :]
        ).astype(jnp.bfloat16)
    me = lax.axis_index("psg")
    rows = group // sources * query_tokens
    half = keep_ref.shape[0]
    for place, d in enumerate(halving_order(sources)):
        start = pl.multiple_of((me ^ d) * rows, rows)
        value = query_ref[pl.ds(start, rows), :]
        if place < half:
            keep_ref[place] = value
        else:
            send_ref[place - half] = value


def query_backward(zw, score, many, target, raised, wanted, sources):
    group = score.shape[0]
    width = raised.shape[1]
    rows = raised.shape[0] // (group + 1) * group
    part = jax.ShapeDtypeStruct((sources // 2, rows // sources, width), jnp.bfloat16)
    return pl.pallas_call(
        lambda *refs: query_kernel(
            rows // group, sources, refs[: len(zw)], *refs[len(zw) :]
        ),
        in_specs=[VMEM] * (len(zw) + 5),
        out_specs=[VMEM] * 3,
        out_shape=[part, part, jax.ShapeDtypeStruct((group, 128), jnp.float32)],
        scratch_shapes=[
            pltpu.VMEM((group, 128), jnp.float32),
            pltpu.VMEM((rows, width), jnp.bfloat16),
        ],
        compiler_params=params(),
        name="query_backward",
    )(*zw, score, many, target, raised, wanted)


def passage_kernel(
    query_tokens,
    list_ref,
    grads_ref,
    qn_ref,
    inverse_ref,
    soft_ref,
    own_ref,
    core_ref,
    far_ref,
    cross_ref,
    grad_ref,
    list_smem,
    sem,
):
    list_copy = pltpu.make_async_copy(list_ref, list_smem, sem)
    list_copy.start()
    pass_count, share, width = own_ref.shape
    group = grads_ref.shape[0]
    stride = group + row_pad
    empty, tables = list_layout(group)
    spread(grad_ref, grads_ref[...], pass_count, stride)
    list_copy.wait()

    def tile(p, row):
        ids = list_ids(list_smem, row, p)
        return [
            (qn_ref[place, :].astype(jnp.float32) * grad_ref[pl.ds(p * stride + n, 1), :]).astype(
                jnp.bfloat16
            )
            for n, place in zip(ids, query_places(ids, query_tokens))
        ]

    def weights(slot):
        value = soft_ref[slot]
        tokens, columns = value.shape
        scale = jnp.broadcast_to(inverse_ref[pl.ds(slot, 1), :], (16, columns)).astype(jnp.bfloat16)
        return (value.reshape(tokens // 16, 16, columns) * scale[None]).reshape(tokens, columns)

    outs = (own_ref, core_ref, far_ref, cross_ref)

    def passage(p):
        pairs = list_smem[tables + 3, p]
        slot = list_smem[tables + 2, p]
        tiles, softs = [], []
        for h in range(2):
            some = pairs > h * chunk_pairs
            tiles += tile(p, jnp.where(some, h * (chunk_pairs // 4), empty))
            softs.append(weights(jnp.where(some, slot + h, 0)))
        value = jnp.dot(
            jnp.concatenate(softs, 1),
            jnp.concatenate(tiles, 0),
            preferred_element_type=jnp.float32,
        ).astype(jnp.bfloat16)
        for place, ref in enumerate(outs):
            ref[p] = value[place * share : (place + 1) * share]

    def step(i, carry):
        for u in range(passage_unroll):
            passage(i * passage_unroll + u)
        return carry

    lax.fori_loop(0, pass_count // passage_unroll, step, 0)

    def rest(i, carry):
        p = list_smem[tables + 5, i]
        b = list_smem[tables + 6, i]
        value = jnp.dot(
            weights(list_smem[tables + 2, p] + b),
            jnp.concatenate(tile(p, b * (chunk_pairs // 4)), 0),
            preferred_element_type=jnp.float32,
        )
        for place, ref in enumerate(outs):
            piece = value[place * share : (place + 1) * share]
            ref[p] = (ref[p].astype(jnp.float32) + piece).astype(jnp.bfloat16)
        return carry

    lax.fori_loop(0, list_smem[tables + 7, 0], rest, 0)


def passage_backward(ids, grads, qn, inverse, soft, pass_count, query_tokens, slices):
    _, tokens, columns = soft.shape
    width = qn.shape[1]
    piece = jax.ShapeDtypeStruct((pass_count, tokens // slices, width), jnp.bfloat16)
    flops = 4 * pass_count * columns * tokens * width
    return pl.pallas_call(
        lambda *refs: passage_kernel(query_tokens, *refs),
        in_specs=[VMEM] * 5,
        out_specs=[VMEM] * 4,
        out_shape=[piece] * 4,
        scratch_shapes=[
            pltpu.VMEM((pass_count * (grads.shape[0] + row_pad), 128), jnp.float32),
            pltpu.SMEM(ids.shape, jnp.int32),
            pltpu.SemaphoreType.DMA,
        ],
        compiler_params=params(),
        cost_estimate=pl.CostEstimate(flops=flops, bytes_accessed=6 << 20, transcendentals=0),
        name="passage_backward",
    )(ids, grads, qn, inverse, soft)


def finish_kernel(query_parts, *refs):
    raw_query, raw_passage = refs[:2]
    query_out, passage_out = refs[-2:]
    queries, passages = refs[2 : 2 + query_parts], refs[2 + query_parts : -3]
    for raw, parts, out in ((raw_query, queries, query_out), (raw_passage, passages, passage_out)):
        grad = sum(ref[...].astype(jnp.float32) for ref in parts)
        out[...] = tangent(raw[...], grad).astype(jnp.bfloat16)


def finish(raw_query, raw_passage, query_parts, passage_parts, ready):
    count = 2 + len(query_parts) + len(passage_parts)
    return pl.pallas_call(
        lambda *refs: finish_kernel(len(query_parts), *refs),
        in_specs=[VMEM] * count + [pl.BlockSpec(memory_space=pl.ANY)],
        out_specs=[VMEM] * 2,
        out_shape=[
            jax.ShapeDtypeStruct(raw_query.shape, jnp.bfloat16),
            jax.ShapeDtypeStruct(raw_passage.shape, jnp.bfloat16),
        ],
        compiler_params=params(),
        name="finish",
    )(raw_query, raw_passage, *query_parts, *passage_parts, ready)


def shards(queries, passages, candidates, teacher):
    query_count, query_tokens, width = queries.shape
    pass_count = passages.shape[0]
    cand_count = candidates.shape[1]
    sources = lax.axis_size("psg")
    slices = lax.axis_size("qry")
    rows = query_count * query_tokens

    received = pack(queries.reshape(rows, width), candidates, teacher, pass_count)[None]
    while received.shape[0] * 4 < sources:
        bit = received.shape[0]
        pairs = [(i, i ^ bit) for i in range(sources)]
        received = jnp.concatenate([received, lax.ppermute(received, "psg", pairs)], 0)
    stride = received.shape[0]
    received = [received] + [
        lax.ppermute(received, "psg", [(i, i ^ d) for i in range(sources)])
        for d in range(stride, sources, stride)
    ]
    norm, flip, own_raw = prepare_passages(passages, slices)
    soft, qn, score, many, target, ids, zw, inverse = forward(
        received, norm, cand_count, query_count, query_tokens
    )

    def swap(values, bit):
        return lax.ppermute(values, "psg", [(i, i ^ bit) for i in range(sources)])

    bit = 1
    while sources // bit > 4:
        zw = zw + swap(zw, bit)
        bit *= 2
    raised_sum, wanted_sum = attend(
        flip, soft, ids, score, many, target, inverse, query_tokens
    )
    zw, raised_sum = lax.optimization_barrier((zw, raised_sum))
    zw = [zw] + [swap(zw, d) for d in range(bit, sources, bit)]
    keep, send, grads = query_backward(
        zw, score, many, target, raised_sum, wanted_sum, sources
    )
    near = [(k, k ^ 1) for k in range(slices)]
    away = [(k, k ^ 2) for k in range(slices)]
    own, core, far, cross = passage_backward(
        ids, grads, qn, inverse, soft, pass_count, query_tokens, slices
    )
    cross = lax.ppermute(cross, "qry", near)
    far = (far.astype(jnp.float32) + cross.astype(jnp.float32)).astype(jnp.bfloat16)
    send, own = lax.optimization_barrier((send, own))
    ready = far
    far = lax.ppermute(far, "qry", away)
    core = lax.ppermute(core, "qry", near)
    bit = 1
    while bit < sources:
        send = lax.ppermute(send, "psg", [(i, i ^ bit) for i in range(sources)])
        if bit == 1:
            send, zw, ready = lax.optimization_barrier((send, zw, ready))
        bit *= 2
        if bit < sources:
            total = keep.astype(jnp.float32) + send.astype(jnp.float32)
            half = total.shape[0] // 2
            keep, send = total[:half], total[half:].astype(jnp.bfloat16)
    query_parts = [keep[0], send[0]]
    grad_queries, grad_passages = finish(
        queries.reshape(rows, width), own_raw, query_parts, [own, core, far], ready
    )

    raised = jnp.exp(teacher)
    raised_sum = jnp.sum(raised, -1, keepdims=True)
    log_target = teacher - jnp.log(raised_sum)
    known = jnp.sum(raised / raised_sum * log_target, -1)
    mine = lax.dynamic_slice_in_dim(
        sum(zw)[:2], lax.axis_index("psg") * query_count, query_count, 1
    )
    pair_loss = known - mine[1] + jnp.log(mine[0])
    return (pair_loss, grad_queries.reshape(queries.shape), grad_passages)


def solution(mesh):
    placed = (
        P(("psg", "qry"), None, None),
        P("psg", None, None),
        P(("psg", "qry"), None),
        P(("psg", "qry"), None),
    )
    return jax.shard_map(
        shards,
        mesh=mesh,
        in_specs=placed,
        out_specs=(P(("psg", "qry")), P(("psg", "qry"), None, None), P("psg", "qry", None)),
        check_vma=False,
    )
```

```python
import math

import jax
import jax.numpy as jnp
from jax import lax
from jax.experimental import pallas as pl
from jax.experimental.pallas import tpu as pltpu
from jax.sharding import PartitionSpec as P

epsilon = 1e-06
softness_scale = 0.05
chunk_pairs = 8
vmem_bytes = 20 << 20
row_pad = 8

VMEM = pl.BlockSpec(memory_space=pltpu.VMEM)
HBM = pl.BlockSpec(memory_space=pltpu.HBM)
chunk_unroll = 16
chunk_tail = 4
passage_unroll = 8
meta_rows = 8


def in_hbm(array):
    return pltpu.with_memory_space_constraint(array, pltpu.HBM)


def params():
    return pltpu.CompilerParams(vmem_limit_bytes=vmem_bytes)


def unit_rows(values):
    widened = values.astype(jnp.float32)
    inverse = lax.rsqrt(jnp.sum(widened * widened, -1, keepdims=True) + epsilon)
    return widened * inverse, inverse


def round_bf16(values):
    return values.astype(jnp.bfloat16).astype(jnp.float32)


def pack_kernel(pass_count, *refs):
    sources, targets, out_ref, sems = refs[:3], refs[4:7], refs[3], refs[7]
    copies = [
        pltpu.make_async_copy(source, target, sems.at[i])
        for i, (source, target) in enumerate(zip(sources, targets))
    ]
    for copy in copies:
        copy.start()
    for copy in copies:
        copy.wait()
    queries_ref, candidates_ref, teacher_ref = targets
    query_count, cand_count = teacher_ref.shape
    ids = candidates_ref[...].astype(jnp.float32)
    owner = jnp.floor((ids + 0.5) * (1.0 / pass_count))
    values = teacher_ref[...]
    high = round_bf16(values)
    middle = round_bf16(values - high)
    low = values - high - middle
    main = jnp.concatenate([owner, ids - owner * pass_count, high, middle], 1)
    blank = jnp.zeros((8 - query_count, 128), jnp.float32)
    low = jnp.concatenate([low, jnp.zeros((query_count, 128 - cand_count), jnp.float32)], 1)
    extra = jnp.concatenate([main, blank, low, blank], 0).astype(jnp.bfloat16)
    rows = queries_ref.shape[0]
    out_ref[:rows, :] = queries_ref[...]
    out_ref[rows:, :] = extra


def pack(queries, candidates, teacher, pass_count):
    rows, width = queries.shape
    return pl.pallas_call(
        lambda *refs: pack_kernel(pass_count, *refs),
        in_specs=[HBM] * 3,
        out_specs=VMEM,
        out_shape=jax.ShapeDtypeStruct((rows + 16, width), jnp.bfloat16),
        scratch_shapes=[
            pltpu.VMEM(queries.shape, queries.dtype),
            pltpu.VMEM(candidates.shape, candidates.dtype),
            pltpu.VMEM(teacher.shape, teacher.dtype),
            pltpu.SemaphoreType.DMA((3,)),
        ],
        compiler_params=params(),
        name="pack",
    )(in_hbm(queries), in_hbm(candidates), in_hbm(teacher))


def lane_ids(shape):
    return lax.broadcasted_iota(jnp.int32, shape, len(shape) - 1)


def tangent(raw, grad):
    unit, inverse = unit_rows(raw)
    return inverse * (grad - unit * jnp.sum(unit * grad, -1, keepdims=True))


def passages_kernel(
    slices, in_hbm_ref, norm_ref, flip_ref, own_ref, in_ref, in_sems
):
    total, tokens, _ = norm_ref.shape
    parts = in_sems.shape[0]
    count = total // parts
    share = tokens // slices
    me = lax.axis_index("qry")

    def in_copy(part):
        place = pl.ds(part * count, count)
        return pltpu.make_async_copy(in_hbm_ref.at[place], in_ref.at[place], in_sems.at[part])

    for part in range(parts):
        in_copy(part).start()
    for part in range(parts):
        in_copy(part).wait()
        for item in range(part * count, (part + 1) * count):
            for place in range(slices):
                start = pl.multiple_of((me ^ place) * share, share)
                raw = in_ref[item, pl.ds(start, share), :]
                if place == 0:
                    own_ref[item] = raw
                norm_ref[item, pl.ds(place * share, share), :] = unit_rows(raw)[0].astype(
                    jnp.bfloat16
                )
            flip_ref[item] = jnp.transpose(norm_ref[item], (1, 0))


def prepare_passages(passages, slices):
    count, tokens, width = passages.shape
    parts = math.gcd(count, 4)
    share = tokens // slices
    return pl.pallas_call(
        lambda *refs: passages_kernel(slices, *refs),
        in_specs=[HBM],
        out_specs=[VMEM] * 3,
        out_shape=[
            jax.ShapeDtypeStruct((count, tokens, width), jnp.bfloat16),
            jax.ShapeDtypeStruct((count, width, tokens), jnp.bfloat16),
            jax.ShapeDtypeStruct((count, share, width), jnp.bfloat16),
        ],
        scratch_shapes=[
            pltpu.VMEM((count, tokens, width), jnp.bfloat16),
            pltpu.SemaphoreType.DMA((parts,)),
        ],
        compiler_params=params(),
        cost_estimate=pl.CostEstimate(flops=1 << 24, bytes_accessed=6 << 20, transcendentals=0),
        name="prepare_passages",
    )(in_hbm(passages))


def list_layout(group):
    empty = -(-group // chunk_pairs) * chunk_pairs // 4
    return empty, empty + chunk_pairs // 4


def slot_total(pass_count, pairs):
    worst = (pairs + pass_count * (chunk_pairs - 1)) // chunk_pairs
    return -(-worst // chunk_tail) * chunk_tail


def list_ids(list_smem, row, p):
    words = [list_smem[row + w, p] for w in range(chunk_pairs // 4)]
    return [(words[r // 4] >> (8 * (r % 4))) & 255 for r in range(chunk_pairs)]


def each_chunk(list_smem, tables, visit):
    total = jnp.maximum(list_smem[tables + 4, 0], 1)
    full = total // chunk_unroll
    tail = (total - full * chunk_unroll + chunk_tail - 1) // chunk_tail

    def step(i, carry):
        visit(i * chunk_unroll, chunk_unroll)
        return carry

    def tail_step(i, carry):
        visit(full * chunk_unroll + i * chunk_tail, chunk_tail)
        return carry

    lax.fori_loop(0, full, step, 0)
    lax.fori_loop(0, tail, tail_step, 0)


def query_places(ids, query_tokens):
    return [pl.ds(pl.multiple_of(n * query_tokens, query_tokens), query_tokens) for n in ids]


def forward_kernel(
    cand_count,
    query_count,
    query_tokens,
    recv_refs,
    norm_ref,
    soft_ref,
    qn_ref,
    score_ref,
    many_ref,
    target_ref,
    list_ref,
    zw_ref,
    inverse_ref,
    ext_ref,
    low_ref,
    sums_ref,
    list_smem,
    sem,
):
    near = recv_refs[0].shape[0]
    sources = near * len(recv_refs)
    pass_count, tokens, width = norm_ref.shape
    group = sources * query_count
    rows = query_count * query_tokens
    stride = group + row_pad
    empty, tables = list_layout(group)
    me = lax.axis_index("psg")
    owner = me.astype(jnp.float32)
    for d in range(sources):
        recv_ref = recv_refs[d // near].at[d % near]
        source = me ^ d
        packed = recv_ref[rows : rows + 16, :].astype(jnp.float32)
        place = pl.ds(pl.multiple_of(source * query_count, query_count), query_count)
        ext_ref[place, :] = packed[:query_count]
        low_ref[place, :] = packed[8 : 8 + query_count]

    main = ext_ref[...]
    lanes = lane_ids(main.shape)
    lanes_float = lanes.astype(jnp.float32)
    live = lanes < cand_count
    local = pltpu.roll(main, 128 - cand_count, 1)
    logits = (
        pltpu.roll(main, 128 - 2 * cand_count, 1)
        + pltpu.roll(main, 128 - 3 * cand_count, 1)
        + low_ref[...]
    )
    raised = jnp.where(live, jnp.exp(logits), 0.0)
    target = raised / jnp.sum(raised, -1, keepdims=True)
    local = jnp.where(main == owner, local, -1.0)
    many = jnp.zeros(main.shape, jnp.float32)
    wanted = jnp.zeros(main.shape, jnp.float32)
    for c in range(cand_count):
        same = local[:, c : c + 1] == lanes_float
        many = many + jnp.where(same, 1.0, 0.0)
        wanted = wanted + jnp.where(same, target[:, c : c + 1], 0.0)
    many_ref[...] = many
    target_ref[...] = wanted
    active = many > 0.0
    lower = (
        lax.broadcasted_iota(jnp.int32, (group, group), 0)
        > lax.broadcasted_iota(jnp.int32, (group, group), 1)
    ).astype(jnp.bfloat16)
    active_value = jnp.where(active, 1.0, 0.0)
    rank = jnp.dot(lower, active_value.astype(jnp.bfloat16), preferred_element_type=jnp.float32)
    rank = jnp.where(active, rank, -1.0)
    less = lax.broadcasted_iota(jnp.int32, main.shape, 0).astype(jnp.float32) - group
    for w in range(empty):
        word = jnp.zeros((1, 128), jnp.int32)
        for b in range(4):
            found = jnp.sum(jnp.where(rank == 4 * w + b, less, 0.0), 0, keepdims=True) + group
            word = word | (found.astype(jnp.int32) << (8 * b))
        list_ref[w : w + 1, :] = word
    blank = jnp.full((tables - empty, 128), group, jnp.int32)
    list_ref[empty:tables, :] = blank | (blank << 8) | (blank << 16) | (blank << 24)
    square = (128, 128)
    first_id = lax.broadcasted_iota(jnp.int32, square, 0)
    second_id = lax.broadcasted_iota(jnp.int32, square, 1)
    counts = lax.dot_general(
        active_value.astype(jnp.bfloat16),
        jnp.ones((group, 128), jnp.bfloat16),
        (((0,), (0,)), ((), ())),
        preferred_element_type=jnp.float32,
    )
    chunks = jnp.floor((counts + (chunk_pairs - 1)) * (1.0 / chunk_pairs))
    more = jnp.maximum(chunks - 2.0, 0.0)
    lower_square = (first_id >= second_id).astype(jnp.bfloat16)
    ends = jnp.dot(lower_square, chunks.astype(jnp.bfloat16), preferred_element_type=jnp.float32)
    more_ends = jnp.dot(lower_square, more.astype(jnp.bfloat16), preferred_element_type=jnp.float32)
    chunk_id = lax.broadcasted_iota(jnp.int32, (1, 128), 1).astype(jnp.float32)

    def places_of(chunk_ends, chunk_counts):
        past = chunk_ends <= second_id.astype(jnp.float32)
        passage_of = jnp.sum(jnp.where(past, 1.0, 0.0), 0, keepdims=True)
        start_of = jnp.sum(jnp.where(past, chunk_counts, 0.0), 0, keepdims=True)
        return passage_of, chunk_id - start_of

    def last_row(values):
        return jnp.sum(jnp.where(first_id == 127, values, 0.0), 0, keepdims=True)

    passage_of, chunk_of = places_of(ends, chunks)
    more_passage, more_chunk = places_of(more_ends, more)
    beyond = passage_of > pass_count - 0.5
    rows_of = (
        jnp.where(beyond, 0.0, passage_of),
        jnp.where(beyond, float(empty), chunk_of * (chunk_pairs // 4)),
        jnp.sum(jnp.where(first_id == second_id, ends - chunks, 0.0), 0, keepdims=True),
        jnp.sum(active_value, 0, keepdims=True),
        last_row(ends),
        more_passage,
        more_chunk + 2.0,
        last_row(more_ends),
    )
    for row, value in enumerate(rows_of):
        list_ref[tables + row : tables + row + 1, :] = value.astype(jnp.int32)
    copy = pltpu.make_async_copy(list_ref, list_smem, sem)
    copy.start()
    for d in range(sources):
        recv_ref = recv_refs[d // near].at[d % near]
        place = pl.ds(pl.multiple_of((me ^ d) * rows, rows), rows)
        qn_ref[place, :] = unit_rows(recv_ref[:rows, :])[0].astype(jnp.bfloat16)
    qn_ref[sources * rows :, :] = jnp.zeros((query_tokens, width), jnp.bfloat16)
    copy.wait()

    def chunk(slot):
        p = list_smem[tables, slot]
        ids = list_ids(list_smem, list_smem[tables + 1, slot], p)
        tile = jnp.concatenate([qn_ref[place, :] for place in query_places(ids, query_tokens)], 0)
        dots = lax.dot_general(
            norm_ref[p], tile, (((1,), (1,)), ((), ())), preferred_element_type=jnp.float32
        )
        power = jnp.exp2(dots * (math.log2(math.e) / softness_scale))
        sums = jnp.sum(power, 0, keepdims=True)
        soft_ref[slot] = power.astype(jnp.bfloat16)
        inverse_ref[pl.ds(slot, 1), :] = 1.0 / sums
        for r, n in enumerate(ids):
            sums_ref[pl.ds(p * stride + n, 1), :query_tokens] = sums[
                :, r * query_tokens : (r + 1) * query_tokens
            ]

    def visit(first, count):
        for u in range(count):
            chunk(first + u)

    each_chunk(list_smem, tables, visit)

    scores = jnp.zeros(main.shape, jnp.float32)
    for p in range(pass_count):
        logs = jnp.log(sums_ref[p * stride : p * stride + group, :])
        value = softness_scale * jnp.sum(
            jnp.where(lanes < query_tokens, logs, 0.0), -1, keepdims=True
        )
        scores = jnp.where(lanes == p, value, scores)
    scores = jnp.where(active, scores, 0.0)
    score_ref[...] = scores
    mass = jnp.sum(many * jnp.exp(scores), -1, keepdims=True)
    agreed = jnp.sum(wanted * scores, -1, keepdims=True)
    same_id = lax.broadcasted_iota(jnp.int32, main.shape, 0) == lanes
    message = jnp.concatenate(
        [
            jnp.sum(jnp.where(same_id, value, 0.0), 0, keepdims=True) for value in (mass, agreed)
        ]
        + [jnp.zeros((6, 128), jnp.float32)],
        0,
    )
    zw_ref[...] = message


def forward(received, norm, cand_count, query_count, query_tokens):
    sources = received[0].shape[0] * len(received)
    pass_count, tokens, width = norm.shape
    group = sources * query_count
    capacity = max(2, -(-5 * query_count * cand_count // (2 * sources)))
    slots = slot_total(pass_count, sources * capacity)
    list_rows = -(-(list_layout(group)[1] + meta_rows) // 8) * 8
    rows = query_count * query_tokens
    soft_shape = (slots, tokens, chunk_pairs * query_tokens)
    flops = 2 * slots * chunk_pairs * query_tokens * tokens * width
    return pl.pallas_call(
        lambda *refs: forward_kernel(
            cand_count, query_count, query_tokens, refs[: len(received)], *refs[len(received) :]
        ),
        in_specs=[VMEM] * (len(received) + 1),
        out_specs=[VMEM] * 8,
        out_shape=[
            jax.ShapeDtypeStruct(soft_shape, jnp.bfloat16),
            jax.ShapeDtypeStruct((sources * rows + query_tokens, width), jnp.bfloat16),
            jax.ShapeDtypeStruct((group, 128), jnp.float32),
            jax.ShapeDtypeStruct((group, 128), jnp.float32),
            jax.ShapeDtypeStruct((group, 128), jnp.float32),
            jax.ShapeDtypeStruct((list_rows, 128), jnp.int32),
            jax.ShapeDtypeStruct((8, 128), jnp.float32),
            jax.ShapeDtypeStruct((slots, chunk_pairs * query_tokens), jnp.float32),
        ],
        scratch_shapes=[
            pltpu.VMEM((group, 128), jnp.float32),
            pltpu.VMEM((group, 128), jnp.float32),
            pltpu.VMEM((pass_count * (group + row_pad), 128), jnp.float32),
            pltpu.SMEM((list_rows, 128), jnp.int32),
            pltpu.SemaphoreType.DMA,
        ],
        compiler_params=params(),
        cost_estimate=pl.CostEstimate(flops=flops, bytes_accessed=12 << 20, transcendentals=1 << 22),
        name="forward",
    )(*received, norm)


def spread(ref, values, pass_count, stride, start=0):
    group = values.shape[0]
    for p in range(pass_count):
        ref[p * stride : p * stride + group, :] = jnp.broadcast_to(
            values[:, start + p : start + p + 1], (group, 128)
        )
        ref[p * stride + group : (p + 1) * stride, :] = jnp.zeros((stride - group, 128), jnp.float32)


def attend_kernel(
    query_tokens,
    flip_ref,
    soft_ref,
    list_ref,
    score_ref,
    many_ref,
    target_ref,
    inverse_ref,
    raised_ref,
    wanted_ref,
    raised_rows,
    wanted_rows,
    list_smem,
    sem,
):
    pass_count = flip_ref.shape[0]
    group = score_ref.shape[0]
    stride = group + row_pad
    list_copy = pltpu.make_async_copy(list_ref, list_smem, sem)
    list_copy.start()
    empty, tables = list_layout(group)

    spread(raised_rows, many_ref[...] * jnp.exp(score_ref[...]), pass_count, stride)
    spread(wanted_rows, target_ref[...], pass_count, stride)
    raised_ref[...] = jnp.zeros(raised_ref.shape, jnp.float32)
    wanted_ref[...] = jnp.zeros(wanted_ref.shape, jnp.float32)
    list_copy.wait()

    def chunk(slot):
        p = list_smem[tables, slot]
        ids = list_ids(list_smem, list_smem[tables + 1, slot], p)
        places = query_places(ids, query_tokens)
        mixed = jnp.dot(flip_ref[p], soft_ref[slot], preferred_element_type=jnp.float32)
        mixed = (mixed * inverse_ref[pl.ds(slot, 1), :]).astype(jnp.bfloat16)
        mixed = jnp.transpose(mixed, (1, 0)).astype(jnp.float32)
        for total, rows in ((raised_ref, raised_rows), (wanted_ref, wanted_rows)):
            added = [
                total[place, :]
                + mixed[r * query_tokens : (r + 1) * query_tokens]
                * rows[pl.ds(p * stride + ids[r], 1), :]
                for r, place in enumerate(places)
            ]
            for place, value in zip(places, added):
                total[place, :] = value

    def visit(first, count):
        for u in range(count):
            chunk(first + u)

    each_chunk(list_smem, tables, visit)


def attend(flip, soft, ids, score, many, target, inverse, query_tokens):
    slots, tokens, columns = soft.shape
    pass_count, width, _ = flip.shape
    group = score.shape[0]
    flops = 2 * slots * columns * tokens * width
    total = jax.ShapeDtypeStruct(((group + 1) * query_tokens, width), jnp.float32)
    rows = pltpu.VMEM((pass_count * (group + row_pad), 128), jnp.float32)
    return pl.pallas_call(
        lambda *refs: attend_kernel(query_tokens, *refs),
        in_specs=[VMEM] * 7,
        out_specs=[VMEM] * 2,
        out_shape=[total, total],
        scratch_shapes=[
            rows,
            rows,
            pltpu.SMEM(ids.shape, jnp.int32),
            pltpu.SemaphoreType.DMA,
        ],
        compiler_params=params(),
        cost_estimate=pl.CostEstimate(flops=flops, bytes_accessed=12 << 20, transcendentals=0),
        name="attend",
    )(flip, soft, ids, score, many, target, inverse)


def halving_order(count):
    order = [0]
    bit = count // 2
    while bit:
        order = order + [x | bit for x in order]
        bit //= 2
    return order


def query_kernel(
    query_tokens,
    sources,
    zw_refs,
    score_ref,
    many_ref,
    target_ref,
    raised_ref,
    wanted_ref,
    keep_ref,
    send_ref,
    grads_ref,
    scale_ref,
    query_ref,
):
    group = score_ref.shape[0]
    sums = sum(ref[...] for ref in zw_refs)
    lanes = lane_ids((group, 128))
    same_id = lax.broadcasted_iota(jnp.int32, (group, 128), 0) == lanes
    inverse = 1.0 / jnp.sum(jnp.where(same_id, sums[:1], 0.0), -1, keepdims=True)
    grads_ref[...] = many_ref[...] * jnp.exp(score_ref[...]) * inverse - target_ref[...]
    scale_ref[...] = jnp.broadcast_to(inverse, scale_ref.shape)
    for n in range(group):
        place = pl.ds(n * query_tokens, query_tokens)
        query_ref[place, :] = (
            raised_ref[place, :] * scale_ref[n : n + 1, :] - wanted_ref[place, :]
        ).astype(jnp.bfloat16)
    me = lax.axis_index("psg")
    rows = group // sources * query_tokens
    half = keep_ref.shape[0]
    for place, d in enumerate(halving_order(sources)):
        start = pl.multiple_of((me ^ d) * rows, rows)
        value = query_ref[pl.ds(start, rows), :]
        if place < half:
            keep_ref[place] = value
        else:
            send_ref[place - half] = value


def query_backward(zw, score, many, target, raised, wanted, sources):
    group = score.shape[0]
    width = raised.shape[1]
    rows = raised.shape[0] // (group + 1) * group
    part = jax.ShapeDtypeStruct((sources // 2, rows // sources, width), jnp.bfloat16)
    return pl.pallas_call(
        lambda *refs: query_kernel(
            rows // group, sources, refs[: len(zw)], *refs[len(zw) :]
        ),
        in_specs=[VMEM] * (len(zw) + 5),
        out_specs=[VMEM] * 3,
        out_shape=[part, part, jax.ShapeDtypeStruct((group, 128), jnp.float32)],
        scratch_shapes=[
            pltpu.VMEM((group, 128), jnp.float32),
            pltpu.VMEM((rows, width), jnp.bfloat16),
        ],
        compiler_params=params(),
        name="query_backward",
    )(*zw, score, many, target, raised, wanted)


def passage_kernel(
    query_tokens,
    list_ref,
    grads_ref,
    qn_ref,
    inverse_ref,
    soft_ref,
    own_ref,
    core_ref,
    far_ref,
    cross_ref,
    grad_ref,
    list_smem,
    sem,
):
    list_copy = pltpu.make_async_copy(list_ref, list_smem, sem)
    list_copy.start()
    pass_count, share, width = own_ref.shape
    group = grads_ref.shape[0]
    stride = group + row_pad
    empty, tables = list_layout(group)
    spread(grad_ref, grads_ref[...], pass_count, stride)
    list_copy.wait()

    def tile(p, row):
        ids = list_ids(list_smem, row, p)
        return [
            (qn_ref[place, :].astype(jnp.float32) * grad_ref[pl.ds(p * stride + n, 1), :]).astype(
                jnp.bfloat16
            )
            for n, place in zip(ids, query_places(ids, query_tokens))
        ]

    def weights(slot):
        value = soft_ref[slot]
        tokens, columns = value.shape
        scale = jnp.broadcast_to(inverse_ref[pl.ds(slot, 1), :], (16, columns)).astype(jnp.bfloat16)
        return (value.reshape(tokens // 16, 16, columns) * scale[None]).reshape(tokens, columns)

    outs = (own_ref, core_ref, far_ref, cross_ref)

    def passage(p):
        pairs = list_smem[tables + 3, p]
        slot = list_smem[tables + 2, p]
        tiles, softs = [], []
        for h in range(2):
            some = pairs > h * chunk_pairs
            tiles += tile(p, jnp.where(some, h * (chunk_pairs // 4), empty))
            softs.append(weights(jnp.where(some, slot + h, 0)))
        value = jnp.dot(
            jnp.concatenate(softs, 1),
            jnp.concatenate(tiles, 0),
            preferred_element_type=jnp.float32,
        ).astype(jnp.bfloat16)
        for place, ref in enumerate(outs):
            ref[p] = value[place * share : (place + 1) * share]

    def step(i, carry):
        for u in range(passage_unroll):
            passage(i * passage_unroll + u)
        return carry

    lax.fori_loop(0, pass_count // passage_unroll, step, 0)

    def rest(i, carry):
        p = list_smem[tables + 5, i]
        b = list_smem[tables + 6, i]
        value = jnp.dot(
            weights(list_smem[tables + 2, p] + b),
            jnp.concatenate(tile(p, b * (chunk_pairs // 4)), 0),
            preferred_element_type=jnp.float32,
        )
        for place, ref in enumerate(outs):
            piece = value[place * share : (place + 1) * share]
            ref[p] = (ref[p].astype(jnp.float32) + piece).astype(jnp.bfloat16)
        return carry

    lax.fori_loop(0, list_smem[tables + 7, 0], rest, 0)


def passage_backward(ids, grads, qn, inverse, soft, pass_count, query_tokens, slices):
    _, tokens, columns = soft.shape
    width = qn.shape[1]
    piece = jax.ShapeDtypeStruct((pass_count, tokens // slices, width), jnp.bfloat16)
    flops = 4 * pass_count * columns * tokens * width
    return pl.pallas_call(
        lambda *refs: passage_kernel(query_tokens, *refs),
        in_specs=[VMEM] * 5,
        out_specs=[VMEM] * 4,
        out_shape=[piece] * 4,
        scratch_shapes=[
            pltpu.VMEM((pass_count * (grads.shape[0] + row_pad), 128), jnp.float32),
            pltpu.SMEM(ids.shape, jnp.int32),
            pltpu.SemaphoreType.DMA,
        ],
        compiler_params=params(),
        cost_estimate=pl.CostEstimate(flops=flops, bytes_accessed=6 << 20, transcendentals=0),
        name="passage_backward",
    )(ids, grads, qn, inverse, soft)


def add_parts(refs, place=slice(None)):
    return sum(ref[place].astype(jnp.float32) for ref in refs)


def finish_first_kernel(raw_ref, own_ref, core_ref, far_ref, out_ref):
    place = pl.ds(0, far_ref.shape[0])
    grad = add_parts((own_ref, core_ref), place) + add_parts((far_ref,))
    out_ref[...] = tangent(raw_ref[place], grad).astype(jnp.bfloat16)


def finish_last_kernel(raw_ref, own_ref, core_ref, far_ref, raw_query, *refs):
    parts, (query_out, out_ref) = refs[:-4], refs[-2:]
    query_out[...] = tangent(raw_query[...], add_parts(parts)).astype(jnp.bfloat16)
    count = far_ref.shape[0]
    place = pl.ds(count, count)
    grad = add_parts((own_ref, core_ref), place) + add_parts((far_ref,))
    out_ref[...] = tangent(raw_ref[place], grad).astype(jnp.bfloat16)


def finish_first(raw, own, core, far):
    return pl.pallas_call(
        finish_first_kernel,
        grid=(1,),
        in_specs=[VMEM] * 4,
        out_specs=pl.BlockSpec(far.shape, lambda i: (0, 0, 0)),
        out_shape=jax.ShapeDtypeStruct(raw.shape, jnp.bfloat16),
        compiler_params=params(),
        name="finish_first",
    )(raw, own, core, far)


def finish_last(raw, own, core, far, raw_query, query_parts, ready, before):
    count = 5 + len(query_parts)
    return pl.pallas_call(
        finish_last_kernel,
        grid=(1,),
        in_specs=[VMEM] * count + [pl.BlockSpec(memory_space=pl.ANY)] * 2,
        out_specs=[
            pl.BlockSpec(raw_query.shape, lambda i: (0, 0)),
            pl.BlockSpec(far.shape, lambda i: (1, 0, 0)),
        ],
        out_shape=[
            jax.ShapeDtypeStruct(raw_query.shape, jnp.bfloat16),
            jax.ShapeDtypeStruct(raw.shape, jnp.bfloat16),
        ],
        input_output_aliases={count + 1: 1},
        compiler_params=params(),
        name="finish_last",
    )(raw, own, core, far, raw_query, *query_parts, ready, before)


def shards(queries, passages, candidates, teacher):
    query_count, query_tokens, width = queries.shape
    pass_count = passages.shape[0]
    cand_count = candidates.shape[1]
    sources = lax.axis_size("psg")
    slices = lax.axis_size("qry")
    rows = query_count * query_tokens

    received = pack(queries.reshape(rows, width), candidates, teacher, pass_count)[None]
    while received.shape[0] * 4 < sources:
        bit = received.shape[0]
        pairs = [(i, i ^ bit) for i in range(sources)]
        received = jnp.concatenate([received, lax.ppermute(received, "psg", pairs)], 0)
    stride = received.shape[0]
    received = [received] + [
        lax.ppermute(received, "psg", [(i, i ^ d) for i in range(sources)])
        for d in range(stride, sources, stride)
    ]
    norm, flip, own_raw = prepare_passages(passages, slices)
    soft, qn, score, many, target, ids, zw, inverse = forward(
        received, norm, cand_count, query_count, query_tokens
    )

    def swap(values, bit):
        return lax.ppermute(values, "psg", [(i, i ^ bit) for i in range(sources)])

    bit = 1
    while sources // bit > 4:
        zw = zw + swap(zw, bit)
        bit *= 2
    raised_sum, wanted_sum = attend(
        flip, soft, ids, score, many, target, inverse, query_tokens
    )
    zw, raised_sum = lax.optimization_barrier((zw, raised_sum))
    zw = [zw] + [swap(zw, d) for d in range(bit, sources, bit)]
    keep, send, grads = query_backward(
        zw, score, many, target, raised_sum, wanted_sum, sources
    )
    near = [(k, k ^ 1) for k in range(slices)]
    away = [(k, k ^ 2) for k in range(slices)]
    own, core, far, cross = passage_backward(
        ids, grads, qn, inverse, soft, pass_count, query_tokens, slices
    )
    cross = lax.ppermute(cross, "qry", near)
    half = pass_count // 2
    far = [
        (far[part].astype(jnp.float32) + cross[part].astype(jnp.float32)).astype(jnp.bfloat16)
        for part in (slice(0, half), slice(half, pass_count))
    ]
    send, own = lax.optimization_barrier((send, own))
    ready = far[1]
    far = [lax.ppermute(piece, "qry", away) for piece in far]
    core = lax.ppermute(core, "qry", near)
    bit = 1
    while bit < sources:
        send = lax.ppermute(send, "psg", [(i, i ^ bit) for i in range(sources)])
        if bit == 1:
            send, zw, ready = lax.optimization_barrier((send, zw, ready))
        bit *= 2
        if bit < sources:
            total = keep.astype(jnp.float32) + send.astype(jnp.float32)
            half = total.shape[0] // 2
            keep, send = total[:half], total[half:].astype(jnp.bfloat16)
    query_parts = [keep[0], send[0]]
    grad_passages = finish_first(own_raw, own, core, far[0])
    grad_queries, grad_passages = finish_last(
        own_raw,
        own,
        core,
        far[1],
        queries.reshape(rows, width),
        query_parts,
        ready,
        grad_passages,
    )

    raised = jnp.exp(teacher)
    raised_sum = jnp.sum(raised, -1, keepdims=True)
    log_target = teacher - jnp.log(raised_sum)
    known = jnp.sum(raised / raised_sum * log_target, -1)
    mine = lax.dynamic_slice_in_dim(
        sum(zw)[:2], lax.axis_index("psg") * query_count, query_count, 1
    )
    pair_loss = known - mine[1] + jnp.log(mine[0])
    return (pair_loss, grad_queries.reshape(queries.shape), grad_passages)


def solution(mesh):
    placed = (
        P(("psg", "qry"), None, None),
        P("psg", None, None),
        P(("psg", "qry"), None),
        P(("psg", "qry"), None),
    )
    return jax.shard_map(
        shards,
        mesh=mesh,
        in_specs=placed,
        out_specs=(P(("psg", "qry")), P(("psg", "qry"), None, None), P("psg", "qry", None)),
        check_vma=False,
    )
```

```python
import math

import jax
import jax.numpy as jnp
from jax import lax
from jax.experimental import pallas as pl
from jax.experimental.pallas import tpu as pltpu
from jax.sharding import PartitionSpec as P

epsilon = 1e-06
softness_scale = 0.05
chunk_pairs = 8
vmem_bytes = 20 << 20
row_pad = 8

VMEM = pl.BlockSpec(memory_space=pltpu.VMEM)
HBM = pl.BlockSpec(memory_space=pltpu.HBM)
chunk_unroll = 16
chunk_tail = 4
passage_unroll = 8
meta_rows = 8


def in_hbm(array):
    return pltpu.with_memory_space_constraint(array, pltpu.HBM)


def params():
    return pltpu.CompilerParams(vmem_limit_bytes=vmem_bytes)


def unit_rows(values):
    widened = values.astype(jnp.float32)
    inverse = lax.rsqrt(jnp.sum(widened * widened, -1, keepdims=True) + epsilon)
    return widened * inverse, inverse


def round_bf16(values):
    return values.astype(jnp.bfloat16).astype(jnp.float32)


def pack_kernel(pass_count, *refs):
    sources, targets, out_ref, sems = refs[:3], refs[4:7], refs[3], refs[7]
    copies = [
        pltpu.make_async_copy(source, target, sems.at[i])
        for i, (source, target) in enumerate(zip(sources, targets))
    ]
    for copy in copies:
        copy.start()
    for copy in copies:
        copy.wait()
    queries_ref, candidates_ref, teacher_ref = targets
    query_count, cand_count = teacher_ref.shape
    ids = candidates_ref[...].astype(jnp.float32)
    owner = jnp.floor((ids + 0.5) * (1.0 / pass_count))
    values = teacher_ref[...]
    high = round_bf16(values)
    middle = round_bf16(values - high)
    low = values - high - middle
    main = jnp.concatenate([owner, ids - owner * pass_count, high, middle], 1)
    blank = jnp.zeros((8 - query_count, 128), jnp.float32)
    low = jnp.concatenate([low, jnp.zeros((query_count, 128 - cand_count), jnp.float32)], 1)
    extra = jnp.concatenate([main, blank, low, blank], 0).astype(jnp.bfloat16)
    rows = queries_ref.shape[0]
    out_ref[:rows, :] = queries_ref[...]
    out_ref[rows:, :] = extra


def pack(queries, candidates, teacher, pass_count):
    rows, width = queries.shape
    return pl.pallas_call(
        lambda *refs: pack_kernel(pass_count, *refs),
        in_specs=[HBM] * 3,
        out_specs=VMEM,
        out_shape=jax.ShapeDtypeStruct((rows + 16, width), jnp.bfloat16),
        scratch_shapes=[
            pltpu.VMEM(queries.shape, queries.dtype),
            pltpu.VMEM(candidates.shape, candidates.dtype),
            pltpu.VMEM(teacher.shape, teacher.dtype),
            pltpu.SemaphoreType.DMA((3,)),
        ],
        compiler_params=params(),
        name="pack",
    )(in_hbm(queries), in_hbm(candidates), in_hbm(teacher))


def lane_ids(shape):
    return lax.broadcasted_iota(jnp.int32, shape, len(shape) - 1)


def tangent(raw, grad):
    unit, inverse = unit_rows(raw)
    return inverse * (grad - unit * jnp.sum(unit * grad, -1, keepdims=True))


def passages_kernel(
    slices, in_hbm_ref, norm_ref, flip_ref, own_ref, in_ref, in_sems
):
    total, tokens, _ = norm_ref.shape
    parts = in_sems.shape[0]
    count = total // parts
    share = tokens // slices
    me = lax.axis_index("qry")

    def in_copy(part):
        place = pl.ds(part * count, count)
        return pltpu.make_async_copy(in_hbm_ref.at[place], in_ref.at[place], in_sems.at[part])

    for part in range(parts):
        in_copy(part).start()
    for part in range(parts):
        in_copy(part).wait()
        for item in range(part * count, (part + 1) * count):
            for place in range(slices):
                start = pl.multiple_of((me ^ place) * share, share)
                raw = in_ref[item, pl.ds(start, share), :]
                if place == 0:
                    own_ref[item] = raw
                norm_ref[item, pl.ds(place * share, share), :] = unit_rows(raw)[0].astype(
                    jnp.bfloat16
                )
            flip_ref[item] = jnp.transpose(norm_ref[item], (1, 0))


def prepare_passages(passages, slices):
    count, tokens, width = passages.shape
    parts = math.gcd(count, 4)
    share = tokens // slices
    return pl.pallas_call(
        lambda *refs: passages_kernel(slices, *refs),
        in_specs=[HBM],
        out_specs=[VMEM] * 3,
        out_shape=[
            jax.ShapeDtypeStruct((count, tokens, width), jnp.bfloat16),
            jax.ShapeDtypeStruct((count, width, tokens), jnp.bfloat16),
            jax.ShapeDtypeStruct((count, share, width), jnp.bfloat16),
        ],
        scratch_shapes=[
            pltpu.VMEM((count, tokens, width), jnp.bfloat16),
            pltpu.SemaphoreType.DMA((parts,)),
        ],
        compiler_params=params(),
        cost_estimate=pl.CostEstimate(flops=1 << 24, bytes_accessed=6 << 20, transcendentals=0),
        name="prepare_passages",
    )(in_hbm(passages))


def list_layout(group):
    empty = -(-group // chunk_pairs) * chunk_pairs // 4
    return empty, empty + chunk_pairs // 4


def slot_total(pass_count, pairs):
    worst = (pairs + pass_count * (chunk_pairs - 1)) // chunk_pairs
    return -(-worst // chunk_tail) * chunk_tail


def list_ids(list_smem, row, p):
    words = [list_smem[row + w, p] for w in range(chunk_pairs // 4)]
    return [(words[r // 4] >> (8 * (r % 4))) & 255 for r in range(chunk_pairs)]


def each_chunk(list_smem, tables, visit):
    total = jnp.maximum(list_smem[tables + 4, 0], 1)
    full = total // chunk_unroll
    tail = (total - full * chunk_unroll + chunk_tail - 1) // chunk_tail

    def step(i, carry):
        visit(i * chunk_unroll, chunk_unroll)
        return carry

    def tail_step(i, carry):
        visit(full * chunk_unroll + i * chunk_tail, chunk_tail)
        return carry

    lax.fori_loop(0, full, step, 0)
    lax.fori_loop(0, tail, tail_step, 0)


def query_places(ids, query_tokens):
    return [pl.ds(pl.multiple_of(n * query_tokens, query_tokens), query_tokens) for n in ids]


def forward_kernel(
    cand_count,
    query_count,
    query_tokens,
    recv_refs,
    norm_ref,
    soft_ref,
    qn_ref,
    score_ref,
    many_ref,
    target_ref,
    list_ref,
    zw_ref,
    inverse_ref,
    ext_ref,
    low_ref,
    sums_ref,
    list_smem,
    sem,
):
    near = recv_refs[0].shape[0]
    sources = near * len(recv_refs)
    pass_count, tokens, width = norm_ref.shape
    group = sources * query_count
    rows = query_count * query_tokens
    stride = group + row_pad
    empty, tables = list_layout(group)
    me = lax.axis_index("psg")
    owner = me.astype(jnp.float32)
    for d in range(sources):
        recv_ref = recv_refs[d // near].at[d % near]
        source = me ^ d
        packed = recv_ref[rows : rows + 16, :].astype(jnp.float32)
        place = pl.ds(pl.multiple_of(source * query_count, query_count), query_count)
        ext_ref[place, :] = packed[:query_count]
        low_ref[place, :] = packed[8 : 8 + query_count]

    main = ext_ref[...]
    lanes = lane_ids(main.shape)
    lanes_float = lanes.astype(jnp.float32)
    live = lanes < cand_count
    local = pltpu.roll(main, 128 - cand_count, 1)
    logits = (
        pltpu.roll(main, 128 - 2 * cand_count, 1)
        + pltpu.roll(main, 128 - 3 * cand_count, 1)
        + low_ref[...]
    )
    raised = jnp.where(live, jnp.exp(logits), 0.0)
    target = raised / jnp.sum(raised, -1, keepdims=True)
    local = jnp.where(main == owner, local, -1.0)
    many = jnp.zeros(main.shape, jnp.float32)
    wanted = jnp.zeros(main.shape, jnp.float32)
    for c in range(cand_count):
        same = local[:, c : c + 1] == lanes_float
        many = many + jnp.where(same, 1.0, 0.0)
        wanted = wanted + jnp.where(same, target[:, c : c + 1], 0.0)
    many_ref[...] = many
    target_ref[...] = wanted
    active = many > 0.0
    lower = (
        lax.broadcasted_iota(jnp.int32, (group, group), 0)
        > lax.broadcasted_iota(jnp.int32, (group, group), 1)
    ).astype(jnp.bfloat16)
    active_value = jnp.where(active, 1.0, 0.0)
    rank = jnp.dot(lower, active_value.astype(jnp.bfloat16), preferred_element_type=jnp.float32)
    rank = jnp.where(active, rank, -1.0)
    less = lax.broadcasted_iota(jnp.int32, main.shape, 0).astype(jnp.float32) - group
    for w in range(empty):
        word = jnp.zeros((1, 128), jnp.int32)
        for b in range(4):
            found = jnp.sum(jnp.where(rank == 4 * w + b, less, 0.0), 0, keepdims=True) + group
            word = word | (found.astype(jnp.int32) << (8 * b))
        list_ref[w : w + 1, :] = word
    blank = jnp.full((tables - empty, 128), group, jnp.int32)
    list_ref[empty:tables, :] = blank | (blank << 8) | (blank << 16) | (blank << 24)
    square = (128, 128)
    first_id = lax.broadcasted_iota(jnp.int32, square, 0)
    second_id = lax.broadcasted_iota(jnp.int32, square, 1)
    counts = lax.dot_general(
        active_value.astype(jnp.bfloat16),
        jnp.ones((group, 128), jnp.bfloat16),
        (((0,), (0,)), ((), ())),
        preferred_element_type=jnp.float32,
    )
    chunks = jnp.floor((counts + (chunk_pairs - 1)) * (1.0 / chunk_pairs))
    more = jnp.maximum(chunks - 2.0, 0.0)
    lower_square = (first_id >= second_id).astype(jnp.bfloat16)
    ends = jnp.dot(lower_square, chunks.astype(jnp.bfloat16), preferred_element_type=jnp.float32)
    more_ends = jnp.dot(lower_square, more.astype(jnp.bfloat16), preferred_element_type=jnp.float32)
    chunk_id = lax.broadcasted_iota(jnp.int32, (1, 128), 1).astype(jnp.float32)

    def places_of(chunk_ends, chunk_counts):
        past = chunk_ends <= second_id.astype(jnp.float32)
        passage_of = jnp.sum(jnp.where(past, 1.0, 0.0), 0, keepdims=True)
        start_of = jnp.sum(jnp.where(past, chunk_counts, 0.0), 0, keepdims=True)
        return passage_of, chunk_id - start_of

    def last_row(values):
        return jnp.sum(jnp.where(first_id == 127, values, 0.0), 0, keepdims=True)

    passage_of, chunk_of = places_of(ends, chunks)
    more_passage, more_chunk = places_of(more_ends, more)
    beyond = passage_of > pass_count - 0.5
    rows_of = (
        jnp.where(beyond, 0.0, passage_of),
        jnp.where(beyond, float(empty), chunk_of * (chunk_pairs // 4)),
        jnp.sum(jnp.where(first_id == second_id, ends - chunks, 0.0), 0, keepdims=True),
        jnp.sum(active_value, 0, keepdims=True),
        last_row(ends),
        more_passage,
        more_chunk + 2.0,
        last_row(more_ends),
    )
    for row, value in enumerate(rows_of):
        list_ref[tables + row : tables + row + 1, :] = value.astype(jnp.int32)
    copy = pltpu.make_async_copy(list_ref, list_smem, sem)
    copy.start()
    for d in range(sources):
        recv_ref = recv_refs[d // near].at[d % near]
        place = pl.ds(pl.multiple_of((me ^ d) * rows, rows), rows)
        qn_ref[place, :] = unit_rows(recv_ref[:rows, :])[0].astype(jnp.bfloat16)
    qn_ref[sources * rows :, :] = jnp.zeros((query_tokens, width), jnp.bfloat16)
    copy.wait()

    def chunk(slot):
        p = list_smem[tables, slot]
        ids = list_ids(list_smem, list_smem[tables + 1, slot], p)
        tile = jnp.concatenate([qn_ref[place, :] for place in query_places(ids, query_tokens)], 0)
        dots = lax.dot_general(
            norm_ref[p], tile, (((1,), (1,)), ((), ())), preferred_element_type=jnp.float32
        )
        power = jnp.exp2(dots * (math.log2(math.e) / softness_scale))
        sums = jnp.sum(power, 0, keepdims=True)
        soft_ref[slot] = power.astype(jnp.bfloat16)
        inverse_ref[pl.ds(slot, 1), :] = 1.0 / sums
        for r, n in enumerate(ids):
            sums_ref[pl.ds(p * stride + n, 1), :query_tokens] = sums[
                :, r * query_tokens : (r + 1) * query_tokens
            ]

    def visit(first, count):
        for u in range(count):
            chunk(first + u)

    each_chunk(list_smem, tables, visit)

    scores = jnp.zeros(main.shape, jnp.float32)
    for p in range(pass_count):
        logs = jnp.log(sums_ref[p * stride : p * stride + group, :])
        value = softness_scale * jnp.sum(
            jnp.where(lanes < query_tokens, logs, 0.0), -1, keepdims=True
        )
        scores = jnp.where(lanes == p, value, scores)
    scores = jnp.where(active, scores, 0.0)
    score_ref[...] = scores
    mass = jnp.sum(many * jnp.exp(scores), -1, keepdims=True)
    agreed = jnp.sum(wanted * scores, -1, keepdims=True)
    same_id = lax.broadcasted_iota(jnp.int32, main.shape, 0) == lanes
    message = jnp.concatenate(
        [
            jnp.sum(jnp.where(same_id, value, 0.0), 0, keepdims=True) for value in (mass, agreed)
        ]
        + [jnp.zeros((6, 128), jnp.float32)],
        0,
    )
    zw_ref[...] = message


def forward(received, norm, cand_count, query_count, query_tokens):
    sources = received[0].shape[0] * len(received)
    pass_count, tokens, width = norm.shape
    group = sources * query_count
    capacity = max(2, -(-5 * query_count * cand_count // (2 * sources)))
    slots = slot_total(pass_count, sources * capacity)
    list_rows = -(-(list_layout(group)[1] + meta_rows) // 8) * 8
    rows = query_count * query_tokens
    soft_shape = (slots, tokens, chunk_pairs * query_tokens)
    flops = 2 * slots * chunk_pairs * query_tokens * tokens * width
    return pl.pallas_call(
        lambda *refs: forward_kernel(
            cand_count, query_count, query_tokens, refs[: len(received)], *refs[len(received) :]
        ),
        in_specs=[VMEM] * (len(received) + 1),
        out_specs=[VMEM] * 8,
        out_shape=[
            jax.ShapeDtypeStruct(soft_shape, jnp.bfloat16),
            jax.ShapeDtypeStruct((sources * rows + query_tokens, width), jnp.bfloat16),
            jax.ShapeDtypeStruct((group, 128), jnp.float32),
            jax.ShapeDtypeStruct((group, 128), jnp.float32),
            jax.ShapeDtypeStruct((group, 128), jnp.float32),
            jax.ShapeDtypeStruct((list_rows, 128), jnp.int32),
            jax.ShapeDtypeStruct((8, 128), jnp.float32),
            jax.ShapeDtypeStruct((slots, chunk_pairs * query_tokens), jnp.float32),
        ],
        scratch_shapes=[
            pltpu.VMEM((group, 128), jnp.float32),
            pltpu.VMEM((group, 128), jnp.float32),
            pltpu.VMEM((pass_count * (group + row_pad), 128), jnp.float32),
            pltpu.SMEM((list_rows, 128), jnp.int32),
            pltpu.SemaphoreType.DMA,
        ],
        compiler_params=params(),
        cost_estimate=pl.CostEstimate(flops=flops, bytes_accessed=12 << 20, transcendentals=1 << 22),
        name="forward",
    )(*received, norm)


def spread(ref, values, pass_count, stride, start=0):
    group = values.shape[0]
    for p in range(pass_count):
        ref[p * stride : p * stride + group, :] = jnp.broadcast_to(
            values[:, start + p : start + p + 1], (group, 128)
        )
        ref[p * stride + group : (p + 1) * stride, :] = jnp.zeros((stride - group, 128), jnp.float32)


def attend_kernel(
    query_tokens,
    flip_ref,
    soft_ref,
    list_ref,
    score_ref,
    many_ref,
    target_ref,
    inverse_ref,
    raised_ref,
    wanted_ref,
    raised_rows,
    wanted_rows,
    list_smem,
    sem,
):
    pass_count = flip_ref.shape[0]
    group = score_ref.shape[0]
    stride = group + row_pad
    list_copy = pltpu.make_async_copy(list_ref, list_smem, sem)
    list_copy.start()
    empty, tables = list_layout(group)

    spread(raised_rows, many_ref[...] * jnp.exp(score_ref[...]), pass_count, stride)
    spread(wanted_rows, target_ref[...], pass_count, stride)
    raised_ref[...] = jnp.zeros(raised_ref.shape, jnp.float32)
    wanted_ref[...] = jnp.zeros(wanted_ref.shape, jnp.float32)
    list_copy.wait()

    def chunk(slot):
        p = list_smem[tables, slot]
        ids = list_ids(list_smem, list_smem[tables + 1, slot], p)
        places = query_places(ids, query_tokens)
        mixed = jnp.dot(flip_ref[p], soft_ref[slot], preferred_element_type=jnp.float32)
        mixed = (mixed * inverse_ref[pl.ds(slot, 1), :]).astype(jnp.bfloat16)
        mixed = jnp.transpose(mixed, (1, 0)).astype(jnp.float32)
        for total, rows in ((raised_ref, raised_rows), (wanted_ref, wanted_rows)):
            added = [
                total[place, :]
                + mixed[r * query_tokens : (r + 1) * query_tokens]
                * rows[pl.ds(p * stride + ids[r], 1), :]
                for r, place in enumerate(places)
            ]
            for place, value in zip(places, added):
                total[place, :] = value

    def visit(first, count):
        for u in range(count):
            chunk(first + u)

    each_chunk(list_smem, tables, visit)


def attend(flip, soft, ids, score, many, target, inverse, query_tokens):
    slots, tokens, columns = soft.shape
    pass_count, width, _ = flip.shape
    group = score.shape[0]
    flops = 2 * slots * columns * tokens * width
    total = jax.ShapeDtypeStruct(((group + 1) * query_tokens, width), jnp.float32)
    rows = pltpu.VMEM((pass_count * (group + row_pad), 128), jnp.float32)
    return pl.pallas_call(
        lambda *refs: attend_kernel(query_tokens, *refs),
        in_specs=[VMEM] * 7,
        out_specs=[VMEM] * 2,
        out_shape=[total, total],
        scratch_shapes=[
            rows,
            rows,
            pltpu.SMEM(ids.shape, jnp.int32),
            pltpu.SemaphoreType.DMA,
        ],
        compiler_params=params(),
        cost_estimate=pl.CostEstimate(flops=flops, bytes_accessed=12 << 20, transcendentals=0),
        name="attend",
    )(flip, soft, ids, score, many, target, inverse)


def halving_order(count):
    order = [0]
    bit = count // 2
    while bit:
        order = order + [x | bit for x in order]
        bit //= 2
    return order


def query_kernel(
    query_tokens,
    sources,
    zw_refs,
    score_ref,
    many_ref,
    target_ref,
    raised_ref,
    wanted_ref,
    keep_ref,
    send_ref,
    grads_ref,
    scale_ref,
    query_ref,
):
    group = score_ref.shape[0]
    sums = sum(ref[...] for ref in zw_refs)
    lanes = lane_ids((group, 128))
    same_id = lax.broadcasted_iota(jnp.int32, (group, 128), 0) == lanes
    inverse = 1.0 / jnp.sum(jnp.where(same_id, sums[:1], 0.0), -1, keepdims=True)
    grads_ref[...] = many_ref[...] * jnp.exp(score_ref[...]) * inverse - target_ref[...]
    scale_ref[...] = jnp.broadcast_to(inverse, scale_ref.shape)
    for n in range(group):
        place = pl.ds(n * query_tokens, query_tokens)
        query_ref[place, :] = (
            raised_ref[place, :] * scale_ref[n : n + 1, :] - wanted_ref[place, :]
        ).astype(jnp.bfloat16)
    me = lax.axis_index("psg")
    rows = group // sources * query_tokens
    half = keep_ref.shape[0]
    for place, d in enumerate(halving_order(sources)):
        start = pl.multiple_of((me ^ d) * rows, rows)
        value = query_ref[pl.ds(start, rows), :]
        if place < half:
            keep_ref[place] = value
        else:
            send_ref[place - half] = value


def query_backward(zw, score, many, target, raised, wanted, sources):
    group = score.shape[0]
    width = raised.shape[1]
    rows = raised.shape[0] // (group + 1) * group
    part = jax.ShapeDtypeStruct((sources // 2, rows // sources, width), jnp.bfloat16)
    return pl.pallas_call(
        lambda *refs: query_kernel(
            rows // group, sources, refs[: len(zw)], *refs[len(zw) :]
        ),
        in_specs=[VMEM] * (len(zw) + 5),
        out_specs=[VMEM] * 3,
        out_shape=[part, part, jax.ShapeDtypeStruct((group, 128), jnp.float32)],
        scratch_shapes=[
            pltpu.VMEM((group, 128), jnp.float32),
            pltpu.VMEM((rows, width), jnp.bfloat16),
        ],
        compiler_params=params(),
        name="query_backward",
    )(*zw, score, many, target, raised, wanted)


def passage_kernel(
    query_tokens,
    list_ref,
    grads_ref,
    qn_ref,
    inverse_ref,
    soft_ref,
    own_ref,
    core_ref,
    far_ref,
    cross_ref,
    grad_ref,
    list_smem,
    sem,
):
    list_copy = pltpu.make_async_copy(list_ref, list_smem, sem)
    list_copy.start()
    pass_count, share, width = own_ref.shape
    group = grads_ref.shape[0]
    stride = group + row_pad
    empty, tables = list_layout(group)
    spread(grad_ref, grads_ref[...], pass_count, stride)
    list_copy.wait()

    def tile(p, row):
        ids = list_ids(list_smem, row, p)
        return [
            (qn_ref[place, :].astype(jnp.float32) * grad_ref[pl.ds(p * stride + n, 1), :]).astype(
                jnp.bfloat16
            )
            for n, place in zip(ids, query_places(ids, query_tokens))
        ]

    def weights(slot):
        value = soft_ref[slot]
        tokens, columns = value.shape
        scale = jnp.broadcast_to(inverse_ref[pl.ds(slot, 1), :], (16, columns)).astype(jnp.bfloat16)
        return (value.reshape(tokens // 16, 16, columns) * scale[None]).reshape(tokens, columns)

    outs = (own_ref, core_ref, far_ref, cross_ref)

    def passage(p):
        pairs = list_smem[tables + 3, p]
        slot = list_smem[tables + 2, p]
        tiles, softs = [], []
        for h in range(2):
            some = pairs > h * chunk_pairs
            tiles += tile(p, jnp.where(some, h * (chunk_pairs // 4), empty))
            softs.append(weights(jnp.where(some, slot + h, 0)))
        value = jnp.dot(
            jnp.concatenate(softs, 1),
            jnp.concatenate(tiles, 0),
            preferred_element_type=jnp.float32,
        ).astype(jnp.bfloat16)
        for place, ref in enumerate(outs):
            ref[p] = value[place * share : (place + 1) * share]

    def step(i, carry):
        for u in range(passage_unroll):
            passage(i * passage_unroll + u)
        return carry

    lax.fori_loop(0, pass_count // passage_unroll, step, 0)

    def rest(i, carry):
        p = list_smem[tables + 5, i]
        b = list_smem[tables + 6, i]
        value = jnp.dot(
            weights(list_smem[tables + 2, p] + b),
            jnp.concatenate(tile(p, b * (chunk_pairs // 4)), 0),
            preferred_element_type=jnp.float32,
        )
        for place, ref in enumerate(outs):
            piece = value[place * share : (place + 1) * share]
            ref[p] = (ref[p].astype(jnp.float32) + piece).astype(jnp.bfloat16)
        return carry

    lax.fori_loop(0, list_smem[tables + 7, 0], rest, 0)


def passage_backward(ids, grads, qn, inverse, soft, pass_count, query_tokens, slices):
    _, tokens, columns = soft.shape
    width = qn.shape[1]
    piece = jax.ShapeDtypeStruct((pass_count, tokens // slices, width), jnp.bfloat16)
    flops = 4 * pass_count * columns * tokens * width
    return pl.pallas_call(
        lambda *refs: passage_kernel(query_tokens, *refs),
        in_specs=[VMEM] * 5,
        out_specs=[VMEM] * 4,
        out_shape=[piece] * 4,
        scratch_shapes=[
            pltpu.VMEM((pass_count * (grads.shape[0] + row_pad), 128), jnp.float32),
            pltpu.SMEM(ids.shape, jnp.int32),
            pltpu.SemaphoreType.DMA,
        ],
        compiler_params=params(),
        cost_estimate=pl.CostEstimate(flops=flops, bytes_accessed=6 << 20, transcendentals=0),
        name="passage_backward",
    )(ids, grads, qn, inverse, soft)


def add_parts(refs, place=slice(None)):
    return sum(ref[place].astype(jnp.float32) for ref in refs)


def finish_first_kernel(raw_ref, own_ref, core_ref, far_ref, out_ref):
    place = pl.ds(0, far_ref.shape[0])
    grad = add_parts((own_ref, core_ref), place) + add_parts((far_ref,))
    out_ref[...] = tangent(raw_ref[place], grad).astype(jnp.bfloat16)


def finish_last_kernel(raw_ref, own_ref, core_ref, far_ref, raw_query, *refs):
    parts, (query_out, out_ref) = refs[:-4], refs[-2:]
    query_out[...] = tangent(raw_query[...], add_parts(parts)).astype(jnp.bfloat16)
    count = far_ref.shape[0]
    place = pl.ds(count, count)
    grad = add_parts((own_ref, core_ref), place) + add_parts((far_ref,))
    out_ref[...] = tangent(raw_ref[place], grad).astype(jnp.bfloat16)


def finish_first(raw, own, core, far):
    return pl.pallas_call(
        finish_first_kernel,
        grid=(1,),
        in_specs=[VMEM] * 4,
        out_specs=pl.BlockSpec(far.shape, lambda i: (0, 0, 0)),
        out_shape=jax.ShapeDtypeStruct(raw.shape, jnp.bfloat16),
        compiler_params=params(),
        name="finish_first",
    )(raw, own, core, far)


def finish_last(raw, own, core, far, raw_query, query_parts, ready, before):
    count = 5 + len(query_parts)
    return pl.pallas_call(
        finish_last_kernel,
        grid=(1,),
        in_specs=[VMEM] * count + [pl.BlockSpec(memory_space=pl.ANY)] * 2,
        out_specs=[
            pl.BlockSpec(raw_query.shape, lambda i: (0, 0)),
            pl.BlockSpec(far.shape, lambda i: (1, 0, 0)),
        ],
        out_shape=[
            jax.ShapeDtypeStruct(raw_query.shape, jnp.bfloat16),
            jax.ShapeDtypeStruct(raw.shape, jnp.bfloat16),
        ],
        input_output_aliases={count + 1: 1},
        compiler_params=params(),
        name="finish_last",
    )(raw, own, core, far, raw_query, *query_parts, ready, before)


def shards(queries, passages, candidates, teacher):
    query_count, query_tokens, width = queries.shape
    pass_count = passages.shape[0]
    cand_count = candidates.shape[1]
    sources = lax.axis_size("psg")
    slices = lax.axis_size("qry")
    rows = query_count * query_tokens

    received = pack(queries.reshape(rows, width), candidates, teacher, pass_count)[None]
    while received.shape[0] * 4 < sources:
        bit = received.shape[0]
        pairs = [(i, i ^ bit) for i in range(sources)]
        received = jnp.concatenate([received, lax.ppermute(received, "psg", pairs)], 0)
    stride = received.shape[0]
    received = [received] + [
        lax.ppermute(received, "psg", [(i, i ^ d) for i in range(sources)])
        for d in range(stride, sources, stride)
    ]
    norm, flip, own_raw = prepare_passages(passages, slices)
    soft, qn, score, many, target, ids, zw, inverse = forward(
        received, norm, cand_count, query_count, query_tokens
    )

    def swap(values, bit):
        return lax.ppermute(values, "psg", [(i, i ^ bit) for i in range(sources)])

    bit = 1
    while sources // bit > 4:
        zw = zw + swap(zw, bit)
        bit *= 2
    raised_sum, wanted_sum = attend(
        flip, soft, ids, score, many, target, inverse, query_tokens
    )
    zw, raised_sum = lax.optimization_barrier((zw, raised_sum))
    zw = [zw] + [swap(zw, d) for d in range(bit, sources, bit)]
    keep, send, grads = query_backward(
        zw, score, many, target, raised_sum, wanted_sum, sources
    )
    near = [(k, k ^ 1) for k in range(slices)]
    away = [(k, k ^ 2) for k in range(slices)]
    own, core, far, cross = passage_backward(
        ids, grads, qn, inverse, soft, pass_count, query_tokens, slices
    )
    cross = lax.ppermute(cross, "qry", near)
    half = pass_count // 2
    far = [
        (far[part].astype(jnp.float32) + cross[part].astype(jnp.float32)).astype(jnp.bfloat16)
        for part in (slice(0, half), slice(half, pass_count))
    ]
    send, own = lax.optimization_barrier((send, own))
    ready = far[1]
    far = [lax.ppermute(piece, "qry", away) for piece in far]
    bit = 1
    while bit < sources:
        send = lax.ppermute(send, "psg", [(i, i ^ bit) for i in range(sources)])
        if bit == 1:
            send, zw, ready, core = lax.optimization_barrier((send, zw, ready, core))
            core = lax.ppermute(core, "qry", near)
        bit *= 2
        if bit < sources:
            total = keep.astype(jnp.float32) + send.astype(jnp.float32)
            half = total.shape[0] // 2
            keep, send = total[:half], total[half:].astype(jnp.bfloat16)
    query_parts = [keep[0], send[0]]
    grad_passages = finish_first(own_raw, own, core, far[0])
    grad_queries, grad_passages = finish_last(
        own_raw,
        own,
        core,
        far[1],
        queries.reshape(rows, width),
        query_parts,
        ready,
        grad_passages,
    )

    raised = jnp.exp(teacher)
    raised_sum = jnp.sum(raised, -1, keepdims=True)
    log_target = teacher - jnp.log(raised_sum)
    known = jnp.sum(raised / raised_sum * log_target, -1)
    mine = lax.dynamic_slice_in_dim(
        sum(zw)[:2], lax.axis_index("psg") * query_count, query_count, 1
    )
    pair_loss = known - mine[1] + jnp.log(mine[0])
    return (pair_loss, grad_queries.reshape(queries.shape), grad_passages)


def solution(mesh):
    placed = (
        P(("psg", "qry"), None, None),
        P("psg", None, None),
        P(("psg", "qry"), None),
        P(("psg", "qry"), None),
    )
    return jax.shard_map(
        shards,
        mesh=mesh,
        in_specs=placed,
        out_specs=(P(("psg", "qry")), P(("psg", "qry"), None, None), P("psg", "qry", None)),
        check_vma=False,
    )
```
